32 devices in a mesh: dp: 4 (over z), space: 8 (over y, x, core).
Axes of the slice: x: 2, y: 2, z: 4, core: 2. Of those that a mesh axis runs over, the one named last changes fastest.
Arguments:
- pre_act: bfloat16 [4, 64, 128, 320], P('dp', 'space'), may hold values from -6 to 6
- out_grad: bfloat16 [4, 64, 128, 320], P('dp', 'space'), may hold values from -6 to 6
- kernel: bfloat16 [3, 3, 320, 320], replicated, may hold values from -0.109375 to 0.109375
Outputs:
- in_grad: bfloat16 [4, 64, 128, 320], P('dp', 'space')
- kernel_grad: float32 [2880, 320], P('dp')
The draws below stay inside these ranges and needn't reach their ends.
All inputs are finite; a program needn't handle non-finite values.
Results may differ from the reference program's by a relative error of at most 0.0029.
Values may be sent and summed in bfloat16 or wider, within the bound.
No kernel may reach another device: no remote copies, remote signals or barrier semaphores. Data moves between devices by JAX's collectives and lax.ppermute only.
A program may use at most 64 MiB of HBM per device.

```python
import jax
import jax.numpy as jnp
from jax import lax

C = 320
COLS = 128
IMAGES = 4
HEIGHT = 64


def strengthened(drawn, own_key, source, target, shards_of, factor):
    def block_of(axis_at):
        return (jnp.arange(drawn.shape[axis_at]) // (drawn.shape[axis_at] // shards_of)).reshape((-1,) + (1,) * (drawn.ndim - 1 - axis_at))

    one_side = jax.random.permutation(own_key, shards_of)[block_of(target)]
    far = (block_of(target) + shards_of // 2) % shards_of
    return jnp.where((block_of(source) == one_side) | (block_of(source) == far), factor * drawn, drawn)


def level_of(own_key, dims, split, low, top_value):
    level, own = 1.0, jax.random.fold_in(own_key, 6)
    for position, parts in split:
        draws = jnp.exp(jax.random.uniform(jax.random.fold_in(own, position), (parts,), jnp.float32, low / len(split), top_value / len(split)))
        level = level * jnp.repeat(draws, dims[position] // parts).reshape([-1 if axis == position else 1 for axis in range(len(dims))])
    return level


def normal_values(rng, extent, scale, most, shards=(), held_as=jnp.bfloat16):
    values = scale * jax.random.normal(rng, extent, jnp.float32)
    if shards:
        values = values * level_of(rng, extent, shards, -0.22, 0.18)
    return jnp.clip(values, -most, most).astype(held_as)


def gaussian_with(stream_key, extent, scale, reach, cuts, heavy, dtype=jnp.bfloat16):
    values = scale * jax.random.normal(stream_key, extent, jnp.float32)
    if cuts:
        values = values * level_of(stream_key, extent, cuts, -0.22, 0.18)
    return jnp.clip(strengthened(values, jax.random.fold_in(stream_key, 3), *heavy), -reach, reach).astype(dtype)


def setup_inputs(seed: int = 0) -> dict:
    keys = jax.random.split(jax.random.key(seed), 4)
    return {
        "pre_act": gaussian_with(keys[0], (IMAGES, HEIGHT, COLS, C), 1.0, 6.0, ((0, 4), (1, 8)), (0, 3, 4, 2.0)),
        "out_grad": normal_values(keys[1], (IMAGES, HEIGHT, COLS, C), 1.0, 6.0, ((0, 4), (1, 8))),
        "kernel": normal_values(keys[2], (3, 3, C, C), (9 * C) ** -0.5, 0.109375),
    }


def reference(pre_act, out_grad, kernel):
    height = pre_act.shape[1]
    width = pre_act.shape[2]
    chans = pre_act.shape[3]

    def one_image(carry, pair):
        feats, grads = pair
        xf = feats.astype(jnp.float32)
        act = jax.nn.silu(xf).astype(jnp.bfloat16)
        act_pad = jnp.pad(act, ((1, 1), (1, 1), (0, 0)))
        grad_pad = jnp.pad(grads, ((1, 1), (1, 1), (0, 0)))
        g_flat = grads.reshape(height * width, chans)
        act_grad = jnp.zeros((height * width, chans), jnp.float32)
        new_carry = carry
        for tap_a in range(3):
            for tap_b in range(3):
                shifted = grad_pad[2 - tap_a:2 - tap_a + height, 2 - tap_b:2 - tap_b + width, :].reshape(height * width, chans)
                act_grad = act_grad + jnp.dot(shifted, kernel[tap_a, tap_b].T, preferred_element_type=jnp.float32)
                window = act_pad[tap_a:tap_a + height, tap_b:tap_b + width, :].reshape(height * width, chans)
                term = jnp.dot(window.T, g_flat, preferred_element_type=jnp.float32)
                new_carry = new_carry.at[tap_a, tap_b].add(term)
        sig = jax.nn.sigmoid(xf)
        deriv = sig * (1.0 + xf * (1.0 - sig))
        in_grad = (act_grad.reshape(height, width, chans) * deriv).astype(jnp.bfloat16)
        return new_carry, in_grad

    start = jnp.zeros((3, 3, chans, chans), jnp.float32)
    total, in_grad = lax.scan(one_image, start, (pre_act, out_grad))
    pixels = pre_act.shape[0] * height * width
    scaled = total * (float(pixels) ** -0.5)
    kernel_grad = jnp.transpose(scaled, (2, 0, 1, 3)).reshape(9 * chans, chans)
    return in_grad, kernel_grad
```

```python
import functools

import jax
import jax.numpy as jnp
from jax import lax
from jax.experimental import pallas as pl
from jax.experimental.pallas import tpu as pltpu
from jax.sharding import PartitionSpec as P

F32 = jnp.float32
BF16 = jnp.bfloat16
LANES = 128
PAIR = 2
PLANE = 4
VMEM_LIMIT = 48 * 1024 * 1024


def vmem():
    return pl.BlockSpec(memory_space=pltpu.VMEM)


def column_shifts(row):
    wide = row.astype(F32)
    width = wide.shape[1]
    at = lax.broadcasted_iota(jnp.int32, wide.shape, 1)
    ahead = jnp.where(at == width - 1, 0.0, pltpu.roll(wide, width - 1, 1))
    behind = jnp.where(at == 0, 0.0, pltpu.roll(wide, 1, 1))
    return ahead.astype(BF16), row, behind.astype(BF16)


def weight_kernel(blocks, pre_ref, grad_ref, up_ref, down_ref, own_ref, send_ref, act_s, taps_s):
    rows, chans, width = pre_ref.shape
    half = chans // PAIR
    core = lax.rem(lax.axis_index("space"), PAIR)
    block = chans // blocks
    for h in range(PAIR):
        taps_s[h, 3 * half :, :] = jnp.zeros((taps_s.shape[1] - 3 * half, taps_s.shape[2]), BF16)
    for r in range(rows + 2):
        row = up_ref[...] if r == 0 else down_ref[...] if r == rows + 1 else grad_ref[r - 1]
        for b, shifted in enumerate(column_shifts(row)):
            for h in range(PAIR):
                taps_s[h, b * half : (b + 1) * half, r * width : (r + 1) * width] = shifted[h * half : (h + 1) * half]
    for r in range(rows):
        x = pre_ref[r].astype(F32)
        act_s[:, r * width : (r + 1) * width] = (x / (1.0 + jnp.exp(-x))).astype(BF16)
    for slot, out_ref in enumerate((send_ref, own_ref)):
        h = core if slot else 1 - core
        for a in range(3):
            at = (2 - a) * width
            term = lax.dot_general(
                act_s[...],
                taps_s[h, :, at : at + rows * width],
                (((1,), (1,)), ((), ())),
                preferred_element_type=F32,
            )
            for p in range(PLANE):
                for z in range(blocks):
                    out_ref[p, z, a] = term[z * block : (z + 1) * block, p * LANES : (p + 1) * LANES].astype(out_ref.dtype)


def input_kernel(pre_ref, grad_ref, up_ref, down_ref, kernel_ref, out_ref, taps_s):
    rows, chans, width = pre_ref.shape
    for r in range(rows + 2):
        row = up_ref[...] if r == 0 else down_ref[...] if r == rows + 1 else grad_ref[r - 1]
        for b, shifted in enumerate(column_shifts(row)):
            taps_s[b, :, r * width : (r + 1) * width] = shifted
    step = 2
    for first in range(0, rows, step):
        total = jnp.zeros((chans, step * width), F32)
        for a in range(3):
            at = (first + 2 - a) * width
            for b in range(3):
                total += jnp.dot(kernel_ref[a, b], taps_s[b, :, at : at + step * width], preferred_element_type=F32)
        for r in range(step):
            x = pre_ref[first + r].astype(F32)
            sig = 1.0 / (1.0 + jnp.exp(-x))
            deriv = sig * (1.0 + x * (1.0 - sig))
            out_ref[first + r] = (total[:, r * width : (r + 1) * width] * deriv).astype(out_ref.dtype)


def place_kernel(parts_ref, out_ref, rows_s):
    _, _, block, _ = parts_ref.shape
    chans = out_ref.shape[0]
    half = chans // PAIR
    for h in range(PAIR):
        for a in range(3):
            wide = jnp.concatenate([parts_ref[q * PAIR + h, a].astype(F32) for q in range(PLANE)], axis=1)
            for b in range(3):
                t = 3 * a + b
                rows_s[t * block : (t + 1) * block, h * half : (h + 1) * half] = wide[:, b * half : (b + 1) * half]
    k = lax.broadcasted_iota(jnp.int32, (block, 9 * block), 0)
    j = lax.broadcasted_iota(jnp.int32, (block, 9 * block), 1)
    pick = jnp.concatenate([jnp.where(j - 9 * k == t, 1.0, 0.0) for t in range(9)], axis=0)
    pick = pick.astype(BF16)
    high = rows_s[...].astype(BF16)
    low = (rows_s[...] - high.astype(F32)).astype(BF16)
    dims = (((0,), (0,)), ((), ()))
    out_ref[...] = lax.dot_general(high, pick, dims, preferred_element_type=F32) + lax.dot_general(
        low, pick, dims, preferred_element_type=F32
    )


def shards(pre_act, out_grad, kernel):
    images, rows, width, chans = pre_act.shape
    assert images == 1
    space, blocks = lax.axis_size("space"), lax.axis_size("dp")
    inner = PAIR * PLANE
    outer = space // inner
    block = chans // blocks
    factor = float(images * rows * width * space * blocks) ** (-0.5)
    params = pltpu.CompilerParams(vmem_limit_bytes=VMEM_LIMIT)

    pre = jnp.swapaxes(pre_act[0], 1, 2)
    grad = jnp.swapaxes(out_grad[0], 1, 2)
    up = lax.ppermute(grad[rows - 1], "space", [(i, i + 1) for i in range(space - 1)])
    down = lax.ppermute(grad[0], "space", [(i + 1, i) for i in range(space - 1)])

    piece = jax.ShapeDtypeStruct((PLANE, blocks, 3, block, LANES), F32)
    flops = 2 * 9 * chans * chans * rows * width
    own, send = pl.pallas_call(
        functools.partial(weight_kernel, blocks),
        out_shape=(piece, piece),
        in_specs=[vmem()] * 4,
        out_specs=(vmem(), vmem()),
        scratch_shapes=[
            pltpu.VMEM((chans, rows * width), BF16),
            pltpu.VMEM((PAIR, PLANE * LANES, (rows + 2) * width), BF16),
        ],
        compiler_params=params,
        cost_estimate=pl.CostEstimate(flops=flops, bytes_accessed=6000000, transcendentals=rows * width * chans),
        name="weight_terms",
    )(pre, grad, up, down)
    recv = lax.ppermute(send, "space", [(i, i + 1 - 2 * (i % 2)) for i in range(space)])
    pair_sum = (own + recv).astype(BF16)

    in_grad = pl.pallas_call(
        input_kernel,
        out_shape=jax.ShapeDtypeStruct((rows, chans, width), BF16),
        in_specs=[vmem()] * 5,
        out_specs=vmem(),
        scratch_shapes=[pltpu.VMEM((3, chans, (rows + 2) * width), BF16)],
        compiler_params=params,
        cost_estimate=pl.CostEstimate(flops=flops, bytes_accessed=4000000, transcendentals=rows * width * chans),
        name="input_grad",
    )(pre, grad, up, down, kernel)

    planes = [[first + PAIR * p + c for p in range(PLANE)] for first in range(0, space, inner) for c in range(PAIR)]
    terms = lax.all_to_all(pair_sum, "space", 0, 0, axis_index_groups=planes, tiled=True)
    plane_sum = jnp.sum(terms.astype(F32), axis=0)
    terms = lax.all_to_all(plane_sum.astype(BF16), "dp", 0, 0, tiled=True)
    total = jnp.sum(terms.astype(F32), axis=0) * factor
    if outer > 1:
        total = lax.psum(total, "space", axis_index_groups=[[o * inner + i for o in range(outer)] for i in range(inner)])
    inners = [[first + i for i in range(inner)] for first in range(0, space, inner)]
    spread = jnp.broadcast_to(total[None], (inner, 3, block, LANES))
    parts = lax.all_to_all(spread, "space", 0, 0, axis_index_groups=inners, tiled=True)

    placed = pl.pallas_call(
        place_kernel,
        out_shape=jax.ShapeDtypeStruct((chans, 9 * block), F32),
        in_specs=[vmem()],
        out_specs=vmem(),
        scratch_shapes=[pltpu.VMEM((9 * block, chans), F32)],
        compiler_params=params,
        cost_estimate=pl.CostEstimate(flops=2 * 81 * block * block * chans, bytes_accessed=2000000, transcendentals=0),
        name="place_rows",
    )(parts)
    return jnp.swapaxes(in_grad, 1, 2)[None], placed.T


def solution(mesh):
    placed = (P("dp", "space", None, None), P("dp", "space", None, None), P())
    return jax.shard_map(
        shards,
        mesh=mesh,
        in_specs=placed,
        out_specs=(P("dp", "space", None, None), P("dp", None)),
        check_vma=False,
    )
```

```python
import jax
import jax.numpy as jnp
from jax import lax
from jax.experimental import pallas as pl
from jax.experimental.pallas import tpu as pltpu
from jax.sharding import PartitionSpec as P

F32 = jnp.float32
BF16 = jnp.bfloat16
LANES = 128
PAIR = 2
PLANE = 4
NEAR = 2
VMEM_LIMIT = 48 * 1024 * 1024
NT = (((1,), (1,)), ((), ()))


def vmem():
    return pl.BlockSpec(memory_space=pltpu.VMEM)


def column_shifts(row):
    wide = row.astype(F32)
    width = wide.shape[1]
    at = lax.broadcasted_iota(jnp.int32, wide.shape, 1)
    ahead = jnp.where(at == width - 1, 0.0, pltpu.roll(wide, width - 1, 1))
    behind = jnp.where(at == 0, 0.0, pltpu.roll(wide, 1, 1))
    return ahead.astype(BF16), row, behind.astype(BF16)


def put_taps(taps_s, slot, row):
    half, width = row.shape
    for b, shifted in enumerate(column_shifts(row)):
        taps_s[b * half : (b + 1) * half, slot * width : (slot + 1) * width] = shifted


def silu(v):
    x = v.astype(F32)
    return (x / (1.0 + jnp.exp(-x))).astype(BF16)


def my_core():
    return lax.rem(lax.axis_index("space"), PAIR)


def own_kernel(pre_ref, grad_ref, term_ref, act_s, taps_s):
    rows, chans, width = pre_ref.shape
    half = chans // PAIR
    mine = pl.ds(pl.multiple_of(my_core() * half, half), half)
    zero = jnp.zeros((half, width), BF16)
    taps_s[3 * half :, :] = jnp.zeros((taps_s.shape[0] - 3 * half, taps_s.shape[1]), BF16)
    for r in range(rows + 2):
        put_taps(taps_s, r, grad_ref[r - 1, mine, :] if 0 < r <= rows else zero)
    for r in range(rows):
        act_s[:, r * width : (r + 1) * width] = silu(pre_ref[r])
    for a in range(3):
        at = (2 - a) * width
        term_ref[a] = lax.dot_general(act_s[...], taps_s[:, at : at + rows * width], NT, preferred_element_type=F32)


def pair_kernel(term_ref, pre_ref, grad_ref, their_pre_ref, their_grad_ref, near_ref, far_ref, out_ref, act_s, taps_s):
    rows, chans, width = pre_ref.shape
    half = chans // PAIR
    _, _, outers, _, block, _ = out_ref.shape
    core = my_core()
    first = core == 0
    mine = pl.ds(pl.multiple_of(core * half, half), half)
    taps_s[3 * half :, :] = jnp.zeros((taps_s.shape[0] - 3 * half, taps_s.shape[1]), BF16)
    put_taps(taps_s, 0, jnp.where(first, near_ref[mine, :], their_grad_ref[rows - 1, mine, :]))
    put_taps(taps_s, 1, jnp.where(first, grad_ref[rows - 1, mine, :], far_ref[...]))
    for r in range(rows):
        put_taps(taps_s, 2 + r, their_grad_ref[r, mine, :])
    put_taps(taps_s, rows + 2, jnp.where(first, far_ref[...], grad_ref[0, mine, :]))
    put_taps(taps_s, rows + 3, jnp.where(first, their_grad_ref[0, mine, :], near_ref[mine, :]))
    act_s[:, :width] = silu(pre_ref[0])
    for r in range(rows):
        act_s[:, (r + 1) * width : (r + 2) * width] = silu(their_pre_ref[r])
    act_s[:, (rows + 1) * width :] = silu(pre_ref[rows - 1])
    for a, (left, right, at) in enumerate(((1, rows + 2, 3), (1, rows + 1, 2), (0, rows + 1, 0))):
        term = term_ref[a] + lax.dot_general(
            act_s[:, left * width : right * width],
            taps_s[:, at * width : (at + right - left) * width],
            NT,
            preferred_element_type=F32,
        )
        for p in range(PLANE):
            for z in range(NEAR * outers):
                out_ref[z % NEAR, p, z // NEAR, a] = term[
                    z * block : (z + 1) * block, p * LANES : (p + 1) * LANES
                ].astype(out_ref.dtype)


def input_kernel(pre_ref, grad_ref, their_grad_ref, near_ref, kernel_ref, out_ref, taps_s):
    rows, chans, width = pre_ref.shape
    first = my_core() == 0
    for r in range(rows + 2):
        if r == 0:
            row = jnp.where(first, near_ref[...], their_grad_ref[rows - 1])
        elif r == rows + 1:
            row = jnp.where(first, their_grad_ref[0], near_ref[...])
        else:
            row = grad_ref[r - 1]
        put_taps(taps_s, r, row)
    step = 2
    for top in range(0, rows, step):
        total = jnp.zeros((chans, step * width), F32)
        for a in range(3):
            at = (top + 2 - a) * width
            for b in range(3):
                taps = taps_s[b * chans : (b + 1) * chans, at : at + step * width]
                total += jnp.dot(kernel_ref[a, b], taps, preferred_element_type=F32)
        for r in range(step):
            x = pre_ref[top + r].astype(F32)
            sig = 1.0 / (1.0 + jnp.exp(-x))
            deriv = sig * (1.0 + x * (1.0 - sig))
            out_ref[top + r] = (total[:, r * width : (r + 1) * width] * deriv).astype(out_ref.dtype)


def place_kernel(parts_ref, out_ref, rows_s):
    _, _, block, _ = parts_ref.shape
    chans = out_ref.shape[0]
    half = chans // PAIR
    for h in range(PAIR):
        for a in range(3):
            wide = jnp.concatenate([parts_ref[q * PAIR + h, a].astype(F32) for q in range(PLANE)], axis=1)
            for b in range(3):
                t = 3 * a + b
                rows_s[t * block : (t + 1) * block, h * half : (h + 1) * half] = wide[:, b * half : (b + 1) * half]
    k = lax.broadcasted_iota(jnp.int32, (block, 9 * block), 0)
    j = lax.broadcasted_iota(jnp.int32, (block, 9 * block), 1)
    pick = jnp.concatenate([jnp.where(j - 9 * k == t, 1.0, 0.0) for t in range(9)], axis=0).astype(BF16)
    dims = (((0,), (0,)), ((), ()))
    out_ref[...] = lax.dot_general(rows_s[...].astype(BF16), pick, dims, preferred_element_type=F32)


def shards(pre_act, out_grad, kernel):
    images, rows, width, chans = pre_act.shape
    assert images == 1
    space, blocks = lax.axis_size("space"), lax.axis_size("dp")
    inner = PAIR * PLANE
    outer = space // inner
    block = chans // blocks
    half = chans // PAIR
    far = blocks // NEAR
    factor = float(images * rows * width * space * blocks) ** (-0.5)
    params = pltpu.CompilerParams(vmem_limit_bytes=VMEM_LIMIT)
    core = my_core()
    flops = 2 * 9 * chans * chans * rows * width

    pre = jnp.swapaxes(pre_act[0], 1, 2)
    grad = jnp.swapaxes(out_grad[0], 1, 2)
    edge = lax.dynamic_index_in_dim(grad, core * (rows - 1), 0, keepdims=False)
    edge_half = lax.dynamic_slice_in_dim(edge, core * half, half, 0)
    beyond = [(i, i + 1 if i % 2 else i - 1) for i in range(space)]
    beyond_two = [(i, i + 2 if i % 2 else i - 2) for i in range(space)]
    pairs = [(i, i + 1 - 2 * (i % 2)) for i in range(space)]

    def inside(moves):
        return [(i, j) for i, j in moves if 0 <= j < space]

    near_row = lax.ppermute(edge, "space", inside(beyond))
    far_row = lax.ppermute(edge_half, "space", inside(beyond_two))
    their_grad = lax.ppermute(grad, "space", pairs)
    their_pre = lax.ppermute(pre, "space", pairs)

    own = pl.pallas_call(
        own_kernel,
        out_shape=jax.ShapeDtypeStruct((3, chans, PLANE * LANES), F32),
        in_specs=[vmem()] * 2,
        out_specs=vmem(),
        scratch_shapes=[
            pltpu.VMEM((chans, rows * width), BF16),
            pltpu.VMEM((PLANE * LANES, (rows + 2) * width), BF16),
        ],
        compiler_params=params,
        cost_estimate=pl.CostEstimate(flops=flops, bytes_accessed=4000000, transcendentals=rows * width * chans),
        name="own_terms",
    )(pre, grad)
    terms = pl.pallas_call(
        pair_kernel,
        out_shape=jax.ShapeDtypeStruct((NEAR, PLANE, far, 3, block, LANES), BF16),
        in_specs=[vmem()] * 7,
        out_specs=vmem(),
        scratch_shapes=[
            pltpu.VMEM((chans, (rows + 2) * width), BF16),
            pltpu.VMEM((PLANE * LANES, (rows + 4) * width), BF16),
        ],
        compiler_params=params,
        cost_estimate=pl.CostEstimate(flops=flops, bytes_accessed=4000000, transcendentals=rows * width * chans),
        name="pair_terms",
    )(own, pre, grad, their_pre, their_grad, near_row, far_row)

    in_grad = pl.pallas_call(
        input_kernel,
        out_shape=jax.ShapeDtypeStruct((rows, chans, width), BF16),
        in_specs=[vmem()] * 5,
        out_specs=vmem(),
        scratch_shapes=[pltpu.VMEM((3 * chans, (rows + 2) * width), BF16)],
        compiler_params=params,
        cost_estimate=pl.CostEstimate(flops=flops, bytes_accessed=4000000, transcendentals=rows * width * chans),
        name="input_grad",
    )(pre, grad, their_grad, near_row, kernel)

    groups = [
        [(NEAR * f + n) * space + first + PAIR * p + c for n in range(NEAR) for p in range(PLANE)]
        for f in range(far)
        for first in range(0, space, inner)
        for c in range(PAIR)
    ]
    terms = terms.reshape(NEAR * PLANE, far, 3, block, LANES)
    got = lax.all_to_all(terms, ("dp", "space"), 0, 0, axis_index_groups=groups, tiled=True)
    near_sum = jnp.sum(got.astype(F32), axis=0)
    mine = lax.axis_index("dp") // NEAR
    total = lax.dynamic_index_in_dim(near_sum, mine, 0, keepdims=False)
    for k in range(1, far):
        theirs = lax.dynamic_index_in_dim(near_sum, mine ^ k, 0, keepdims=False).astype(BF16)
        moves = [(z, z ^ (k * NEAR)) for z in range(blocks)]
        total = total + lax.ppermute(theirs, "dp", moves).astype(F32)
    total = total * factor
    if outer > 1:
        total = lax.psum(total, "space", axis_index_groups=[[o * inner + i for o in range(outer)] for i in range(inner)])
    inners = [[first + i for i in range(inner)] for first in range(0, space, inner)]
    spread = jnp.broadcast_to(total.astype(BF16)[None], (inner, 3, block, LANES))
    parts = lax.all_to_all(spread, "space", 0, 0, axis_index_groups=inners, tiled=True)

    placed = pl.pallas_call(
        place_kernel,
        out_shape=jax.ShapeDtypeStruct((chans, 9 * block), F32),
        in_specs=[vmem()],
        out_specs=vmem(),
        scratch_shapes=[pltpu.VMEM((9 * block, chans), F32)],
        compiler_params=params,
        cost_estimate=pl.CostEstimate(flops=2 * 81 * block * block * chans, bytes_accessed=2000000, transcendentals=0),
        name="place_rows",
    )(parts)
    return jnp.swapaxes(in_grad, 1, 2)[None], placed.T


def solution(mesh):
    placed = (P("dp", "space", None, None), P("dp", "space", None, None), P())
    return jax.shard_map(
        shards,
        mesh=mesh,
        in_specs=placed,
        out_specs=(P("dp", "space", None, None), P("dp", None)),
        check_vma=False,
    )
```

```python
import jax
import jax.numpy as jnp
from jax import lax
from jax.experimental import pallas as pl
from jax.experimental.pallas import tpu as pltpu
from jax.sharding import PartitionSpec as P

F32 = jnp.float32
BF16 = jnp.bfloat16
LANES = 128
PAIR = 2
PLANE = 4
NEAR = 2
VMEM_LIMIT = 48 * 1024 * 1024
NT = (((1,), (1,)), ((), ()))


def vmem():
    return pl.BlockSpec(memory_space=pltpu.VMEM)


def anywhere():
    return pl.BlockSpec(memory_space=pltpu.HBM)


def column_shifts(row):
    wide = row.astype(F32)
    width = wide.shape[1]
    at = lax.broadcasted_iota(jnp.int32, wide.shape, 1)
    ahead = jnp.where(at == width - 1, 0.0, pltpu.roll(wide, width - 1, 1))
    behind = jnp.where(at == 0, 0.0, pltpu.roll(wide, 1, 1))
    return ahead.astype(BF16), row, behind.astype(BF16)


def put_taps(taps_s, slot, row):
    half, width = row.shape
    for b, shifted in enumerate(column_shifts(row)):
        taps_s[b * half : (b + 1) * half, slot * width : (slot + 1) * width] = shifted


def plane_index():
    return lax.rem(lax.axis_index("space") // PAIR, PLANE)


def near_index():
    return lax.rem(lax.axis_index("dp"), NEAR) * PLANE + plane_index()


def silu(v):
    x = v.astype(F32)
    return (x / (1.0 + jnp.exp(-x))).astype(BF16)


def my_core():
    return lax.rem(lax.axis_index("space"), PAIR)


def fetch(pairs, sem):
    copies = [pltpu.make_async_copy(src, dst, sem.at[i]) for i, (src, dst) in enumerate(pairs)]
    for copy in copies:
        copy.start()
    return copies


def own_kernel(pre_hbm, grad_hbm, term_ref, act_edge_ref, grad_edge_ref, pre_ref, grad_ref, act_s, taps_s, sem):
    rows, chans, width = pre_ref.shape
    half = chans // PAIR
    order = [(grad_hbm.at[r], grad_ref.at[r]) for r in range(rows)] + [(pre_hbm.at[r], pre_ref.at[r]) for r in range(rows)]
    copies = fetch(order, sem)
    mine = pl.ds(pl.multiple_of(my_core() * half, half), half)
    zero = jnp.zeros((half, width), BF16)
    taps_s[3 * half :, :] = jnp.zeros((taps_s.shape[0] - 3 * half, taps_s.shape[1]), BF16)
    put_taps(taps_s, 0, zero)
    put_taps(taps_s, rows + 1, zero)
    for r in range(rows):
        copies[r].wait()
        put_taps(taps_s, r + 1, grad_ref[r, mine, :])
    for r in range(rows):
        copies[rows + r].wait()
        act_s[:, r * width : (r + 1) * width] = silu(pre_ref[r])
    for i, r in enumerate((0, rows - 1)):
        act_edge_ref[i] = act_s[:, r * width : (r + 1) * width]
        grad_edge_ref[i] = grad_ref[r, mine, :]
    for a in range(3):
        at = (2 - a) * width
        term_ref[a] = lax.dot_general(act_s[...], taps_s[:, at : at + rows * width], NT, preferred_element_type=F32)


def pair_kernel(term_ref, act_edge_ref, grad_edge_ref, their_pre_ref, their_grad_ref, near_ref, far_ref, *refs):
    out_refs, (act_s, taps_s, term_s) = refs[: PLANE * NEAR], refs[PLANE * NEAR :]
    rows, chans, width = their_pre_ref.shape
    half = chans // PAIR
    outers, _, block, _ = out_refs[0].shape
    core = my_core()
    first = core == 0
    mine = pl.ds(pl.multiple_of(core * half, half), half)
    taps_s[3 * half :, :] = jnp.zeros((taps_s.shape[0] - 3 * half, taps_s.shape[1]), BF16)
    put_taps(taps_s, 0, jnp.where(first, near_ref[mine, :], their_grad_ref[rows - 1, mine, :]))
    put_taps(taps_s, 1, jnp.where(first, grad_edge_ref[1], far_ref[mine, :]))
    for r in range(rows):
        put_taps(taps_s, 2 + r, their_grad_ref[r, mine, :])
    put_taps(taps_s, rows + 2, jnp.where(first, far_ref[mine, :], grad_edge_ref[0]))
    put_taps(taps_s, rows + 3, jnp.where(first, their_grad_ref[0, mine, :], near_ref[mine, :]))
    act_s[:, :width] = act_edge_ref[0]
    for r in range(rows):
        act_s[:, (r + 1) * width : (r + 2) * width] = silu(their_pre_ref[r])
    act_s[:, (rows + 1) * width :] = act_edge_ref[1]
    for a, (left, right, at) in enumerate(((1, rows + 2, 3), (1, rows + 1, 2), (0, rows + 1, 0))):
        term = term_ref[a] + lax.dot_general(
            act_s[:, left * width : right * width],
            taps_s[:, at * width : (at + right - left) * width],
            NT,
            preferred_element_type=F32,
        )
        for p in range(PLANE):
            for z in range(NEAR * outers):
                term_s[z % NEAR * PLANE + p, z // NEAR, a] = term[
                    z * block : (z + 1) * block, p * LANES : (p + 1) * LANES
                ].astype(term_s.dtype)
    at, outer_at = near_index(), lax.axis_index("dp") // NEAR
    for k, out_ref in enumerate(out_refs):
        for j in range(outers):
            out_ref[j] = term_s[at ^ k, outer_at ^ j]


def input_kernel(pre_hbm, grad_hbm, their_grad_ref, near_ref, kernel_hbm, out_ref, pre_ref, grad_ref, kernel_ref, taps_s, sem):
    rows, chans, width = pre_ref.shape
    first = my_core() == 0
    order = [(grad_hbm.at[r], grad_ref.at[r]) for r in range(rows)]
    order += [(kernel_hbm.at[a], kernel_ref.at[a]) for a in range(3)]
    order += [(pre_hbm.at[r], pre_ref.at[r]) for r in range(rows)]
    copies = fetch(order, sem)
    for copy in copies:
        copy.wait()
    for r in range(rows + 2):
        if r == 0:
            row = jnp.where(first, near_ref[...], their_grad_ref[rows - 1])
        elif r == rows + 1:
            row = jnp.where(first, their_grad_ref[0], near_ref[...])
        else:
            row = grad_ref[r - 1]
        put_taps(taps_s, r, row)
    step = 2
    for top in range(0, rows, step):
        total = jnp.zeros((chans, step * width), F32)
        for a in range(3):
            at = (top + 2 - a) * width
            for b in range(3):
                taps = taps_s[b * chans : (b + 1) * chans, at : at + step * width]
                total += jnp.dot(kernel_ref[a, b], taps, preferred_element_type=F32)
        for r in range(step):
            x = pre_ref[top + r].astype(F32)
            sig = 1.0 / (1.0 + jnp.exp(-x))
            deriv = sig * (1.0 + x * (1.0 - sig))
            out_ref[top + r] = (total[:, r * width : (r + 1) * width] * deriv).astype(out_ref.dtype)


def place_kernel(*refs):
    parts, (out_ref, wide_s, rows_s) = refs[: PAIR * PLANE], refs[PAIR * PLANE :]
    _, block, _ = parts[0].shape
    chans = out_ref.shape[0]
    half = chans // PAIR
    core, at = my_core(), plane_index()
    for i, part in enumerate(parts):
        lanes = pl.ds(pl.multiple_of((at ^ (i % PLANE)) * LANES, LANES), LANES)
        wide_s[core ^ (i // PLANE), :, :, lanes] = part[...].astype(F32)
    for h in range(PAIR):
        for a in range(3):
            for b in range(3):
                t = 3 * a + b
                rows_s[t * block : (t + 1) * block, h * half : (h + 1) * half] = wide_s[h, a, :, b * half : (b + 1) * half]
    k = lax.broadcasted_iota(jnp.int32, (block, 9 * block), 0)
    j = lax.broadcasted_iota(jnp.int32, (block, 9 * block), 1)
    pick = jnp.concatenate([jnp.where(j - 9 * k == t, 1.0, 0.0) for t in range(9)], axis=0).astype(BF16)
    dims = (((0,), (0,)), ((), ()))
    out_ref[...] = lax.dot_general(rows_s[...].astype(BF16), pick, dims, preferred_element_type=F32)


def shards(pre_act, out_grad, kernel):
    images, rows, width, chans = pre_act.shape
    assert images == 1
    space, blocks = lax.axis_size("space"), lax.axis_size("dp")
    inner = PAIR * PLANE
    outer = space // inner
    block = chans // blocks
    half = chans // PAIR
    far = blocks // NEAR
    factor = float(images * rows * width * space * blocks) ** (-0.5)
    params = pltpu.CompilerParams(vmem_limit_bytes=VMEM_LIMIT)
    core = my_core()
    flops = 2 * 9 * chans * chans * rows * width

    pre = jnp.swapaxes(pre_act[0], 1, 2)
    grad = jnp.swapaxes(out_grad[0], 1, 2)
    edge = lax.dynamic_index_in_dim(grad, core * (rows - 1), 0, keepdims=False)
    beyond = [(i, i + 1 if i % 2 else i - 1) for i in range(space)]
    beyond_two = [(i, i + 2 if i % 2 else i - 2) for i in range(space)]
    pairs = [(i, i + 1 - 2 * (i % 2)) for i in range(space)]

    def inside(moves):
        return [(i, j) for i, j in moves if 0 <= j < space]

    near_row = lax.ppermute(edge, "space", inside(beyond))
    far_row = lax.ppermute(edge, "space", inside(beyond_two))
    their_grad = lax.ppermute(grad, "space", pairs)
    their_pre = lax.ppermute(pre, "space", pairs)

    row_block = pltpu.VMEM((rows, chans, width), BF16)
    own, act_edge, grad_edge = pl.pallas_call(
        own_kernel,
        out_shape=(
            jax.ShapeDtypeStruct((3, chans, PLANE * LANES), F32),
            jax.ShapeDtypeStruct((2, chans, width), BF16),
            jax.ShapeDtypeStruct((2, half, width), BF16),
        ),
        in_specs=[anywhere()] * 2,
        out_specs=(vmem(),) * 3,
        scratch_shapes=[
            row_block,
            row_block,
            pltpu.VMEM((chans, rows * width), BF16),
            pltpu.VMEM((PLANE * LANES, (rows + 2) * width), BF16),
            pltpu.SemaphoreType.DMA((2 * rows,)),
        ],
        compiler_params=params,
        cost_estimate=pl.CostEstimate(flops=flops, bytes_accessed=4000000, transcendentals=rows * width * chans),
        name="own_terms",
    )(pre, grad)
    piece = jax.ShapeDtypeStruct((far, 3, block, LANES), BF16)
    terms = pl.pallas_call(
        pair_kernel,
        out_shape=(piece,) * (NEAR * PLANE),
        in_specs=[vmem()] * 7,
        out_specs=(vmem(),) * (NEAR * PLANE),
        scratch_shapes=[
            pltpu.VMEM((chans, (rows + 2) * width), BF16),
            pltpu.VMEM((PLANE * LANES, (rows + 4) * width), BF16),
            pltpu.VMEM((NEAR * PLANE, far, 3, block, LANES), BF16),
        ],
        compiler_params=params,
        cost_estimate=pl.CostEstimate(flops=flops, bytes_accessed=4000000, transcendentals=rows * width * chans),
        name="pair_terms",
    )(own, act_edge, grad_edge, their_pre, their_grad, near_row, far_row)

    got = [terms[0]]
    for k in range(NEAR * PLANE - 1, 0, -1):
        moves = []
        for z in range(blocks):
            for i in range(space):
                to_z, to_i = z ^ (k // PLANE), i ^ (k % PLANE * PAIR)
                moves.append((z * space + i, to_z * space + to_i))
        got.append(lax.ppermute(terms[k], ("dp", "space"), moves))

    in_grad = pl.pallas_call(
        input_kernel,
        out_shape=jax.ShapeDtypeStruct((rows, chans, width), BF16),
        in_specs=[anywhere(), anywhere(), vmem(), vmem(), anywhere()],
        out_specs=vmem(),
        scratch_shapes=[
            row_block,
            row_block,
            pltpu.VMEM(kernel.shape, BF16),
            pltpu.VMEM((3 * chans, (rows + 2) * width), BF16),
            pltpu.SemaphoreType.DMA((2 * rows + 3,)),
        ],
        compiler_params=params,
        cost_estimate=pl.CostEstimate(flops=flops, bytes_accessed=4000000, transcendentals=rows * width * chans),
        name="input_grad",
    )(pre, grad, their_grad, near_row, kernel)
    *got, in_grad = lax.optimization_barrier((*got, in_grad))

    near_sum = sum(part.astype(F32) for part in got)
    total = near_sum[0]
    for k in range(1, far):
        moves = [(z, z ^ (k * NEAR)) for z in range(blocks)]
        total = total + lax.ppermute(near_sum[k].astype(BF16), "dp", moves).astype(F32)
    total = total * factor
    if outer > 1:
        total = lax.psum(total, "space", axis_index_groups=[[o * inner + i for o in range(outer)] for i in range(inner)])
    final = total.astype(BF16)
    parts = [final]
    for k in range(1, PLANE):
        parts.append(lax.ppermute(final, "space", [(i, i ^ (k * PAIR)) for i in range(space)]))
    parts += [lax.ppermute(part, "space", pairs) for part in parts]

    placed = pl.pallas_call(
        place_kernel,
        out_shape=jax.ShapeDtypeStruct((chans, 9 * block), F32),
        in_specs=[vmem()] * inner,
        out_specs=vmem(),
        scratch_shapes=[
            pltpu.VMEM((PAIR, 3, block, PLANE * LANES), F32),
            pltpu.VMEM((9 * block, chans), F32),
        ],
        compiler_params=params,
        cost_estimate=pl.CostEstimate(flops=2 * 81 * block * block * chans, bytes_accessed=2000000, transcendentals=0),
        name="place_rows",
    )(*parts)
    return jnp.swapaxes(in_grad, 1, 2)[None], placed.T


def solution(mesh):
    placed = (P("dp", "space", None, None), P("dp", "space", None, None), P())
    return jax.shard_map(
        shards,
        mesh=mesh,
        in_specs=placed,
        out_specs=(P("dp", "space", None, None), P("dp", None)),
        check_vma=False,
    )
```

```python
import functools

import jax
import jax.numpy as jnp
from jax import lax
from jax.experimental import pallas as pl
from jax.experimental.pallas import tpu as pltpu
from jax.sharding import PartitionSpec as P

F32 = jnp.float32
BF16 = jnp.bfloat16
LANES = 128
PAIR = 2
PLANE = 4
NEAR = 2
VMEM_LIMIT = 48 * 1024 * 1024
NT = (((1,), (1,)), ((), ()))


def vmem():
    return pl.BlockSpec(memory_space=pltpu.VMEM)


def anywhere():
    return pl.BlockSpec(memory_space=pl.ANY)


def column_shifts(row):
    wide = row.astype(F32)
    width = wide.shape[1]
    at = lax.broadcasted_iota(jnp.int32, wide.shape, 1)
    ahead = jnp.where(at == width - 1, 0.0, pltpu.roll(wide, width - 1, 1))
    behind = jnp.where(at == 0, 0.0, pltpu.roll(wide, 1, 1))
    return ahead.astype(BF16), row, behind.astype(BF16)


def put_taps(taps_s, slot, row):
    half, width = row.shape
    for b, shifted in enumerate(column_shifts(row)):
        taps_s[b * half : (b + 1) * half, slot * width : (slot + 1) * width] = shifted


def plane_index():
    return lax.rem(lax.axis_index("space") // PAIR, PLANE)


def near_index():
    return lax.rem(lax.axis_index("dp"), NEAR) * PLANE + plane_index()


def silu(v):
    x = v.astype(F32)
    return (x / (1.0 + jnp.exp(-x))).astype(BF16)


def my_core():
    return lax.rem(lax.axis_index("space"), PAIR)


def edge_kernel(pre_ref, grad_ref, out_ref):
    row = my_core() * (pre_ref.shape[0] - 1)
    out_ref[0] = grad_ref[row]
    out_ref[1] = pre_ref[row]


def own_kernel(pre_ref, grad_ref, term_ref, act_edge_ref, grad_edge_ref, act_s, taps_s):
    rows, chans, width = pre_ref.shape
    half = chans // PAIR
    mine = pl.ds(pl.multiple_of(my_core() * half, half), half)
    zero = jnp.zeros((half, width), BF16)
    taps_s[3 * half :, :] = jnp.zeros((taps_s.shape[0] - 3 * half, taps_s.shape[1]), BF16)
    for r in range(rows + 2):
        put_taps(taps_s, r, grad_ref[r - 1, mine, :] if 0 < r <= rows else zero)
    for r in range(rows):
        act_s[:, r * width : (r + 1) * width] = silu(pre_ref[r])
    for i, r in enumerate((0, rows - 1)):
        act_edge_ref[i] = act_s[:, r * width : (r + 1) * width]
        grad_edge_ref[i] = grad_ref[r, mine, :]
    for a in range(3):
        at = (2 - a) * width
        term_ref[a] = lax.dot_general(act_s[...], taps_s[:, at : at + rows * width], NT, preferred_element_type=F32)


def pair_kernel(term_ref, act_edge_ref, grad_edge_ref, their_pre_ref, their_grad_ref, near_ref, *refs):
    out_refs, (act_s, taps_s, term_s) = refs[: PLANE * NEAR], refs[PLANE * NEAR :]
    rows, chans, width = their_pre_ref.shape
    half = chans // PAIR
    outers, _, block, _ = out_refs[0].shape
    core = my_core()
    first = core == 0
    mine = pl.ds(pl.multiple_of(core * half, half), half)
    taps_s[3 * half :, :] = jnp.zeros((taps_s.shape[0] - 3 * half, taps_s.shape[1]), BF16)
    for r in range(rows):
        act_s[:, (2 + r) * width : (3 + r) * width] = silu(their_pre_ref[r])
    near_act = silu(near_ref[1])
    their_top = act_s[:, 2 * width : 3 * width]
    their_end = act_s[:, (rows + 1) * width : (rows + 2) * width]
    extra = ((0, their_top, act_edge_ref[0]), (1, act_edge_ref[0], near_act))
    extra += ((rows + 2, act_edge_ref[1], their_end), (rows + 3, near_act, act_edge_ref[1]))
    for slot, if_first, if_second in extra:
        act_s[:, slot * width : (slot + 1) * width] = jnp.where(first, if_first, if_second)
    near_grad = near_ref[0, mine, :]
    their_top, their_end = their_grad_ref[0, mine, :], their_grad_ref[rows - 1, mine, :]
    zero = jnp.zeros((half, width), BF16)
    put_taps(taps_s, 0, jnp.where(first, grad_edge_ref[1], their_end))
    put_taps(taps_s, 1, jnp.where(first, near_grad, grad_edge_ref[1]))
    put_taps(taps_s, 2, zero)
    for r in range(rows):
        put_taps(taps_s, 3 + r, their_grad_ref[r, mine, :])
    put_taps(taps_s, rows + 3, zero)
    put_taps(taps_s, rows + 4, jnp.where(first, their_top, grad_edge_ref[0]))
    put_taps(taps_s, rows + 5, jnp.where(first, grad_edge_ref[0], near_grad))
    for a, (left, right, at) in enumerate(((2, rows + 4, 4), (2, rows + 2, 3), (0, rows + 2, 0))):
        term = term_ref[a] + lax.dot_general(
            act_s[:, left * width : right * width],
            taps_s[:, at * width : (at + right - left) * width],
            NT,
            preferred_element_type=F32,
        )
        for p in range(PLANE):
            for z in range(NEAR * outers):
                term_s[z % NEAR * PLANE + p, z // NEAR, a] = term[
                    z * block : (z + 1) * block, p * LANES : (p + 1) * LANES
                ].astype(term_s.dtype)
    at, outer_at = near_index(), lax.axis_index("dp") // NEAR
    for k, out_ref in enumerate(out_refs):
        for j in range(outers):
            out_ref[j] = term_s[at ^ k, outer_at ^ j]


def input_kernel(start, pre_ref, grad_ref, their_grad_ref, near_ref, kernel_ref, *refs):
    out_ref, taps_s = refs[-2:]
    rows, chans, width = pre_ref.shape
    count = out_ref.shape[0]
    first = my_core() == 0
    for r in range(count + 2):
        at = start + r
        if at == 0:
            row = jnp.where(first, near_ref[0], their_grad_ref[rows - 1])
        elif at == rows + 1:
            row = jnp.where(first, their_grad_ref[0], near_ref[0])
        else:
            row = grad_ref[at - 1]
        put_taps(taps_s, r, row)
    step = 2
    for top in range(0, count, step):
        total = jnp.zeros((chans, step * width), F32)
        for a in range(3):
            at = (top + 2 - a) * width
            for b in range(3):
                taps = taps_s[b * chans : (b + 1) * chans, at : at + step * width]
                total += jnp.dot(kernel_ref[a, b], taps, preferred_element_type=F32)
        for r in range(step):
            x = pre_ref[start + top + r].astype(F32)
            sig = 1.0 / (1.0 + jnp.exp(-x))
            deriv = sig * (1.0 + x * (1.0 - sig))
            out_ref[top + r] = (total[:, r * width : (r + 1) * width] * deriv).astype(out_ref.dtype)


def pick_kernel(out_ref):
    taps = 9
    block = out_ref.shape[0] // taps
    k = lax.broadcasted_iota(jnp.int32, (block, taps * block), 0)
    j = lax.broadcasted_iota(jnp.int32, (block, taps * block), 1)
    for t in range(taps):
        out_ref[t * block : (t + 1) * block, :] = jnp.where(j - taps * k == t, 1.0, 0.0).astype(BF16)


def place_kernel(flip, parts_ref, pick_ref, *refs):
    out_hbm, wide_s, rows_s, out_s, sem = refs[-5:]
    _, _, block, _ = parts_ref.shape
    half = out_s.shape[0]
    for k in range(PLANE):
        lanes = pl.ds(pl.multiple_of((plane_index() ^ k) * LANES, LANES), LANES)
        wide_s[:, :, lanes] = parts_ref[k].astype(F32)
    for a in range(3):
        for b in range(3):
            t = 3 * a + b
            rows_s[t * block : (t + 1) * block, :] = wide_s[a, :, b * half : (b + 1) * half]
    dims = (((0,), (0,)), ((), ()))
    out_s[...] = lax.dot_general(rows_s[...].astype(BF16), pick_ref[...], dims, preferred_element_type=F32)
    count = sem.shape[0]
    step = half // count
    first = (my_core() ^ flip) * half
    copies = []
    for i in range(count):
        to = pl.ds(pl.multiple_of(first + i * step, 8), step)
        copies.append(pltpu.make_async_copy(out_s.at[pl.ds(i * step, step)], out_hbm.at[to], sem.at[i]))
        copies[-1].start()
    for copy in copies:
        copy.wait()


def shards(pre_act, out_grad, kernel):
    images, rows, width, chans = pre_act.shape
    assert images == 1
    space, blocks = lax.axis_size("space"), lax.axis_size("dp")
    inner = PAIR * PLANE
    outer = space // inner
    block = chans // blocks
    half = chans // PAIR
    far = blocks // NEAR
    factor = float(images * rows * width * space * blocks) ** (-0.5)
    params = pltpu.CompilerParams(vmem_limit_bytes=VMEM_LIMIT)
    flops = 2 * 9 * chans * chans * rows * width

    pre = jnp.swapaxes(pre_act[0], 1, 2)
    grad = jnp.swapaxes(out_grad[0], 1, 2)
    edge = pl.pallas_call(
        edge_kernel,
        out_shape=jax.ShapeDtypeStruct((2, chans, width), BF16),
        in_specs=[vmem()] * 2,
        out_specs=vmem(),
        compiler_params=params,
        name="edge_rows",
    )(pre, grad)
    beyond = [(i, i + 1 if i % 2 else i - 1) for i in range(space)]
    pairs = [(i, i + 1 - 2 * (i % 2)) for i in range(space)]

    def inside(moves):
        return [(i, j) for i, j in moves if 0 <= j < space]

    near_row = lax.ppermute(edge, "space", inside(beyond))
    their_grad = lax.ppermute(grad, "space", pairs)
    their_pre = lax.ppermute(pre, "space", pairs)

    own, act_edge, grad_edge = pl.pallas_call(
        own_kernel,
        out_shape=(
            jax.ShapeDtypeStruct((3, chans, PLANE * LANES), F32),
            jax.ShapeDtypeStruct((2, chans, width), BF16),
            jax.ShapeDtypeStruct((2, half, width), BF16),
        ),
        in_specs=[vmem()] * 2,
        out_specs=(vmem(),) * 3,
        scratch_shapes=[
            pltpu.VMEM((chans, rows * width), BF16),
            pltpu.VMEM((PLANE * LANES, (rows + 2) * width), BF16),
        ],
        compiler_params=params,
        cost_estimate=pl.CostEstimate(flops=flops, bytes_accessed=4000000, transcendentals=rows * width * chans),
        name="own_terms",
    )(pre, grad)
    piece = jax.ShapeDtypeStruct((far, 3, block, LANES), BF16)
    terms = pl.pallas_call(
        pair_kernel,
        out_shape=(piece,) * (NEAR * PLANE),
        in_specs=[vmem()] * 6,
        out_specs=(vmem(),) * (NEAR * PLANE),
        scratch_shapes=[
            pltpu.VMEM((chans, (rows + 4) * width), BF16),
            pltpu.VMEM((PLANE * LANES, (rows + 6) * width), BF16),
            pltpu.VMEM((NEAR * PLANE, far, 3, block, LANES), BF16),
        ],
        compiler_params=params,
        cost_estimate=pl.CostEstimate(flops=flops, bytes_accessed=4000000, transcendentals=rows * width * chans),
        name="pair_terms",
    )(own, act_edge, grad_edge, their_pre, their_grad, near_row)

    got = [terms[0]]
    for k in range(NEAR * PLANE - 1, 0, -1):
        moves = []
        for z in range(blocks):
            for i in range(space):
                to_z, to_i = z ^ (k // PLANE), i ^ (k % PLANE * PAIR)
                moves.append((z * space + i, to_z * space + to_i))
        got.append(lax.ppermute(terms[k], ("dp", "space"), moves))

    def input_part(part, *before):
        count = rows // 2
        return pl.pallas_call(
            functools.partial(input_kernel, part * count),
            grid=(1,),
            out_shape=jax.ShapeDtypeStruct((rows, chans, width), BF16),
            in_specs=[vmem()] * 5 + [anywhere()] * len(before),
            out_specs=pl.BlockSpec((count, chans, width), lambda i: (part, 0, 0)),
            scratch_shapes=[pltpu.VMEM((3 * chans, (count + 2) * width), BF16)],
            input_output_aliases={5: 0} if before else {},
            compiler_params=params,
            cost_estimate=pl.CostEstimate(
                flops=flops // 2, bytes_accessed=3000000, transcendentals=rows * width * chans // 2
            ),
            name="input_grad",
        )(pre, grad, their_grad, near_row, kernel, *before)

    pick = pl.pallas_call(
        pick_kernel,
        out_shape=jax.ShapeDtypeStruct((9 * block, 9 * block), BF16),
        out_specs=vmem(),
        name="pick_rows",
    )()
    in_grad = input_part(0)
    *got, in_grad, pick = lax.optimization_barrier((*got, in_grad, pick))

    near_sum = sum(part.astype(F32) for part in got)
    others = []
    for k in range(1, far):
        moves = [(z, z ^ (k * NEAR)) for z in range(blocks)]
        others.append(lax.ppermute(near_sum[k].astype(BF16), "dp", moves))
    in_grad = input_part(1, in_grad)
    *others, in_grad = lax.optimization_barrier((*others, in_grad))
    total = near_sum[0] + sum(other.astype(F32) for other in others)
    total = total * factor
    if outer > 1:
        total = lax.psum(total, "space", axis_index_groups=[[o * inner + i for o in range(outer)] for i in range(inner)])
    final = total.astype(BF16)
    parts = [final]
    for k in range(1, PLANE):
        parts.append(lax.ppermute(final, "space", [(i, i ^ (k * PAIR)) for i in range(space)]))
    parts = jnp.stack(parts)
    their_parts = lax.ppermute(parts, "space", pairs)

    def place(flip, parts, *before):
        return pl.pallas_call(
            functools.partial(place_kernel, flip),
            out_shape=jax.ShapeDtypeStruct((chans, 9 * block), F32),
            in_specs=[vmem()] * 2 + [anywhere()] * len(before),
            out_specs=anywhere(),
            scratch_shapes=[
                pltpu.VMEM((3, block, PLANE * LANES), F32),
                pltpu.VMEM((9 * block, half), F32),
                pltpu.VMEM((half, 9 * block), F32),
                pltpu.SemaphoreType.DMA((4,)),
            ],
            input_output_aliases={2: 0} if before else {},
            compiler_params=params,
            cost_estimate=pl.CostEstimate(flops=81 * block * block * chans, bytes_accessed=1000000, transcendentals=0),
            name="place_rows",
        )(parts, pick, *before)

    placed = place(1, their_parts, place(0, parts))
    return jnp.swapaxes(in_grad, 1, 2)[None], placed.T


def solution(mesh):
    placed = (P("dp", "space", None, None), P("dp", "space", None, None), P())
    return jax.shard_map(
        shards,
        mesh=mesh,
        in_specs=placed,
        out_specs=(P("dp", "space", None, None), P("dp", None)),
        check_vma=False,
    )
```

```python
import functools

import jax
import jax.numpy as jnp
from jax import lax
from jax.experimental import pallas as pl
from jax.experimental.pallas import tpu as pltpu
from jax.sharding import PartitionSpec as P

F32 = jnp.float32
BF16 = jnp.bfloat16
LANES = 128
PAIR = 2
PLANE = 4
NEAR = 2
VMEM_LIMIT = 16 * 1024 * 1024
NT = (((1,), (1,)), ((), ()))


def vmem():
    return pl.BlockSpec(memory_space=pltpu.VMEM)


def anywhere():
    return pl.BlockSpec(memory_space=pl.ANY)


def column_shifts(row):
    wide = row.astype(F32)
    width = wide.shape[1]
    at = lax.broadcasted_iota(jnp.int32, wide.shape, 1)
    ahead = jnp.where(at == width - 1, 0.0, pltpu.roll(wide, width - 1, 1))
    behind = jnp.where(at == 0, 0.0, pltpu.roll(wide, 1, 1))
    return ahead.astype(BF16), row, behind.astype(BF16)


def put_taps(taps_s, slot, row):
    half, width = row.shape
    for b, shifted in enumerate(column_shifts(row)):
        taps_s[b * half : (b + 1) * half, slot * width : (slot + 1) * width] = shifted


def plane_index():
    return lax.rem(lax.axis_index("space") // PAIR, PLANE)


def near_index():
    return lax.rem(lax.axis_index("dp"), NEAR) * PLANE + plane_index()


def silu(v):
    x = v.astype(F32)
    return (x / (1.0 + jnp.exp(-x))).astype(BF16)


def my_core():
    return lax.rem(lax.axis_index("space"), PAIR)


def own_kernel(pre_ref, grad_ref, term_ref, act_edge_ref, grad_edge_ref, act_s, taps_s):
    rows, chans, width = pre_ref.shape
    half = chans // PAIR
    mine = pl.ds(pl.multiple_of(my_core() * half, half), half)
    zero = jnp.zeros((half, width), BF16)
    taps_s[3 * half :, :] = jnp.zeros((taps_s.shape[0] - 3 * half, taps_s.shape[1]), BF16)
    for r in range(rows + 2):
        put_taps(taps_s, r, grad_ref[r - 1, mine, :] if 0 < r <= rows else zero)
    for r in range(rows):
        act_s[:, r * width : (r + 1) * width] = silu(pre_ref[r])
    for i, r in enumerate((0, rows - 1)):
        act_edge_ref[i] = act_s[:, r * width : (r + 1) * width]
        grad_edge_ref[i] = grad_ref[r, mine, :]
    for a in range(3):
        at = (2 - a) * width
        term_ref[a] = lax.dot_general(act_s[...], taps_s[:, at : at + rows * width], NT, preferred_element_type=F32)


def pair_kernel(term_ref, act_edge_ref, grad_edge_ref, their_pre_ref, their_grad_ref, near_ref, *refs):
    out_refs, (act_s, taps_s, term_s) = refs[: PLANE * NEAR], refs[PLANE * NEAR :]
    rows, chans, width = their_pre_ref.shape
    half = chans // PAIR
    outers, _, block, _ = out_refs[0].shape
    core = my_core()
    first = core == 0
    mine = pl.ds(pl.multiple_of(core * half, half), half)
    taps_s[3 * half :, :] = jnp.zeros((taps_s.shape[0] - 3 * half, taps_s.shape[1]), BF16)
    for r in range(rows):
        act_s[:, (2 + r) * width : (3 + r) * width] = silu(their_pre_ref[r])
    near_act = silu(near_ref[1])
    their_top = act_s[:, 2 * width : 3 * width]
    their_end = act_s[:, (rows + 1) * width : (rows + 2) * width]
    extra = ((0, their_top, act_edge_ref[0]), (1, act_edge_ref[0], near_act))
    extra += ((rows + 2, act_edge_ref[1], their_end), (rows + 3, near_act, act_edge_ref[1]))
    for slot, if_first, if_second in extra:
        act_s[:, slot * width : (slot + 1) * width] = jnp.where(first, if_first, if_second)
    near_grad = near_ref[0, mine, :]
    their_top, their_end = their_grad_ref[0, mine, :], their_grad_ref[rows - 1, mine, :]
    zero = jnp.zeros((half, width), BF16)
    put_taps(taps_s, 0, jnp.where(first, grad_edge_ref[1], their_end))
    put_taps(taps_s, 1, jnp.where(first, near_grad, grad_edge_ref[1]))
    put_taps(taps_s, 2, zero)
    for r in range(rows):
        put_taps(taps_s, 3 + r, their_grad_ref[r, mine, :])
    put_taps(taps_s, rows + 3, zero)
    put_taps(taps_s, rows + 4, jnp.where(first, their_top, grad_edge_ref[0]))
    put_taps(taps_s, rows + 5, jnp.where(first, grad_edge_ref[0], near_grad))
    for a, (left, right, at) in enumerate(((2, rows + 4, 4), (2, rows + 2, 3), (0, rows + 2, 0))):
        term = term_ref[a] + lax.dot_general(
            act_s[:, left * width : right * width],
            taps_s[:, at * width : (at + right - left) * width],
            NT,
            preferred_element_type=F32,
        )
        for p in range(PLANE):
            for z in range(NEAR * outers):
                term_s[z % NEAR * PLANE + p, z // NEAR, a] = term[
                    z * block : (z + 1) * block, p * LANES : (p + 1) * LANES
                ].astype(term_s.dtype)
    at, outer_at = near_index(), lax.axis_index("dp") // NEAR
    for k, out_ref in enumerate(out_refs):
        for j in range(outers):
            out_ref[j] = term_s[at ^ k, outer_at ^ j]


def input_kernel(side, pre_ref, grad_ref, edge_ref, kernel_ref, *refs):
    out_hbm, taps_s, out_s, sem = refs[-4:]
    rows, chans, width = pre_ref.shape
    count = rows // 2
    upper = my_core() == side
    start = jnp.where(upper, 0, count)
    put_taps(taps_s, 0, jnp.where(upper, edge_ref[0], grad_ref[count - 1]))
    for r in range(count):
        put_taps(taps_s, r + 1, grad_ref[start + r])
    put_taps(taps_s, count + 1, jnp.where(upper, grad_ref[count], edge_ref[0]))
    step = 2
    copies = []
    for top in range(0, count, step):
        total = jnp.zeros((chans, step * width), F32)
        for a in range(3):
            at = (top + 2 - a) * width
            for b in range(3):
                taps = taps_s[b * chans : (b + 1) * chans, at : at + step * width]
                total += jnp.dot(kernel_ref[a, b], taps, preferred_element_type=F32)
        for r in range(step):
            x = pre_ref[start + top + r].astype(F32)
            sig = 1.0 / (1.0 + jnp.exp(-x))
            deriv = sig * (1.0 + x * (1.0 - sig))
            out_s[top + r] = (total[:, r * width : (r + 1) * width] * deriv).astype(out_s.dtype)
        copies.append(
            pltpu.make_async_copy(
                out_s.at[pl.ds(top, step)], out_hbm.at[pl.ds(start + top, step)], sem.at[top // step]
            )
        )
        copies[-1].start()
    for copy in copies:
        copy.wait()


def pick_kernel(after_ref, out_ref):
    taps = 9
    block = out_ref.shape[0] // taps
    k = lax.broadcasted_iota(jnp.int32, (block, taps * block), 0)
    j = lax.broadcasted_iota(jnp.int32, (block, taps * block), 1)
    for t in range(taps):
        out_ref[t * block : (t + 1) * block, :] = jnp.where(j - taps * k == t, 1.0, 0.0).astype(BF16)


def place_kernel(flip, parts_ref, pick_ref, *refs):
    out_hbm, wide_s, rows_s, out_s, sem = refs[-5:]
    _, _, block, _ = parts_ref.shape
    half = out_s.shape[0]
    for k in range(PLANE):
        lanes = pl.ds(pl.multiple_of((plane_index() ^ k) * LANES, LANES), LANES)
        wide_s[:, :, lanes] = parts_ref[k].astype(F32)
    for a in range(3):
        for b in range(3):
            t = 3 * a + b
            rows_s[t * block : (t + 1) * block, :] = wide_s[a, :, b * half : (b + 1) * half]
    dims = (((0,), (0,)), ((), ()))
    out_s[...] = lax.dot_general(rows_s[...].astype(BF16), pick_ref[...], dims, preferred_element_type=F32)
    count = sem.shape[0]
    step = half // count
    first = (my_core() ^ flip) * half
    copies = []
    for i in range(count):
        to = pl.ds(pl.multiple_of(first + i * step, 8), step)
        copies.append(pltpu.make_async_copy(out_s.at[pl.ds(i * step, step)], out_hbm.at[to], sem.at[i]))
        copies[-1].start()
    for copy in copies:
        copy.wait()


def shards(pre_act, out_grad, kernel):
    images, rows, width, chans = pre_act.shape
    assert images == 1
    space, blocks = lax.axis_size("space"), lax.axis_size("dp")
    inner = PAIR * PLANE
    outer = space // inner
    block = chans // blocks
    half = chans // PAIR
    far = blocks // NEAR
    factor = float(images * rows * width * space * blocks) ** (-0.5)
    params = pltpu.CompilerParams(vmem_limit_bytes=VMEM_LIMIT)
    flops = 2 * 9 * chans * chans * rows * width

    pre = jnp.swapaxes(pre_act[0], 1, 2)
    grad = jnp.swapaxes(out_grad[0], 1, 2)
    row = my_core() * (rows - 1)
    edge = jnp.stack([lax.dynamic_index_in_dim(grad, row, 0, False), lax.dynamic_index_in_dim(pre, row, 0, False)])
    beyond = [(i, i + 1 if i % 2 else i - 1) for i in range(space)]
    pairs = [(i, i + 1 - 2 * (i % 2)) for i in range(space)]

    def inside(moves):
        return [(i, j) for i, j in moves if 0 <= j < space]

    near_row = lax.ppermute(edge, "space", inside(beyond))
    pick = pl.pallas_call(
        pick_kernel,
        out_shape=jax.ShapeDtypeStruct((9 * block, 9 * block), BF16),
        in_specs=[anywhere()],
        out_specs=vmem(),
        compiler_params=params,
        cost_estimate=pl.CostEstimate(flops=flops, bytes_accessed=4000000, transcendentals=0),
        name="pick_rows",
    )(edge)
    own, act_edge, grad_edge = pl.pallas_call(
        own_kernel,
        out_shape=(
            jax.ShapeDtypeStruct((3, chans, PLANE * LANES), F32),
            jax.ShapeDtypeStruct((2, chans, width), BF16),
            jax.ShapeDtypeStruct((2, half, width), BF16),
        ),
        in_specs=[vmem()] * 2,
        out_specs=(vmem(),) * 3,
        scratch_shapes=[
            pltpu.VMEM((chans, rows * width), BF16),
            pltpu.VMEM((PLANE * LANES, (rows + 2) * width), BF16),
        ],
        compiler_params=params,
        cost_estimate=pl.CostEstimate(flops=flops, bytes_accessed=4000000, transcendentals=rows * width * chans),
        name="own_terms",
    )(pre, grad)
    near_row, pick, own, act_edge, grad_edge, my_pre, my_grad = lax.optimization_barrier(
        (near_row, pick, own, act_edge, grad_edge, pre, grad)
    )
    their_grad = lax.ppermute(my_grad, "space", pairs)
    their_pre = lax.ppermute(my_pre, "space", pairs)
    def input_part(side, edge_rows, *before):
        count = rows // 2
        return pl.pallas_call(
            functools.partial(input_kernel, side),
            out_shape=jax.ShapeDtypeStruct((rows, chans, width), BF16),
            in_specs=[vmem()] * 4 + [anywhere()] * len(before),
            out_specs=anywhere(),
            scratch_shapes=[
                pltpu.VMEM((3 * chans, (count + 2) * width), BF16),
                pltpu.VMEM((count, chans, width), BF16),
                pltpu.SemaphoreType.DMA((count // 2,)),
            ],
            input_output_aliases={4: 0} if before else {},
            compiler_params=params,
            cost_estimate=pl.CostEstimate(
                flops=flops // 2, bytes_accessed=3000000, transcendentals=rows * width * chans // 2
            ),
            name="input_grad",
        )(pre, grad, edge_rows, kernel, *before)

    in_grad = input_part(0, near_row)
    their_grad, their_pre, in_grad = lax.optimization_barrier((their_grad, their_pre, in_grad))
    piece = jax.ShapeDtypeStruct((far, 3, block, LANES), BF16)
    terms = pl.pallas_call(
        pair_kernel,
        out_shape=(piece,) * (NEAR * PLANE),
        in_specs=[vmem()] * 6,
        out_specs=(vmem(),) * (NEAR * PLANE),
        scratch_shapes=[
            pltpu.VMEM((chans, (rows + 4) * width), BF16),
            pltpu.VMEM((PLANE * LANES, (rows + 6) * width), BF16),
            pltpu.VMEM((NEAR * PLANE, far, 3, block, LANES), BF16),
        ],
        compiler_params=params,
        cost_estimate=pl.CostEstimate(flops=flops, bytes_accessed=4000000, transcendentals=rows * width * chans),
        name="pair_terms",
    )(own, act_edge, grad_edge, their_pre, their_grad, near_row)

    got = [terms[0]]
    for k in range(NEAR * PLANE - 1, 0, -1):
        moves = []
        for z in range(blocks):
            for i in range(space):
                to_z, to_i = z ^ (k // PLANE), i ^ (k % PLANE * PAIR)
                moves.append((z * space + i, to_z * space + to_i))
        got.append(lax.ppermute(terms[k], ("dp", "space"), moves))


    their_edge = lax.dynamic_index_in_dim(their_grad, my_core() * (rows - 1), 0)
    in_grad = input_part(1, their_edge, in_grad)
    *got, in_grad = lax.optimization_barrier((*got, in_grad))

    near_sum = sum(part.astype(F32) for part in got)
    others = []
    for k in range(1, far):
        moves = [(z, z ^ (k * NEAR)) for z in range(blocks)]
        others.append(lax.ppermute(near_sum[k].astype(BF16), "dp", moves))
    total = near_sum[0] + sum(other.astype(F32) for other in others)
    total = total * factor
    if outer > 1:
        total = lax.psum(total, "space", axis_index_groups=[[o * inner + i for o in range(outer)] for i in range(inner)])
    final = total.astype(BF16)
    parts = [final]
    for k in range(1, PLANE):
        parts.append(lax.ppermute(final, "space", [(i, i ^ (k * PAIR)) for i in range(space)]))
    parts = jnp.stack(parts)
    their_parts = lax.ppermute(parts, "space", pairs)

    def place(flip, parts, *before):
        return pl.pallas_call(
            functools.partial(place_kernel, flip),
            out_shape=jax.ShapeDtypeStruct((chans, 9 * block), F32),
            in_specs=[vmem()] * 2 + [anywhere()] * len(before),
            out_specs=anywhere(),
            scratch_shapes=[
                pltpu.VMEM((3, block, PLANE * LANES), F32),
                pltpu.VMEM((9 * block, half), F32),
                pltpu.VMEM((half, 9 * block), F32),
                pltpu.SemaphoreType.DMA((4,)),
            ],
            input_output_aliases={2: 0} if before else {},
            compiler_params=params,
            cost_estimate=pl.CostEstimate(flops=81 * block * block * chans, bytes_accessed=1000000, transcendentals=0),
            name="place_rows",
        )(parts, pick, *before)

    placed = place(1, their_parts, place(0, parts))
    return jnp.swapaxes(in_grad, 1, 2)[None], placed.T


def solution(mesh):
    placed = (P("dp", "space", None, None), P("dp", "space", None, None), P())
    return jax.shard_map(
        shards,
        mesh=mesh,
        in_specs=placed,
        out_specs=(P("dp", "space", None, None), P("dp", None)),
        check_vma=False,
    )
```

```python
import functools

import jax
import jax.numpy as jnp
from jax import lax
from jax.experimental import pallas as pl
from jax.experimental.pallas import tpu as pltpu
from jax.sharding import PartitionSpec as P

F32 = jnp.float32
BF16 = jnp.bfloat16
LANES = 128
PAIR = 2
PLANE = 4
NEAR = 2
VMEM_LIMIT = 16 * 1024 * 1024
NT = (((1,), (1,)), ((), ()))


def vmem():
    return pl.BlockSpec(memory_space=pltpu.VMEM)


def anywhere():
    return pl.BlockSpec(memory_space=pl.ANY)


def column_shifts(row):
    wide = row.astype(F32)
    width = wide.shape[1]
    at = lax.broadcasted_iota(jnp.int32, wide.shape, 1)
    ahead = jnp.where(at == width - 1, 0.0, pltpu.roll(wide, width - 1, 1))
    behind = jnp.where(at == 0, 0.0, pltpu.roll(wide, 1, 1))
    return ahead.astype(BF16), row, behind.astype(BF16)


def put_taps(taps_s, slot, row):
    half, width = row.shape
    for b, shifted in enumerate(column_shifts(row)):
        taps_s[b * half : (b + 1) * half, slot * width : (slot + 1) * width] = shifted


def plane_index():
    return lax.rem(lax.axis_index("space") // PAIR, PLANE)


def near_index():
    return lax.rem(lax.axis_index("dp"), NEAR) * PLANE + plane_index()


def silu(v):
    x = v.astype(F32)
    return (x / (1.0 + jnp.exp(-x))).astype(BF16)


def my_core():
    return lax.rem(lax.axis_index("space"), PAIR)


def own_kernel(pre_ref, grad_ref, term_ref, act_edge_ref, grad_edge_ref, act_s, taps_s):
    rows, chans, width = pre_ref.shape
    half = chans // PAIR
    mine = pl.ds(pl.multiple_of(my_core() * half, half), half)
    zero = jnp.zeros((half, width), BF16)
    taps_s[3 * half :, :] = jnp.zeros((taps_s.shape[0] - 3 * half, taps_s.shape[1]), BF16)
    for r in range(rows + 2):
        put_taps(taps_s, r, grad_ref[r - 1, mine, :] if 0 < r <= rows else zero)
    for r in range(rows):
        act_s[:, r * width : (r + 1) * width] = silu(pre_ref[r])
    for i, r in enumerate((0, rows - 1)):
        act_edge_ref[i] = act_s[:, r * width : (r + 1) * width]
        grad_edge_ref[i] = grad_ref[r, mine, :]
    for a in range(3):
        at = (2 - a) * width
        term_ref[a] = lax.dot_general(act_s[...], taps_s[:, at : at + rows * width], NT, preferred_element_type=F32)


def pair_kernel(term_ref, act_edge_ref, grad_edge_ref, their_pre_ref, their_grad_ref, out_ref, act_s, taps_s):
    rows, chans, width = their_pre_ref.shape
    half = chans // PAIR
    core = my_core()
    first = core == 0
    mine = pl.ds(pl.multiple_of(core * half, half), half)
    zero = jnp.zeros((half, width), BF16)
    zero_act = jnp.zeros((chans, width), BF16)
    taps_s[3 * half :, :] = jnp.zeros((taps_s.shape[0] - 3 * half, taps_s.shape[1]), BF16)
    act_s[:, :width] = jnp.where(first, zero_act, act_edge_ref[0])
    for r in range(rows):
        act_s[:, (1 + r) * width : (2 + r) * width] = silu(their_pre_ref[r])
    act_s[:, (rows + 1) * width :] = jnp.where(first, act_edge_ref[1], zero_act)
    put_taps(taps_s, 0, their_grad_ref[rows - 1, mine, :])
    put_taps(taps_s, 1, jnp.where(first, grad_edge_ref[1], zero))
    for r in range(rows):
        put_taps(taps_s, 2 + r, their_grad_ref[r, mine, :])
    put_taps(taps_s, rows + 2, jnp.where(first, zero, grad_edge_ref[0]))
    put_taps(taps_s, rows + 3, their_grad_ref[0, mine, :])
    for a, (left, right, at) in enumerate(((1, rows + 2, 3), (1, rows + 1, 2), (0, rows + 1, 0))):
        out_ref[a] = term_ref[a] + lax.dot_general(
            act_s[:, left * width : right * width],
            taps_s[:, at * width : (at + right - left) * width],
            NT,
            preferred_element_type=F32,
        )


def edge_kernel(term_ref, act_edge_ref, grad_edge_ref, near_ref, *refs):
    out_refs, (taps_s, term_s) = refs[: PLANE * NEAR], refs[PLANE * NEAR :]
    _, chans, width = near_ref.shape
    half = chans // PAIR
    outers, _, block, _ = out_refs[0].shape
    core = my_core()
    first = core == 0
    near_act = silu(near_ref[1])
    near_grad = near_ref[0, pl.ds(pl.multiple_of(core * half, half), half), :]
    taps_s[3 * half :, :] = jnp.zeros((taps_s.shape[0] - 3 * half, taps_s.shape[1]), BF16)
    put_taps(taps_s, 0, jnp.where(first, grad_edge_ref[0], near_grad))
    put_taps(taps_s, 1, jnp.where(first, near_grad, grad_edge_ref[1]))
    acts = {0: jnp.where(first, near_act, act_edge_ref[1]), 2: jnp.where(first, act_edge_ref[0], near_act)}
    for a in range(3):
        term = term_ref[a]
        if a in acts:
            taps = taps_s[:, a // 2 * width : (a // 2 + 1) * width]
            term += lax.dot_general(acts[a], taps, NT, preferred_element_type=F32)
        for p in range(PLANE):
            for z in range(NEAR * outers):
                term_s[z % NEAR * PLANE + p, z // NEAR, a] = term[
                    z * block : (z + 1) * block, p * LANES : (p + 1) * LANES
                ].astype(term_s.dtype)
    at, outer_at = near_index(), lax.axis_index("dp") // NEAR
    for k, out_ref in enumerate(out_refs):
        for j in range(outers):
            out_ref[j] = term_s[at ^ k, outer_at ^ j]


def input_kernel(side, pre_ref, grad_ref, edge_ref, kernel_ref, *refs):
    out_hbm, taps_s, out_s, sem = refs[-4:]
    rows, chans, width = pre_ref.shape
    count = rows // 2
    upper = my_core() == side
    start = jnp.where(upper, 0, count)
    put_taps(taps_s, 0, jnp.where(upper, edge_ref[0], grad_ref[count - 1]))
    for r in range(count):
        put_taps(taps_s, r + 1, grad_ref[start + r])
    put_taps(taps_s, count + 1, jnp.where(upper, grad_ref[count], edge_ref[0]))
    step = 2
    copies = []
    for top in range(0, count, step):
        total = jnp.zeros((chans, step * width), F32)
        for a in range(3):
            at = (top + 2 - a) * width
            for b in range(3):
                taps = taps_s[b * chans : (b + 1) * chans, at : at + step * width]
                total += jnp.dot(kernel_ref[a, b], taps, preferred_element_type=F32)
        for r in range(step):
            x = pre_ref[start + top + r].astype(F32)
            sig = 1.0 / (1.0 + jnp.exp(-x))
            deriv = sig * (1.0 + x * (1.0 - sig))
            out_s[top + r] = (total[:, r * width : (r + 1) * width] * deriv).astype(out_s.dtype)
        copies.append(
            pltpu.make_async_copy(
                out_s.at[pl.ds(top, step)], out_hbm.at[pl.ds(start + top, step)], sem.at[top // step]
            )
        )
        copies[-1].start()
    for copy in copies:
        copy.wait()


def pick_kernel(after_ref, out_ref):
    group = out_ref.shape[0] // 9
    k = lax.broadcasted_iota(jnp.int32, (group, 9 * group), 0)
    j = lax.broadcasted_iota(jnp.int32, (group, 9 * group), 1)
    for t in range(9):
        out_ref[t * group : (t + 1) * group, :] = jnp.where(j - 9 * k == t, 1.0, 0.0)


def place_kernel(flip, parts_ref, pick_ref, *refs):
    out_hbm, wide_s, out_s, sem = refs[-4:]
    _, _, block, _ = parts_ref.shape
    half = out_s.shape[0]
    width = pick_ref.shape[0]
    group = width // 9
    for k in range(PLANE):
        lanes = pl.ds(pl.multiple_of((plane_index() ^ k) * LANES, LANES), LANES)
        wide_s[:, :, lanes] = parts_ref[k].astype(F32)
    pick = pick_ref[...].astype(BF16)
    for g in range(block // group):
        rows = [wide_s[t // 3, g * group : (g + 1) * group, t % 3 * half : (t % 3 + 1) * half] for t in range(9)]
        rows = jnp.concatenate(rows, axis=0).astype(BF16)
        out_s[:, g * width : (g + 1) * width] = lax.dot_general(
            rows, pick, (((0,), (0,)), ((), ())), preferred_element_type=F32
        )
    count = sem.shape[0]
    step = half // count
    first = (my_core() ^ flip) * half
    copies = []
    for i in range(count):
        to = pl.ds(pl.multiple_of(first + i * step, 8), step)
        copies.append(pltpu.make_async_copy(out_s.at[pl.ds(i * step, step)], out_hbm.at[to], sem.at[i]))
        copies[-1].start()
    for copy in copies:
        copy.wait()


def shards(pre_act, out_grad, kernel):
    images, rows, width, chans = pre_act.shape
    assert images == 1
    space, blocks = lax.axis_size("space"), lax.axis_size("dp")
    inner = PAIR * PLANE
    outer = space // inner
    block = chans // blocks
    half = chans // PAIR
    group = 16 if block % 16 == 0 else block
    far = blocks // NEAR
    factor = float(images * rows * width * space * blocks) ** (-0.5)
    params = pltpu.CompilerParams(vmem_limit_bytes=VMEM_LIMIT)
    flops = 2 * 9 * chans * chans * rows * width

    pre = jnp.swapaxes(pre_act[0], 1, 2)
    grad = jnp.swapaxes(out_grad[0], 1, 2)
    row = my_core() * (rows - 1)
    edge = jnp.stack([lax.dynamic_index_in_dim(grad, row, 0, False), lax.dynamic_index_in_dim(pre, row, 0, False)])
    beyond = [(i, i + 1 if i % 2 else i - 1) for i in range(space)]
    pairs = [(i, i + 1 - 2 * (i % 2)) for i in range(space)]

    def inside(moves):
        return [(i, j) for i, j in moves if 0 <= j < space]

    near_row = lax.ppermute(edge, "space", inside(beyond))
    _, my_pre, my_grad = lax.optimization_barrier((edge, pre, grad))
    their_grad = lax.ppermute(my_grad, "space", pairs)
    their_pre = lax.ppermute(my_pre, "space", pairs)
    pick = pl.pallas_call(
        pick_kernel,
        out_shape=jax.ShapeDtypeStruct((9 * group, 9 * group), F32),
        in_specs=[anywhere()],
        out_specs=vmem(),
        compiler_params=params,
        cost_estimate=pl.CostEstimate(flops=flops, bytes_accessed=4000000, transcendentals=0),
        name="pick_rows",
    )(edge)
    pick, own_pre, own_grad = lax.optimization_barrier((pick, pre, grad))
    own, act_edge, grad_edge = pl.pallas_call(
        own_kernel,
        out_shape=(
            jax.ShapeDtypeStruct((3, chans, PLANE * LANES), F32),
            jax.ShapeDtypeStruct((2, chans, width), BF16),
            jax.ShapeDtypeStruct((2, half, width), BF16),
        ),
        in_specs=[vmem()] * 2,
        out_specs=(vmem(),) * 3,
        scratch_shapes=[
            pltpu.VMEM((chans, rows * width), BF16),
            pltpu.VMEM((PLANE * LANES, (rows + 2) * width), BF16),
        ],
        compiler_params=params,
        cost_estimate=pl.CostEstimate(flops=flops, bytes_accessed=4000000, transcendentals=rows * width * chans),
        name="own_terms",
    )(own_pre, own_grad)

    def input_part(side, edge_rows, *before):
        count = rows // 2
        return pl.pallas_call(
            functools.partial(input_kernel, side),
            out_shape=jax.ShapeDtypeStruct((rows, chans, width), BF16),
            in_specs=[vmem()] * 4 + [anywhere()] * len(before),
            out_specs=anywhere(),
            scratch_shapes=[
                pltpu.VMEM((3 * chans, (count + 2) * width), BF16),
                pltpu.VMEM((count, chans, width), BF16),
                pltpu.SemaphoreType.DMA((count // 2,)),
            ],
            input_output_aliases={4: 0} if before else {},
            compiler_params=params,
            cost_estimate=pl.CostEstimate(
                flops=flops // 2, bytes_accessed=3000000, transcendentals=rows * width * chans // 2
            ),
            name="input_grad",
        )(pre, grad, edge_rows, kernel, *before)

    piece = jax.ShapeDtypeStruct((far, 3, block, LANES), BF16)
    term = pl.pallas_call(
        pair_kernel,
        out_shape=jax.ShapeDtypeStruct((3, chans, PLANE * LANES), F32),
        in_specs=[vmem()] * 5,
        out_specs=vmem(),
        scratch_shapes=[
            pltpu.VMEM((chans, (rows + 2) * width), BF16),
            pltpu.VMEM((PLANE * LANES, (rows + 4) * width), BF16),
        ],
        compiler_params=params,
        cost_estimate=pl.CostEstimate(flops=flops, bytes_accessed=4000000, transcendentals=rows * width * chans),
        name="pair_terms",
    )(own, act_edge, grad_edge, their_pre, their_grad)
    terms = pl.pallas_call(
        edge_kernel,
        out_shape=(piece,) * (NEAR * PLANE),
        in_specs=[vmem()] * 4,
        out_specs=(vmem(),) * (NEAR * PLANE),
        scratch_shapes=[
            pltpu.VMEM((PLANE * LANES, 2 * width), BF16),
            pltpu.VMEM((NEAR * PLANE, far, 3, block, LANES), BF16),
        ],
        compiler_params=params,
        cost_estimate=pl.CostEstimate(flops=flops // 8, bytes_accessed=4000000, transcendentals=width * chans),
        name="edge_terms",
    )(term, act_edge, grad_edge, near_row)

    got = [terms[0]]
    for k in (3, 4, 7, 5, 6, 2, 1):
        moves = []
        for z in range(blocks):
            for i in range(space):
                to_z, to_i = z ^ (k // PLANE), i ^ (k % PLANE * PAIR)
                moves.append((z * space + i, to_z * space + to_i))
        got.append(lax.ppermute(terms[k], ("dp", "space"), moves))


    in_grad = input_part(0, near_row)
    *got, in_grad = lax.optimization_barrier((*got, in_grad))
    their_edge = lax.dynamic_index_in_dim(their_grad, my_core() * (rows - 1), 0)
    near_sum = sum(part.astype(F32) for part in got)
    others = []
    for k in range(1, far):
        moves = [(z, z ^ (k * NEAR)) for z in range(blocks)]
        others.append(lax.ppermute(near_sum[k].astype(BF16), "dp", moves))
    in_grad = input_part(1, their_edge, in_grad)
    *others, in_grad = lax.optimization_barrier((*others, in_grad))
    total = near_sum[0] + sum(other.astype(F32) for other in others)
    total = total * factor
    if outer > 1:
        total = lax.psum(total, "space", axis_index_groups=[[o * inner + i for o in range(outer)] for i in range(inner)])
    final = total.astype(BF16)
    parts = [final]
    for k in range(1, PLANE):
        parts.append(lax.ppermute(final, "space", [(i, i ^ (k * PAIR)) for i in range(space)]))
    parts = jnp.stack(parts)
    their_parts = lax.ppermute(parts, "space", pairs)

    def place(flip, parts, *before):
        return pl.pallas_call(
            functools.partial(place_kernel, flip),
            out_shape=jax.ShapeDtypeStruct((chans, 9 * block), F32),
            in_specs=[vmem()] * 2 + [anywhere()] * len(before),
            out_specs=anywhere(),
            scratch_shapes=[
                pltpu.VMEM((3, block, PLANE * LANES), F32),
                pltpu.VMEM((half, 9 * block), F32),
                pltpu.SemaphoreType.DMA((4,)),
            ],
            input_output_aliases={2: 0} if before else {},
            compiler_params=params,
            cost_estimate=pl.CostEstimate(flops=81 * block * block * chans, bytes_accessed=1000000, transcendentals=0),
            name="place_rows",
        )(parts, pick, *before)

    placed = place(1, their_parts, place(0, parts))
    return jnp.swapaxes(in_grad, 1, 2)[None], placed.T


def solution(mesh):
    placed = (P("dp", "space", None, None), P("dp", "space", None, None), P())
    return jax.shard_map(
        shards,
        mesh=mesh,
        in_specs=placed,
        out_specs=(P("dp", "space", None, None), P("dp", None)),
        check_vma=False,
    )
```

```python
import functools

import jax
import jax.numpy as jnp
from jax import lax
from jax.experimental import pallas as pl
from jax.experimental.pallas import tpu as pltpu
from jax.sharding import PartitionSpec as P

F32 = jnp.float32
BF16 = jnp.bfloat16
LANES = 128
PAIR = 2
PLANE = 4
NEAR = 2
VMEM_LIMIT = 16 * 1024 * 1024
NT = (((1,), (1,)), ((), ()))


def vmem():
    return pl.BlockSpec(memory_space=pltpu.VMEM)


def anywhere():
    return pl.BlockSpec(memory_space=pl.ANY)


def column_shifts(row):
    wide = row.astype(F32)
    width = wide.shape[1]
    at = lax.broadcasted_iota(jnp.int32, wide.shape, 1)
    ahead = jnp.where(at == width - 1, 0.0, pltpu.roll(wide, width - 1, 1))
    behind = jnp.where(at == 0, 0.0, pltpu.roll(wide, 1, 1))
    return ahead.astype(BF16), row, behind.astype(BF16)


def put_taps(taps_s, slot, row):
    half, width = row.shape
    for b, shifted in enumerate(column_shifts(row)):
        taps_s[b * half : (b + 1) * half, slot * width : (slot + 1) * width] = shifted


def plane_index():
    return lax.rem(lax.axis_index("space") // PAIR, PLANE)


def near_index():
    return lax.rem(lax.axis_index("dp"), NEAR) * PLANE + plane_index()


def silu(v):
    x = v.astype(F32)
    return (x / (1.0 + jnp.exp(-x))).astype(BF16)


def my_core():
    return lax.rem(lax.axis_index("space"), PAIR)


def own_kernel(pre_ref, grad_ref, term_ref, act_edge_ref, grad_edge_ref, act_s, taps_s):
    rows, chans, width = pre_ref.shape
    half = chans // PAIR
    mine = pl.ds(pl.multiple_of(my_core() * half, half), half)
    zero = jnp.zeros((half, width), BF16)
    taps_s[3 * half :, :] = jnp.zeros((taps_s.shape[0] - 3 * half, taps_s.shape[1]), BF16)
    for r in range(rows + 2):
        put_taps(taps_s, r, grad_ref[r - 1, mine, :] if 0 < r <= rows else zero)
    for r in range(rows):
        act_s[:, r * width : (r + 1) * width] = silu(pre_ref[r])
    for i, r in enumerate((0, rows - 1)):
        act_edge_ref[i] = act_s[:, r * width : (r + 1) * width]
        grad_edge_ref[i] = grad_ref[r, mine, :]
    for a in range(3):
        at = (2 - a) * width
        term_ref[a] = lax.dot_general(act_s[...], taps_s[:, at : at + rows * width], NT, preferred_element_type=F32)


def pair_kernel(term_ref, act_edge_ref, grad_edge_ref, their_pre_ref, their_grad_ref, out_ref, act_s, taps_s):
    rows, chans, width = their_pre_ref.shape
    half = chans // PAIR
    core = my_core()
    first = core == 0
    mine = pl.ds(pl.multiple_of(core * half, half), half)
    zero = jnp.zeros((half, width), BF16)
    zero_act = jnp.zeros((chans, width), BF16)
    taps_s[3 * half :, :] = jnp.zeros((taps_s.shape[0] - 3 * half, taps_s.shape[1]), BF16)
    act_s[:, :width] = jnp.where(first, zero_act, act_edge_ref[0])
    for r in range(rows):
        act_s[:, (1 + r) * width : (2 + r) * width] = silu(their_pre_ref[r])
    act_s[:, (rows + 1) * width :] = jnp.where(first, act_edge_ref[1], zero_act)
    put_taps(taps_s, 0, their_grad_ref[rows - 1, mine, :])
    put_taps(taps_s, 1, jnp.where(first, grad_edge_ref[1], zero))
    for r in range(rows):
        put_taps(taps_s, 2 + r, their_grad_ref[r, mine, :])
    put_taps(taps_s, rows + 2, jnp.where(first, zero, grad_edge_ref[0]))
    put_taps(taps_s, rows + 3, their_grad_ref[0, mine, :])
    for a, (left, right, at) in enumerate(((1, rows + 2, 3), (1, rows + 1, 2), (0, rows + 1, 0))):
        out_ref[a] = term_ref[a] + lax.dot_general(
            act_s[:, left * width : right * width],
            taps_s[:, at * width : (at + right - left) * width],
            NT,
            preferred_element_type=F32,
        )


def edge_kernel(term_ref, act_edge_ref, grad_edge_ref, near_ref, *refs):
    out_refs, (taps_s, term_s) = refs[: PLANE * NEAR], refs[PLANE * NEAR :]
    _, chans, width = near_ref.shape
    half = chans // PAIR
    outers, _, block, _ = out_refs[0].shape
    core = my_core()
    first = core == 0
    near_act = silu(near_ref[1])
    near_grad = near_ref[0, pl.ds(pl.multiple_of(core * half, half), half), :]
    taps_s[3 * half :, :] = jnp.zeros((taps_s.shape[0] - 3 * half, taps_s.shape[1]), BF16)
    put_taps(taps_s, 0, jnp.where(first, grad_edge_ref[0], near_grad))
    put_taps(taps_s, 1, jnp.where(first, near_grad, grad_edge_ref[1]))
    acts = {0: jnp.where(first, near_act, act_edge_ref[1]), 2: jnp.where(first, act_edge_ref[0], near_act)}
    for a in range(3):
        term = term_ref[a]
        if a in acts:
            taps = taps_s[:, a // 2 * width : (a // 2 + 1) * width]
            term += lax.dot_general(acts[a], taps, NT, preferred_element_type=F32)
        for p in range(PLANE):
            for z in range(NEAR * outers):
                term_s[z % NEAR * PLANE + p, z // NEAR, a] = term[
                    z * block : (z + 1) * block, p * LANES : (p + 1) * LANES
                ].astype(term_s.dtype)
    at, outer_at = near_index(), lax.axis_index("dp") // NEAR
    for k, out_ref in enumerate(out_refs):
        for j in range(outers):
            out_ref[j] = term_s[at ^ k, outer_at ^ j]


def input_kernel(side, pre_ref, grad_ref, edge_ref, kernel_ref, *refs):
    out_hbm, taps_s, out_s, sem = refs[-4:]
    rows, chans, width = pre_ref.shape
    count = rows // 2
    upper = my_core() == side
    start = jnp.where(upper, 0, count)
    put_taps(taps_s, 0, jnp.where(upper, edge_ref[0], grad_ref[count - 1]))
    for r in range(count):
        put_taps(taps_s, r + 1, grad_ref[start + r])
    put_taps(taps_s, count + 1, jnp.where(upper, grad_ref[count], edge_ref[0]))
    step = 2
    copies = []
    for top in range(0, count, step):
        total = jnp.zeros((chans, step * width), F32)
        for a in range(3):
            at = (top + 2 - a) * width
            for b in range(3):
                taps = taps_s[b * chans : (b + 1) * chans, at : at + step * width]
                total += jnp.dot(kernel_ref[a, b], taps, preferred_element_type=F32)
        for r in range(step):
            x = pre_ref[start + top + r].astype(F32)
            sig = 1.0 / (1.0 + jnp.exp(-x))
            deriv = sig * (1.0 + x * (1.0 - sig))
            out_s[top + r] = (total[:, r * width : (r + 1) * width] * deriv).astype(out_s.dtype)
        copies.append(
            pltpu.make_async_copy(
                out_s.at[pl.ds(top, step)], out_hbm.at[pl.ds(start + top, step)], sem.at[top // step]
            )
        )
        copies[-1].start()
    for copy in copies:
        copy.wait()


def pick_kernel(out_ref):
    size = out_ref.shape[0]
    group = size // 9
    j = lax.broadcasted_iota(jnp.int32, (size, size), 0)
    k = lax.broadcasted_iota(jnp.int32, (size, size), 1)
    pick = jnp.zeros((size, size), F32)
    for t in range(9):
        c = k - t * group
        pick = jnp.where((c >= 0) & (c < group) & (j == 9 * c + t), 1.0, pick)
    out_ref[...] = pick


def place_kernel(flip, parts_ref, pick_ref, *refs):
    out_hbm, wide_s, turned_s, out_s, sem = refs[-5:]
    _, _, block, _ = parts_ref.shape
    half = out_s.shape[0]
    width = pick_ref.shape[0]
    group = width // 9
    for k in range(PLANE):
        lanes = pl.ds(pl.multiple_of((plane_index() ^ k) * LANES, LANES), LANES)
        wide_s[:, :, lanes] = parts_ref[k].astype(F32)
    pick = pick_ref[...].astype(BF16)
    for g in range(block // group):
        rows = [wide_s[t // 3, g * group : (g + 1) * group, t % 3 * half : (t % 3 + 1) * half] for t in range(9)]
        rows = jnp.concatenate(rows, axis=0).astype(BF16)
        turned_s[g * width : (g + 1) * width, :] = jnp.dot(pick, rows, preferred_element_type=F32)
    i = lax.broadcasted_iota(jnp.int32, (half, half), 0)
    j = lax.broadcasted_iota(jnp.int32, (half, half), 1)
    same = jnp.where(i == j, 1.0, 0.0).astype(BF16)
    out_s[...] = lax.dot_general(same, turned_s[...].astype(BF16), NT, preferred_element_type=F32)
    count = sem.shape[0]
    step = half // count
    first = (my_core() ^ flip) * half
    copies = []
    for i in range(count):
        to = pl.ds(pl.multiple_of(first + i * step, 8), step)
        copies.append(pltpu.make_async_copy(out_s.at[pl.ds(i * step, step)], out_hbm.at[to], sem.at[i]))
        copies[-1].start()
    for copy in copies:
        copy.wait()


def shards(pre_act, out_grad, kernel):
    images, rows, width, chans = pre_act.shape
    assert images == 1
    space, blocks = lax.axis_size("space"), lax.axis_size("dp")
    inner = PAIR * PLANE
    outer = space // inner
    block = chans // blocks
    half = chans // PAIR
    group = 16 if block % 16 == 0 else block
    far = blocks // NEAR
    factor = float(images * rows * width * space * blocks) ** (-0.5)
    params = pltpu.CompilerParams(vmem_limit_bytes=VMEM_LIMIT)
    flops = 2 * 9 * chans * chans * rows * width

    pre = jnp.swapaxes(pre_act[0], 1, 2)
    grad = jnp.swapaxes(out_grad[0], 1, 2)
    beyond = [(i, i - PAIR if i % 2 else i + PAIR) for i in range(space)]
    pairs = [(i, i + 1 - 2 * (i % 2)) for i in range(space)]

    def inside(moves):
        return [(i, j) for i, j in moves if 0 <= j < space]

    their_grad = lax.ppermute(grad, "space", pairs)
    their_pre = lax.ppermute(pre, "space", pairs)
    pick = pl.pallas_call(
        pick_kernel,
        out_shape=jax.ShapeDtypeStruct((9 * group, 9 * group), F32),
        out_specs=vmem(),
        compiler_params=params,
        cost_estimate=pl.CostEstimate(flops=flops, bytes_accessed=4000000, transcendentals=0),
        name="pick_rows",
    )()
    pick, own_pre, own_grad = lax.optimization_barrier((pick, pre, grad))
    own, act_edge, grad_edge = pl.pallas_call(
        own_kernel,
        out_shape=(
            jax.ShapeDtypeStruct((3, chans, PLANE * LANES), F32),
            jax.ShapeDtypeStruct((2, chans, width), BF16),
            jax.ShapeDtypeStruct((2, half, width), BF16),
        ),
        in_specs=[vmem()] * 2,
        out_specs=(vmem(),) * 3,
        scratch_shapes=[
            pltpu.VMEM((chans, rows * width), BF16),
            pltpu.VMEM((PLANE * LANES, (rows + 2) * width), BF16),
        ],
        compiler_params=params,
        cost_estimate=pl.CostEstimate(flops=flops, bytes_accessed=4000000, transcendentals=rows * width * chans),
        name="own_terms",
    )(own_pre, own_grad)

    row = (1 - my_core()) * (rows - 1)
    ready = lax.optimization_barrier((own, act_edge, grad_edge, their_grad, their_pre))
    own, act_edge, grad_edge, their_grad, their_pre = ready
    outer_row = jnp.stack([lax.dynamic_index_in_dim(x, row, 0, False) for x in (their_grad, their_pre)])
    near_row = lax.ppermute(outer_row, "space", inside(beyond))

    def input_part(side, edge_rows, *before):
        count = rows // 2
        return pl.pallas_call(
            functools.partial(input_kernel, side),
            out_shape=jax.ShapeDtypeStruct((rows, chans, width), BF16),
            in_specs=[vmem()] * 4 + [anywhere()] * len(before),
            out_specs=anywhere(),
            scratch_shapes=[
                pltpu.VMEM((3 * chans, (count + 2) * width), BF16),
                pltpu.VMEM((count, chans, width), BF16),
                pltpu.SemaphoreType.DMA((count // 2,)),
            ],
            input_output_aliases={4: 0} if before else {},
            compiler_params=params,
            cost_estimate=pl.CostEstimate(
                flops=flops // 2, bytes_accessed=3000000, transcendentals=rows * width * chans // 2
            ),
            name="input_grad",
        )(pre, grad, edge_rows, kernel, *before)

    piece = jax.ShapeDtypeStruct((far, 3, block, LANES), BF16)
    term = pl.pallas_call(
        pair_kernel,
        out_shape=jax.ShapeDtypeStruct((3, chans, PLANE * LANES), F32),
        in_specs=[vmem()] * 5,
        out_specs=vmem(),
        scratch_shapes=[
            pltpu.VMEM((chans, (rows + 2) * width), BF16),
            pltpu.VMEM((PLANE * LANES, (rows + 4) * width), BF16),
        ],
        compiler_params=params,
        cost_estimate=pl.CostEstimate(flops=flops, bytes_accessed=4000000, transcendentals=rows * width * chans),
        name="pair_terms",
    )(own, act_edge, grad_edge, their_pre, their_grad)
    terms = pl.pallas_call(
        edge_kernel,
        out_shape=(piece,) * (NEAR * PLANE),
        in_specs=[vmem()] * 4,
        out_specs=(vmem(),) * (NEAR * PLANE),
        scratch_shapes=[
            pltpu.VMEM((PLANE * LANES, 2 * width), BF16),
            pltpu.VMEM((NEAR * PLANE, far, 3, block, LANES), BF16),
        ],
        compiler_params=params,
        cost_estimate=pl.CostEstimate(flops=flops // 8, bytes_accessed=4000000, transcendentals=width * chans),
        name="edge_terms",
    )(term, act_edge, grad_edge, near_row)

    got = [terms[0]]
    for k in (3, 4, 7, 5, 6, 2, 1):
        moves = []
        for z in range(blocks):
            for i in range(space):
                to_z, to_i = z ^ (k // PLANE), i ^ (k % PLANE * PAIR)
                moves.append((z * space + i, to_z * space + to_i))
        got.append(lax.ppermute(terms[k], ("dp", "space"), moves))


    in_grad = input_part(0, near_row)
    *got, in_grad = lax.optimization_barrier((*got, in_grad))
    their_edge = lax.dynamic_index_in_dim(their_grad, my_core() * (rows - 1), 0)
    near_sum = sum(part.astype(F32) for part in got)
    others = []
    for k in range(1, far):
        moves = [(z, z ^ (k * NEAR)) for z in range(blocks)]
        others.append(lax.ppermute(near_sum[k].astype(BF16), "dp", moves))
    in_grad = input_part(1, their_edge, in_grad)
    *others, in_grad = lax.optimization_barrier((*others, in_grad))
    total = near_sum[0] + sum(other.astype(F32) for other in others)
    total = total * factor
    if outer > 1:
        total = lax.psum(total, "space", axis_index_groups=[[o * inner + i for o in range(outer)] for i in range(inner)])
    final = total.astype(BF16)
    parts = [final]
    for k in range(1, PLANE):
        parts.append(lax.ppermute(final, "space", [(i, i ^ (k * PAIR)) for i in range(space)]))
    parts = jnp.stack(parts)
    their_parts = lax.ppermute(parts, "space", pairs)

    def place(flip, parts, *before):
        return pl.pallas_call(
            functools.partial(place_kernel, flip),
            out_shape=jax.ShapeDtypeStruct((chans, 9 * block), F32),
            in_specs=[vmem()] * 2 + [anywhere()] * len(before),
            out_specs=anywhere(),
            scratch_shapes=[
                pltpu.VMEM((3, block, PLANE * LANES), F32),
                pltpu.VMEM((9 * block, half), F32),
                pltpu.VMEM((half, 9 * block), F32),
                pltpu.SemaphoreType.DMA((10,)),
            ],
            input_output_aliases={2: 0} if before else {},
            compiler_params=params,
            cost_estimate=pl.CostEstimate(flops=81 * block * block * chans, bytes_accessed=1000000, transcendentals=0),
            name="place_rows",
        )(parts, pick, *before)

    placed = place(1, their_parts, place(0, parts))
    return jnp.swapaxes(in_grad, 1, 2)[None], placed.T


def solution(mesh):
    placed = (P("dp", "space", None, None), P("dp", "space", None, None), P())
    return jax.shard_map(
        shards,
        mesh=mesh,
        in_specs=placed,
        out_specs=(P("dp", "space", None, None), P("dp", None)),
        check_vma=False,
    )
```

```python
import functools

import jax
import jax.numpy as jnp
from jax import lax
from jax.experimental import pallas as pl
from jax.experimental.pallas import tpu as pltpu
from jax.sharding import PartitionSpec as P

F32 = jnp.float32
BF16 = jnp.bfloat16
LANES = 128
PAIR = 2
PLANE = 4
NEAR = 2
VMEM_LIMIT = 16 * 1024 * 1024
NT = (((1,), (1,)), ((), ()))


def vmem():
    return pl.BlockSpec(memory_space=pltpu.VMEM)


def anywhere():
    return pl.BlockSpec(memory_space=pl.ANY)


def column_shifts(row):
    wide = row.astype(F32)
    width = wide.shape[1]
    at = lax.broadcasted_iota(jnp.int32, wide.shape, 1)
    ahead = jnp.where(at == width - 1, 0.0, pltpu.roll(wide, width - 1, 1))
    behind = jnp.where(at == 0, 0.0, pltpu.roll(wide, 1, 1))
    return ahead.astype(BF16), row, behind.astype(BF16)


def put_taps(taps_s, slot, row):
    half, width = row.shape
    for b, shifted in enumerate(column_shifts(row)):
        taps_s[b * half : (b + 1) * half, slot * width : (slot + 1) * width] = shifted


def plane_index():
    return lax.rem(lax.axis_index("space") // PAIR, PLANE)


def near_index():
    return lax.rem(lax.axis_index("dp"), NEAR) * PLANE + plane_index()


def silu(v):
    x = v.astype(F32)
    return (x / (1.0 + jnp.exp(-x))).astype(BF16)


def my_core():
    return lax.rem(lax.axis_index("space"), PAIR)


def own_kernel(pre_ref, grad_ref, term_ref, act_edge_ref, grad_edge_ref, act_s, taps_s):
    rows, chans, width = pre_ref.shape
    half = chans // PAIR
    mine = pl.ds(pl.multiple_of(my_core() * half, half), half)
    zero = jnp.zeros((half, width), BF16)
    taps_s[3 * half :, :] = jnp.zeros((taps_s.shape[0] - 3 * half, taps_s.shape[1]), BF16)
    for r in range(rows + 2):
        put_taps(taps_s, r, grad_ref[r - 1, mine, :] if 0 < r <= rows else zero)
    for r in range(rows):
        act_s[:, r * width : (r + 1) * width] = silu(pre_ref[r])
    for i, r in enumerate((0, rows - 1)):
        act_edge_ref[i] = act_s[:, r * width : (r + 1) * width]
        grad_edge_ref[i] = grad_ref[r, mine, :]
    for a in range(3):
        at = (2 - a) * width
        term_ref[a] = lax.dot_general(act_s[...], taps_s[:, at : at + rows * width], NT, preferred_element_type=F32)


def pair_kernel(term_ref, act_edge_ref, grad_edge_ref, their_pre_ref, their_grad_ref, out_ref, act_s, taps_s):
    rows, chans, width = their_pre_ref.shape
    half = chans // PAIR
    core = my_core()
    first = core == 0
    mine = pl.ds(pl.multiple_of(core * half, half), half)
    zero = jnp.zeros((half, width), BF16)
    zero_act = jnp.zeros((chans, width), BF16)
    taps_s[3 * half :, :] = jnp.zeros((taps_s.shape[0] - 3 * half, taps_s.shape[1]), BF16)
    act_s[:, :width] = jnp.where(first, zero_act, act_edge_ref[0])
    for r in range(rows):
        act_s[:, (1 + r) * width : (2 + r) * width] = silu(their_pre_ref[r])
    act_s[:, (rows + 1) * width :] = jnp.where(first, act_edge_ref[1], zero_act)
    put_taps(taps_s, 0, their_grad_ref[rows - 1, mine, :])
    put_taps(taps_s, 1, jnp.where(first, grad_edge_ref[1], zero))
    for r in range(rows):
        put_taps(taps_s, 2 + r, their_grad_ref[r, mine, :])
    put_taps(taps_s, rows + 2, jnp.where(first, zero, grad_edge_ref[0]))
    put_taps(taps_s, rows + 3, their_grad_ref[0, mine, :])
    for a, (left, right, at) in enumerate(((1, rows + 2, 3), (1, rows + 1, 2), (0, rows + 1, 0))):
        out_ref[a] = term_ref[a] + lax.dot_general(
            act_s[:, left * width : right * width],
            taps_s[:, at * width : (at + right - left) * width],
            NT,
            preferred_element_type=F32,
        )


def edge_kernel(term_ref, act_edge_ref, grad_edge_ref, near_ref, *refs):
    out_refs, (taps_s, term_s) = refs[: PLANE * NEAR], refs[PLANE * NEAR :]
    _, chans, width = near_ref.shape
    half = chans // PAIR
    outers, _, block, _ = out_refs[0].shape
    core = my_core()
    first = core == 0
    near_act = silu(near_ref[1])
    near_grad = near_ref[0, pl.ds(pl.multiple_of(core * half, half), half), :]
    taps_s[3 * half :, :] = jnp.zeros((taps_s.shape[0] - 3 * half, taps_s.shape[1]), BF16)
    put_taps(taps_s, 0, jnp.where(first, grad_edge_ref[0], near_grad))
    put_taps(taps_s, 1, jnp.where(first, near_grad, grad_edge_ref[1]))
    acts = {0: jnp.where(first, near_act, act_edge_ref[1]), 2: jnp.where(first, act_edge_ref[0], near_act)}
    for a in range(3):
        term = term_ref[a]
        if a in acts:
            taps = taps_s[:, a // 2 * width : (a // 2 + 1) * width]
            term += lax.dot_general(acts[a], taps, NT, preferred_element_type=F32)
        for p in range(PLANE):
            for z in range(NEAR * outers):
                term_s[z % NEAR * PLANE + p, z // NEAR, a] = term[
                    z * block : (z + 1) * block, p * LANES : (p + 1) * LANES
                ].astype(term_s.dtype)
    at, outer_at = near_index(), lax.axis_index("dp") // NEAR
    for k, out_ref in enumerate(out_refs):
        for j in range(outers):
            out_ref[j] = term_s[at ^ k, outer_at ^ j]


def input_kernel(side, pre_ref, grad_ref, edge_ref, kernel_ref, *refs):
    out_hbm, taps_s, out_s, sem = refs[-4:]
    rows, chans, width = pre_ref.shape
    count = rows // 2
    upper = my_core() == side
    start = jnp.where(upper, 0, count)
    put_taps(taps_s, 0, jnp.where(upper, edge_ref[0], grad_ref[count - 1]))
    for r in range(count):
        put_taps(taps_s, r + 1, grad_ref[start + r])
    put_taps(taps_s, count + 1, jnp.where(upper, grad_ref[count], edge_ref[0]))
    step = 2
    copies = []
    for top in range(0, count, step):
        total = jnp.zeros((chans, step * width), F32)
        for a in range(3):
            at = (top + 2 - a) * width
            for b in range(3):
                taps = taps_s[b * chans : (b + 1) * chans, at : at + step * width]
                total += jnp.dot(kernel_ref[a, b], taps, preferred_element_type=F32)
        for r in range(step):
            x = pre_ref[start + top + r].astype(F32)
            sig = 1.0 / (1.0 + jnp.exp(-x))
            deriv = sig * (1.0 + x * (1.0 - sig))
            out_s[top + r] = (total[:, r * width : (r + 1) * width] * deriv).astype(out_s.dtype)
        copies.append(
            pltpu.make_async_copy(
                out_s.at[pl.ds(top, step)], out_hbm.at[pl.ds(start + top, step)], sem.at[top // step]
            )
        )
        copies[-1].start()
    for copy in copies:
        copy.wait()


def pick_kernel(after_ref, out_ref):
    size = out_ref.shape[0]
    group = size // 9
    j = lax.broadcasted_iota(jnp.int32, (size, size), 0)
    k = lax.broadcasted_iota(jnp.int32, (size, size), 1)
    pick = jnp.zeros((size, size), F32)
    for t in range(9):
        c = k - t * group
        pick = jnp.where((c >= 0) & (c < group) & (j == 9 * c + t), 1.0, pick)
    out_ref[...] = pick


def place_kernel(flip, parts_ref, pick_ref, *refs):
    out_hbm, wide_s, turned_s, out_s, sem = refs[-5:]
    _, _, block, _ = parts_ref.shape
    half = out_s.shape[0]
    width = pick_ref.shape[0]
    group = width // 9
    for k in range(PLANE):
        lanes = pl.ds(pl.multiple_of((plane_index() ^ k) * LANES, LANES), LANES)
        wide_s[:, :, lanes] = parts_ref[k].astype(F32)
    pick = pick_ref[...].astype(BF16)
    for g in range(block // group):
        rows = [wide_s[t // 3, g * group : (g + 1) * group, t % 3 * half : (t % 3 + 1) * half] for t in range(9)]
        rows = jnp.concatenate(rows, axis=0).astype(BF16)
        turned_s[g * width : (g + 1) * width, :] = jnp.dot(pick, rows, preferred_element_type=F32)
    i = lax.broadcasted_iota(jnp.int32, (half, half), 0)
    j = lax.broadcasted_iota(jnp.int32, (half, half), 1)
    same = jnp.where(i == j, 1.0, 0.0).astype(BF16)
    out_s[...] = lax.dot_general(same, turned_s[...].astype(BF16), NT, preferred_element_type=F32)
    count = sem.shape[0]
    step = half // count
    first = (my_core() ^ flip) * half
    copies = []
    for i in range(count):
        to = pl.ds(pl.multiple_of(first + i * step, 8), step)
        copies.append(pltpu.make_async_copy(out_s.at[pl.ds(i * step, step)], out_hbm.at[to], sem.at[i]))
        copies[-1].start()
    for copy in copies:
        copy.wait()


def shards(pre_act, out_grad, kernel):
    images, rows, width, chans = pre_act.shape
    assert images == 1
    space, blocks = lax.axis_size("space"), lax.axis_size("dp")
    inner = PAIR * PLANE
    outer = space // inner
    block = chans // blocks
    half = chans // PAIR
    group = 16 if block % 16 == 0 else block
    far = blocks // NEAR
    factor = float(images * rows * width * space * blocks) ** (-0.5)
    params = pltpu.CompilerParams(vmem_limit_bytes=VMEM_LIMIT)
    flops = 2 * 9 * chans * chans * rows * width

    pre = jnp.swapaxes(pre_act[0], 1, 2)
    grad = jnp.swapaxes(out_grad[0], 1, 2)
    row = my_core() * (rows - 1)
    edge = jnp.stack([lax.dynamic_index_in_dim(grad, row, 0, False), lax.dynamic_index_in_dim(pre, row, 0, False)])
    beyond = [(i, i + 1 if i % 2 else i - 1) for i in range(space)]
    pairs = [(i, i + 1 - 2 * (i % 2)) for i in range(space)]

    def inside(moves):
        return [(i, j) for i, j in moves if 0 <= j < space]

    near_row = lax.ppermute(edge, "space", inside(beyond))
    _, my_pre, my_grad = lax.optimization_barrier((edge, pre, grad))
    their_grad = lax.ppermute(my_grad, "space", pairs)
    their_pre = lax.ppermute(my_pre, "space", pairs)
    pick = pl.pallas_call(
        pick_kernel,
        out_shape=jax.ShapeDtypeStruct((9 * group, 9 * group), F32),
        in_specs=[anywhere()],
        out_specs=vmem(),
        compiler_params=params,
        cost_estimate=pl.CostEstimate(flops=flops, bytes_accessed=4000000, transcendentals=0),
        name="pick_rows",
    )(edge)
    pick, own_pre, own_grad = lax.optimization_barrier((pick, pre, grad))
    own, act_edge, grad_edge = pl.pallas_call(
        own_kernel,
        out_shape=(
            jax.ShapeDtypeStruct((3, chans, PLANE * LANES), F32),
            jax.ShapeDtypeStruct((2, chans, width), BF16),
            jax.ShapeDtypeStruct((2, half, width), BF16),
        ),
        in_specs=[vmem()] * 2,
        out_specs=(vmem(),) * 3,
        scratch_shapes=[
            pltpu.VMEM((chans, rows * width), BF16),
            pltpu.VMEM((PLANE * LANES, (rows + 2) * width), BF16),
        ],
        compiler_params=params,
        cost_estimate=pl.CostEstimate(flops=flops, bytes_accessed=4000000, transcendentals=rows * width * chans),
        name="own_terms",
    )(own_pre, own_grad)

    def input_part(side, edge_rows, *before):
        count = rows // 2
        return pl.pallas_call(
            functools.partial(input_kernel, side),
            out_shape=jax.ShapeDtypeStruct((rows, chans, width), BF16),
            in_specs=[vmem()] * 4 + [anywhere()] * len(before),
            out_specs=anywhere(),
            scratch_shapes=[
                pltpu.VMEM((3 * chans, (count + 2) * width), BF16),
                pltpu.VMEM((count, chans, width), BF16),
                pltpu.SemaphoreType.DMA((count // 2,)),
            ],
            input_output_aliases={4: 0} if before else {},
            compiler_params=params,
            cost_estimate=pl.CostEstimate(
                flops=flops // 2, bytes_accessed=3000000, transcendentals=rows * width * chans // 2
            ),
            name="input_grad",
        )(pre, grad, edge_rows, kernel, *before)

    piece = jax.ShapeDtypeStruct((far, 3, block, LANES), BF16)
    term = pl.pallas_call(
        pair_kernel,
        out_shape=jax.ShapeDtypeStruct((3, chans, PLANE * LANES), F32),
        in_specs=[vmem()] * 5,
        out_specs=vmem(),
        scratch_shapes=[
            pltpu.VMEM((chans, (rows + 2) * width), BF16),
            pltpu.VMEM((PLANE * LANES, (rows + 4) * width), BF16),
        ],
        compiler_params=params,
        cost_estimate=pl.CostEstimate(flops=flops, bytes_accessed=4000000, transcendentals=rows * width * chans),
        name="pair_terms",
    )(own, act_edge, grad_edge, their_pre, their_grad)
    terms = pl.pallas_call(
        edge_kernel,
        out_shape=(piece,) * (NEAR * PLANE),
        in_specs=[vmem()] * 4,
        out_specs=(vmem(),) * (NEAR * PLANE),
        scratch_shapes=[
            pltpu.VMEM((PLANE * LANES, 2 * width), BF16),
            pltpu.VMEM((NEAR * PLANE, far, 3, block, LANES), BF16),
        ],
        compiler_params=params,
        cost_estimate=pl.CostEstimate(flops=flops // 8, bytes_accessed=4000000, transcendentals=width * chans),
        name="edge_terms",
    )(term, act_edge, grad_edge, near_row)

    got = [terms[0]]
    for k in (4, 6, 1, 7, 5, 3, 2):
        moves = []
        for z in range(blocks):
            for i in range(space):
                to_z, to_i = z ^ (k // PLANE), i ^ (k % PLANE * PAIR)
                moves.append((z * space + i, to_z * space + to_i))
        got.append(lax.ppermute(terms[k], ("dp", "space"), moves))


    their_edge = lax.dynamic_index_in_dim(their_grad, my_core() * (rows - 1), 0)
    got[1], got[2], near_row, their_edge = lax.optimization_barrier((got[1], got[2], near_row, their_edge))
    in_grad = input_part(1, their_edge, input_part(0, near_row))
    *got, in_grad = lax.optimization_barrier((*got, in_grad))
    near_sum = sum(part.astype(F32) for part in got)
    others = []
    for k in range(1, far):
        moves = [(z, z ^ (k * NEAR)) for z in range(blocks)]
        others.append(lax.ppermute(near_sum[k].astype(BF16), "dp", moves))
    total = near_sum[0] + sum(other.astype(F32) for other in others)
    total = total * factor
    if outer > 1:
        total = lax.psum(total, "space", axis_index_groups=[[o * inner + i for o in range(outer)] for i in range(inner)])
    final = total.astype(BF16)
    parts = [final]
    for k in range(1, PLANE):
        parts.append(lax.ppermute(final, "space", [(i, i ^ (k * PAIR)) for i in range(space)]))
    parts = jnp.stack(parts)
    their_parts = lax.ppermute(parts, "space", pairs)

    def place(flip, parts, *before):
        return pl.pallas_call(
            functools.partial(place_kernel, flip),
            out_shape=jax.ShapeDtypeStruct((chans, 9 * block), F32),
            in_specs=[vmem()] * 2 + [anywhere()] * len(before),
            out_specs=anywhere(),
            scratch_shapes=[
                pltpu.VMEM((3, block, PLANE * LANES), F32),
                pltpu.VMEM((9 * block, half), F32),
                pltpu.VMEM((half, 9 * block), F32),
                pltpu.SemaphoreType.DMA((10,)),
            ],
            input_output_aliases={2: 0} if before else {},
            compiler_params=params,
            cost_estimate=pl.CostEstimate(flops=81 * block * block * chans, bytes_accessed=1000000, transcendentals=0),
            name="place_rows",
        )(parts, pick, *before)

    placed = place(1, their_parts, place(0, parts))
    return jnp.swapaxes(in_grad, 1, 2)[None], placed.T


def solution(mesh):
    placed = (P("dp", "space", None, None), P("dp", "space", None, None), P())
    return jax.shard_map(
        shards,
        mesh=mesh,
        in_specs=placed,
        out_specs=(P("dp", "space", None, None), P("dp", None)),
        check_vma=False,
    )
```

```python
import functools

import jax
import jax.numpy as jnp
from jax import lax
from jax.experimental import pallas as pl
from jax.experimental.pallas import tpu as pltpu
from jax.sharding import PartitionSpec as P

F32 = jnp.float32
BF16 = jnp.bfloat16
LANES = 128
PAIR = 2
PLANE = 4
NEAR = 2
VMEM_LIMIT = 16 * 1024 * 1024
NT = (((1,), (1,)), ((), ()))


def vmem():
    return pl.BlockSpec(memory_space=pltpu.VMEM)


def anywhere():
    return pl.BlockSpec(memory_space=pl.ANY)


def column_shifts(row):
    wide = row.astype(F32)
    width = wide.shape[1]
    at = lax.broadcasted_iota(jnp.int32, wide.shape, 1)
    ahead = jnp.where(at == width - 1, 0.0, pltpu.roll(wide, width - 1, 1))
    behind = jnp.where(at == 0, 0.0, pltpu.roll(wide, 1, 1))
    return ahead.astype(BF16), row, behind.astype(BF16)


def put_taps(taps_s, slot, row):
    half, width = row.shape
    for b, shifted in enumerate(column_shifts(row)):
        taps_s[b * half : (b + 1) * half, slot * width : (slot + 1) * width] = shifted


def plane_index():
    return lax.rem(lax.axis_index("space") // PAIR, PLANE)


def near_index():
    return lax.rem(lax.axis_index("dp"), NEAR) * PLANE + plane_index()


def silu(v):
    x = v.astype(F32)
    return (x / (1.0 + jnp.exp(-x))).astype(BF16)


def my_core():
    return lax.rem(lax.axis_index("space"), PAIR)


def own_kernel(pre_ref, grad_ref, term_ref, act_edge_ref, grad_edge_ref, act_s, taps_s):
    rows, chans, width = pre_ref.shape
    half = chans // PAIR
    mine = pl.ds(pl.multiple_of(my_core() * half, half), half)
    zero = jnp.zeros((half, width), BF16)
    taps_s[3 * half :, :] = jnp.zeros((taps_s.shape[0] - 3 * half, taps_s.shape[1]), BF16)
    for r in range(rows + 2):
        put_taps(taps_s, r, grad_ref[r - 1, mine, :] if 0 < r <= rows else zero)
    for r in range(rows):
        act_s[:, r * width : (r + 1) * width] = silu(pre_ref[r])
    for i, r in enumerate((0, rows - 1)):
        act_edge_ref[i] = act_s[:, r * width : (r + 1) * width]
        grad_edge_ref[i] = grad_ref[r, mine, :]
    for a in range(3):
        at = (2 - a) * width
        term_ref[a] = lax.dot_general(act_s[...], taps_s[:, at : at + rows * width], NT, preferred_element_type=F32)


def pair_kernel(term_ref, act_edge_ref, grad_edge_ref, their_pre_ref, their_grad_ref, out_ref, act_s, taps_s):
    rows, chans, width = their_pre_ref.shape
    half = chans // PAIR
    core = my_core()
    first = core == 0
    mine = pl.ds(pl.multiple_of(core * half, half), half)
    zero = jnp.zeros((half, width), BF16)
    zero_act = jnp.zeros((chans, width), BF16)
    taps_s[3 * half :, :] = jnp.zeros((taps_s.shape[0] - 3 * half, taps_s.shape[1]), BF16)
    act_s[:, :width] = jnp.where(first, zero_act, act_edge_ref[0])
    for r in range(rows):
        act_s[:, (1 + r) * width : (2 + r) * width] = silu(their_pre_ref[r])
    act_s[:, (rows + 1) * width :] = jnp.where(first, act_edge_ref[1], zero_act)
    put_taps(taps_s, 0, their_grad_ref[rows - 1, mine, :])
    put_taps(taps_s, 1, jnp.where(first, grad_edge_ref[1], zero))
    for r in range(rows):
        put_taps(taps_s, 2 + r, their_grad_ref[r, mine, :])
    put_taps(taps_s, rows + 2, jnp.where(first, zero, grad_edge_ref[0]))
    put_taps(taps_s, rows + 3, their_grad_ref[0, mine, :])
    for a, (left, right, at) in enumerate(((1, rows + 2, 3), (1, rows + 1, 2), (0, rows + 1, 0))):
        out_ref[a] = term_ref[a] + lax.dot_general(
            act_s[:, left * width : right * width],
            taps_s[:, at * width : (at + right - left) * width],
            NT,
            preferred_element_type=F32,
        )


def sends(outers):
    whole, split = (4, 6, 1), (7, 5, 3, 2)
    return (
        [(k, 0, outers) for k in whole] + [(k, 1, outers) for k in split] + [(k, 0, 1) for k in split]
    )


def edge_kernel(term_ref, act_edge_ref, grad_edge_ref, near_ref, *refs):
    out_refs, (own_ref, taps_s, term_s) = refs[:-3], refs[-3:]
    _, chans, width = near_ref.shape
    half = chans // PAIR
    outers, _, block, _ = own_ref.shape
    core = my_core()
    first = core == 0
    near_act = silu(near_ref[1])
    near_grad = near_ref[0, pl.ds(pl.multiple_of(core * half, half), half), :]
    taps_s[3 * half :, :] = jnp.zeros((taps_s.shape[0] - 3 * half, taps_s.shape[1]), BF16)
    put_taps(taps_s, 0, jnp.where(first, grad_edge_ref[0], near_grad))
    put_taps(taps_s, 1, jnp.where(first, near_grad, grad_edge_ref[1]))
    acts = {0: jnp.where(first, near_act, act_edge_ref[1]), 2: jnp.where(first, act_edge_ref[0], near_act)}
    for a in range(3):
        term = term_ref[a]
        if a in acts:
            taps = taps_s[:, a // 2 * width : (a // 2 + 1) * width]
            term += lax.dot_general(acts[a], taps, NT, preferred_element_type=F32)
        for p in range(PLANE):
            for z in range(NEAR * outers):
                term_s[z % NEAR * PLANE + p, z // NEAR, a] = term[z * block : (z + 1) * block, p * LANES : (p + 1) * LANES]
    at, outer_at = near_index(), lax.axis_index("dp") // NEAR
    for j in range(outers):
        own_ref[j] = term_s[at, outer_at ^ j]
    for (k, first_j, last_j), out_ref in zip(sends(outers), out_refs):
        for j in range(first_j, last_j):
            out_ref[j - first_j] = term_s[at ^ k, outer_at ^ j].astype(out_ref.dtype)


def input_kernel(side, pre_ref, grad_ref, edge_ref, kernel_ref, *refs):
    out_hbm, taps_s, out_s, sem = refs[-4:]
    rows, chans, width = pre_ref.shape
    count = rows // 2
    upper = my_core() == side
    start = jnp.where(upper, 0, count)
    put_taps(taps_s, 0, jnp.where(upper, edge_ref[0], grad_ref[count - 1]))
    for r in range(count):
        put_taps(taps_s, r + 1, grad_ref[start + r])
    put_taps(taps_s, count + 1, jnp.where(upper, grad_ref[count], edge_ref[0]))
    step = 2
    copies = []
    for top in range(0, count, step):
        total = jnp.zeros((chans, step * width), F32)
        for a in range(3):
            at = (top + 2 - a) * width
            for b in range(3):
                taps = taps_s[b * chans : (b + 1) * chans, at : at + step * width]
                total += jnp.dot(kernel_ref[a, b], taps, preferred_element_type=F32)
        for r in range(step):
            x = pre_ref[start + top + r].astype(F32)
            sig = 1.0 / (1.0 + jnp.exp(-x))
            deriv = sig * (1.0 + x * (1.0 - sig))
            out_s[top + r] = (total[:, r * width : (r + 1) * width] * deriv).astype(out_s.dtype)
        copies.append(
            pltpu.make_async_copy(
                out_s.at[pl.ds(top, step)], out_hbm.at[pl.ds(start + top, step)], sem.at[top // step]
            )
        )
        copies[-1].start()
    for copy in copies:
        copy.wait()


def pick_kernel(after_ref, out_ref):
    size = out_ref.shape[0]
    group = size // 9
    j = lax.broadcasted_iota(jnp.int32, (size, size), 0)
    k = lax.broadcasted_iota(jnp.int32, (size, size), 1)
    pick = jnp.zeros((size, size), F32)
    for t in range(9):
        c = k - t * group
        pick = jnp.where((c >= 0) & (c < group) & (j == 9 * c + t), 1.0, pick)
    out_ref[...] = pick


def place_kernel(flip, parts_ref, pick_ref, *refs):
    out_hbm, wide_s, turned_s, out_s, sem = refs[-5:]
    _, _, block, _ = parts_ref.shape
    half = out_s.shape[0]
    width = pick_ref.shape[0]
    group = width // 9
    for k in range(PLANE):
        lanes = pl.ds(pl.multiple_of((plane_index() ^ k) * LANES, LANES), LANES)
        wide_s[:, :, lanes] = parts_ref[k].astype(F32)
    pick = pick_ref[...].astype(BF16)
    for g in range(block // group):
        rows = [wide_s[t // 3, g * group : (g + 1) * group, t % 3 * half : (t % 3 + 1) * half] for t in range(9)]
        rows = jnp.concatenate(rows, axis=0).astype(BF16)
        turned_s[g * width : (g + 1) * width, :] = jnp.dot(pick, rows, preferred_element_type=F32)
    i = lax.broadcasted_iota(jnp.int32, (half, half), 0)
    j = lax.broadcasted_iota(jnp.int32, (half, half), 1)
    same = jnp.where(i == j, 1.0, 0.0).astype(BF16)
    out_s[...] = lax.dot_general(same, turned_s[...].astype(BF16), NT, preferred_element_type=F32)
    count = sem.shape[0]
    step = half // count
    first = (my_core() ^ flip) * half
    copies = []
    for i in range(count):
        to = pl.ds(pl.multiple_of(first + i * step, 8), step)
        copies.append(pltpu.make_async_copy(out_s.at[pl.ds(i * step, step)], out_hbm.at[to], sem.at[i]))
        copies[-1].start()
    for copy in copies:
        copy.wait()


def shards(pre_act, out_grad, kernel):
    images, rows, width, chans = pre_act.shape
    assert images == 1
    space, blocks = lax.axis_size("space"), lax.axis_size("dp")
    inner = PAIR * PLANE
    outer = space // inner
    block = chans // blocks
    half = chans // PAIR
    group = 16 if block % 16 == 0 else block
    far = blocks // NEAR
    factor = float(images * rows * width * space * blocks) ** (-0.5)
    params = pltpu.CompilerParams(vmem_limit_bytes=VMEM_LIMIT)
    flops = 2 * 9 * chans * chans * rows * width

    pre = jnp.swapaxes(pre_act[0], 1, 2)
    grad = jnp.swapaxes(out_grad[0], 1, 2)
    row = my_core() * (rows - 1)
    edge = jnp.stack([lax.dynamic_index_in_dim(grad, row, 0, False), lax.dynamic_index_in_dim(pre, row, 0, False)])
    beyond = [(i, i + 1 if i % 2 else i - 1) for i in range(space)]
    pairs = [(i, i + 1 - 2 * (i % 2)) for i in range(space)]

    def inside(moves):
        return [(i, j) for i, j in moves if 0 <= j < space]

    near_row = lax.ppermute(edge, "space", inside(beyond))
    _, my_pre, my_grad = lax.optimization_barrier((edge, pre, grad))
    their_grad = lax.ppermute(my_grad, "space", pairs)
    their_pre = lax.ppermute(my_pre, "space", pairs)
    pick = pl.pallas_call(
        pick_kernel,
        out_shape=jax.ShapeDtypeStruct((9 * group, 9 * group), F32),
        in_specs=[anywhere()],
        out_specs=vmem(),
        compiler_params=params,
        cost_estimate=pl.CostEstimate(flops=flops, bytes_accessed=4000000, transcendentals=0),
        name="pick_rows",
    )(edge)
    pick, own_pre, own_grad = lax.optimization_barrier((pick, pre, grad))
    own, act_edge, grad_edge = pl.pallas_call(
        own_kernel,
        out_shape=(
            jax.ShapeDtypeStruct((3, chans, PLANE * LANES), F32),
            jax.ShapeDtypeStruct((2, chans, width), BF16),
            jax.ShapeDtypeStruct((2, half, width), BF16),
        ),
        in_specs=[vmem()] * 2,
        out_specs=(vmem(),) * 3,
        scratch_shapes=[
            pltpu.VMEM((chans, rows * width), BF16),
            pltpu.VMEM((PLANE * LANES, (rows + 2) * width), BF16),
        ],
        compiler_params=params,
        cost_estimate=pl.CostEstimate(flops=flops, bytes_accessed=4000000, transcendentals=rows * width * chans),
        name="own_terms",
    )(own_pre, own_grad)

    def input_part(side, edge_rows, *before):
        count = rows // 2
        return pl.pallas_call(
            functools.partial(input_kernel, side),
            out_shape=jax.ShapeDtypeStruct((rows, chans, width), BF16),
            in_specs=[vmem()] * 4 + [anywhere()] * len(before),
            out_specs=anywhere(),
            scratch_shapes=[
                pltpu.VMEM((3 * chans, (count + 2) * width), BF16),
                pltpu.VMEM((count, chans, width), BF16),
                pltpu.SemaphoreType.DMA((count // 2,)),
            ],
            input_output_aliases={4: 0} if before else {},
            compiler_params=params,
            cost_estimate=pl.CostEstimate(
                flops=flops // 2, bytes_accessed=3000000, transcendentals=rows * width * chans // 2
            ),
            name="input_grad",
        )(pre, grad, edge_rows, kernel, *before)

    order = sends(far)
    pieces = [jax.ShapeDtypeStruct((last_j - first_j, 3, block, LANES), BF16) for _, first_j, last_j in order]
    pieces.append(jax.ShapeDtypeStruct((far, 3, block, LANES), F32))
    term = pl.pallas_call(
        pair_kernel,
        out_shape=jax.ShapeDtypeStruct((3, chans, PLANE * LANES), F32),
        in_specs=[vmem()] * 5,
        out_specs=vmem(),
        scratch_shapes=[
            pltpu.VMEM((chans, (rows + 2) * width), BF16),
            pltpu.VMEM((PLANE * LANES, (rows + 4) * width), BF16),
        ],
        compiler_params=params,
        cost_estimate=pl.CostEstimate(flops=flops, bytes_accessed=4000000, transcendentals=rows * width * chans),
        name="pair_terms",
    )(own, act_edge, grad_edge, their_pre, their_grad)
    *terms, own_piece = pl.pallas_call(
        edge_kernel,
        out_shape=tuple(pieces),
        in_specs=[vmem()] * 4,
        out_specs=(vmem(),) * len(pieces),
        scratch_shapes=[
            pltpu.VMEM((PLANE * LANES, 2 * width), BF16),
            pltpu.VMEM((NEAR * PLANE, far, 3, block, LANES), F32),
        ],
        compiler_params=params,
        cost_estimate=pl.CostEstimate(flops=flops // 8, bytes_accessed=4000000, transcendentals=width * chans),
        name="edge_terms",
    )(term, act_edge, grad_edge, near_row)

    got = []
    for (k, _, _), term in zip(order, terms):
        moves = []
        for z in range(blocks):
            for i in range(space):
                to_z, to_i = z ^ (k // PLANE), i ^ (k % PLANE * PAIR)
                moves.append((z * space + i, to_z * space + to_i))
        got.append(lax.ppermute(term, ("dp", "space"), moves))


    their_edge = lax.dynamic_index_in_dim(their_grad, my_core() * (rows - 1), 0)
    got[0], got[1], near_row, their_edge = lax.optimization_barrier((got[0], got[1], near_row, their_edge))
    in_grad = input_part(0, near_row)
    *first_got, in_grad = lax.optimization_barrier((*got[:7], in_grad))
    got[:7] = first_got
    travel = own_piece[1:] + sum(part[-(far - 1) :].astype(F32) for part in got[:7])
    others = []
    for k in range(1, far):
        moves = [(z, z ^ (k * NEAR)) for z in range(blocks)]
        others.append(lax.ppermute(travel[k - 1].astype(BF16), "dp", moves))
    in_grad = input_part(1, their_edge, in_grad)
    *others, in_grad = lax.optimization_barrier((*others, in_grad))
    total = own_piece[0] + sum(part[0].astype(F32) for part in got[:3] + got[7:])
    total = total + sum(other.astype(F32) for other in others)
    total = total * factor
    if outer > 1:
        total = lax.psum(total, "space", axis_index_groups=[[o * inner + i for o in range(outer)] for i in range(inner)])
    final = total.astype(BF16)
    parts = [final]
    for k in range(1, PLANE):
        parts.append(lax.ppermute(final, "space", [(i, i ^ (k * PAIR)) for i in range(space)]))
    parts = jnp.stack(parts)
    their_parts = lax.ppermute(parts, "space", pairs)

    def place(flip, parts, *before):
        return pl.pallas_call(
            functools.partial(place_kernel, flip),
            out_shape=jax.ShapeDtypeStruct((chans, 9 * block), F32),
            in_specs=[vmem()] * 2 + [anywhere()] * len(before),
            out_specs=anywhere(),
            scratch_shapes=[
                pltpu.VMEM((3, block, PLANE * LANES), F32),
                pltpu.VMEM((9 * block, half), F32),
                pltpu.VMEM((half, 9 * block), F32),
                pltpu.SemaphoreType.DMA((10,)),
            ],
            input_output_aliases={2: 0} if before else {},
            compiler_params=params,
            cost_estimate=pl.CostEstimate(flops=81 * block * block * chans, bytes_accessed=1000000, transcendentals=0),
            name="place_rows",
        )(parts, pick, *before)

    placed = place(1, their_parts, place(0, parts))
    return jnp.swapaxes(in_grad, 1, 2)[None], placed.T


def solution(mesh):
    placed = (P("dp", "space", None, None), P("dp", "space", None, None), P())
    return jax.shard_map(
        shards,
        mesh=mesh,
        in_specs=placed,
        out_specs=(P("dp", "space", None, None), P("dp", None)),
        check_vma=False,
    )
```

```python
import functools

import jax
import jax.numpy as jnp
from jax import lax
from jax.experimental import pallas as pl
from jax.experimental.pallas import tpu as pltpu
from jax.sharding import PartitionSpec as P

F32 = jnp.float32
BF16 = jnp.bfloat16
LANES = 128
PAIR = 2
PLANE = 4
NEAR = 2
VMEM_LIMIT = 16 * 1024 * 1024
NT = (((1,), (1,)), ((), ()))


def vmem():
    return pl.BlockSpec(memory_space=pltpu.VMEM)


def anywhere():
    return pl.BlockSpec(memory_space=pl.ANY)


def column_shifts(row):
    wide = row.astype(F32)
    width = wide.shape[1]
    at = lax.broadcasted_iota(jnp.int32, wide.shape, 1)
    ahead = jnp.where(at == width - 1, 0.0, pltpu.roll(wide, width - 1, 1))
    behind = jnp.where(at == 0, 0.0, pltpu.roll(wide, 1, 1))
    return ahead.astype(BF16), row, behind.astype(BF16)


def put_taps(taps_s, slot, row):
    half, width = row.shape
    for b, shifted in enumerate(column_shifts(row)):
        taps_s[b * half : (b + 1) * half, slot * width : (slot + 1) * width] = shifted


def plane_index():
    return lax.rem(lax.axis_index("space") // PAIR, PLANE)


def near_index():
    return lax.rem(lax.axis_index("dp"), NEAR) * PLANE + plane_index()


def silu(v):
    x = v.astype(F32)
    return (x / (1.0 + jnp.exp(-x))).astype(BF16)


def my_core():
    return lax.rem(lax.axis_index("space"), PAIR)


def chip_kernel(pre_ref, grad_ref, their_pre_ref, their_grad_ref, out_ref, act_edge_ref, grad_edge_ref, act_s, taps_s):
    rows, chans, width = pre_ref.shape
    half = chans // PAIR
    core = my_core()
    first = core == 0
    mine = pl.ds(pl.multiple_of(core * half, half), half)
    zero = jnp.zeros((half, width), BF16)
    taps_s[3 * half :, :] = jnp.zeros((taps_s.shape[0] - 3 * half, taps_s.shape[1]), BF16)
    for part, (ref, other_ref, upper) in enumerate(((grad_ref, their_grad_ref, first), (their_grad_ref, grad_ref, ~first))):
        at = part * (rows + 2)
        put_taps(taps_s, at, jnp.where(upper, zero, other_ref[rows - 1, mine, :]))
        for r in range(rows):
            put_taps(taps_s, at + r + 1, ref[r, mine, :])
        put_taps(taps_s, at + rows + 1, jnp.where(upper, other_ref[0, mine, :], zero))
    for part, ref in enumerate((pre_ref, their_pre_ref)):
        for r in range(rows):
            act_s[:, (part * rows + r) * width : (part * rows + r + 1) * width] = silu(ref[r])
    for i, r in enumerate((0, rows - 1)):
        act_edge_ref[i] = act_s[:, r * width : (r + 1) * width]
        grad_edge_ref[i] = grad_ref[r, mine, :]
    for a in range(3):
        terms = []
        for part in range(PAIR):
            at = (part * (rows + 2) + 2 - a) * width
            terms.append(
                lax.dot_general(
                    act_s[:, part * rows * width : (part + 1) * rows * width],
                    taps_s[:, at : at + rows * width],
                    NT,
                    preferred_element_type=F32,
                )
            )
        out_ref[a] = terms[0] + terms[1]


def edge_kernel(term_ref, act_edge_ref, grad_edge_ref, near_ref, *refs):
    out_refs, (taps_s, term_s) = refs[: PLANE * NEAR], refs[PLANE * NEAR :]
    _, chans, width = near_ref.shape
    half = chans // PAIR
    outers, _, block, _ = out_refs[0].shape
    core = my_core()
    first = core == 0
    near_act = silu(near_ref[1])
    near_grad = near_ref[0, pl.ds(pl.multiple_of(core * half, half), half), :]
    taps_s[3 * half :, :] = jnp.zeros((taps_s.shape[0] - 3 * half, taps_s.shape[1]), BF16)
    put_taps(taps_s, 0, jnp.where(first, grad_edge_ref[0], near_grad))
    put_taps(taps_s, 1, jnp.where(first, near_grad, grad_edge_ref[1]))
    acts = {0: jnp.where(first, near_act, act_edge_ref[1]), 2: jnp.where(first, act_edge_ref[0], near_act)}
    for a in range(3):
        term = term_ref[a]
        if a in acts:
            taps = taps_s[:, a // 2 * width : (a // 2 + 1) * width]
            term += lax.dot_general(acts[a], taps, NT, preferred_element_type=F32)
        for p in range(PLANE):
            for z in range(NEAR * outers):
                term_s[z % NEAR * PLANE + p, z // NEAR, a] = term[z * block : (z + 1) * block, p * LANES : (p + 1) * LANES]
    at, outer_at = near_index(), lax.axis_index("dp") // NEAR
    for k, out_ref in enumerate(out_refs):
        for j in range(outers):
            out_ref[j] = term_s[at ^ k, outer_at ^ j].astype(out_ref.dtype)


def input_kernel(side, pre_ref, grad_ref, edge_ref, kernel_ref, *refs):
    out_hbm, taps_s, out_s, sem = refs[-4:]
    rows, chans, width = pre_ref.shape
    count = rows // 2
    upper = my_core() == side
    start = jnp.where(upper, 0, count)
    put_taps(taps_s, 0, jnp.where(upper, edge_ref[0], grad_ref[count - 1]))
    for r in range(count):
        put_taps(taps_s, r + 1, grad_ref[start + r])
    put_taps(taps_s, count + 1, jnp.where(upper, grad_ref[count], edge_ref[0]))
    step = 2
    copies = []
    for top in range(0, count, step):
        total = jnp.zeros((chans, step * width), F32)
        for a in range(3):
            at = (top + 2 - a) * width
            for b in range(3):
                taps = taps_s[b * chans : (b + 1) * chans, at : at + step * width]
                total += jnp.dot(kernel_ref[a, b], taps, preferred_element_type=F32)
        for r in range(step):
            x = pre_ref[start + top + r].astype(F32)
            sig = 1.0 / (1.0 + jnp.exp(-x))
            deriv = sig * (1.0 + x * (1.0 - sig))
            out_s[top + r] = (total[:, r * width : (r + 1) * width] * deriv).astype(out_s.dtype)
        copies.append(
            pltpu.make_async_copy(
                out_s.at[pl.ds(top, step)], out_hbm.at[pl.ds(start + top, step)], sem.at[top // step]
            )
        )
        copies[-1].start()
    for copy in copies:
        copy.wait()


def pick_kernel(after_ref, out_ref):
    size = out_ref.shape[0]
    group = size // 9
    j = lax.broadcasted_iota(jnp.int32, (size, size), 0)
    k = lax.broadcasted_iota(jnp.int32, (size, size), 1)
    pick = jnp.zeros((size, size), F32)
    for t in range(9):
        c = k - t * group
        pick = jnp.where((c >= 0) & (c < group) & (j == 9 * c + t), 1.0, pick)
    out_ref[...] = pick


def place_kernel(flip, parts_ref, pick_ref, *refs):
    out_hbm, wide_s, turned_s, out_s, sem = refs[-5:]
    _, _, block, _ = parts_ref.shape
    half = out_s.shape[0]
    width = pick_ref.shape[0]
    group = width // 9
    for k in range(PLANE):
        lanes = pl.ds(pl.multiple_of((plane_index() ^ k) * LANES, LANES), LANES)
        wide_s[:, :, lanes] = parts_ref[k].astype(F32)
    pick = pick_ref[...].astype(BF16)
    for g in range(block // group):
        rows = [wide_s[t // 3, g * group : (g + 1) * group, t % 3 * half : (t % 3 + 1) * half] for t in range(9)]
        rows = jnp.concatenate(rows, axis=0).astype(BF16)
        turned_s[g * width : (g + 1) * width, :] = jnp.dot(pick, rows, preferred_element_type=F32)
    turned = turned_s[...].astype(BF16)
    step = half // sem.shape[0]
    first = (my_core() ^ flip) * half
    copies = []
    for n in range(sem.shape[0]):
        i = lax.broadcasted_iota(jnp.int32, (step, half), 0)
        j = lax.broadcasted_iota(jnp.int32, (step, half), 1)
        same = jnp.where(i + n * step == j, 1.0, 0.0).astype(BF16)
        here = slice(n * step, (n + 1) * step)
        out_s[here, :] = lax.dot_general(same, turned, NT, preferred_element_type=F32)
        to = pl.ds(pl.multiple_of(first + n * step, 8), step)
        copies.append(pltpu.make_async_copy(out_s.at[here], out_hbm.at[to], sem.at[n]))
        copies[-1].start()
    for copy in copies:
        copy.wait()


def shards(pre_act, out_grad, kernel):
    images, rows, width, chans = pre_act.shape
    assert images == 1
    space, blocks = lax.axis_size("space"), lax.axis_size("dp")
    inner = PAIR * PLANE
    outer = space // inner
    block = chans // blocks
    half = chans // PAIR
    group = 16 if block % 16 == 0 else block
    far = blocks // NEAR
    factor = float(images * rows * width * space * blocks) ** (-0.5)
    params = pltpu.CompilerParams(vmem_limit_bytes=VMEM_LIMIT)
    flops = 2 * 9 * chans * chans * rows * width

    pre = jnp.swapaxes(pre_act[0], 1, 2)
    grad = jnp.swapaxes(out_grad[0], 1, 2)
    row = my_core() * (rows - 1)
    edge = jnp.stack([lax.dynamic_index_in_dim(grad, row, 0, False), lax.dynamic_index_in_dim(pre, row, 0, False)])
    beyond = [(i, i + 1 if i % 2 else i - 1) for i in range(space)]
    pairs = [(i, i + 1 - 2 * (i % 2)) for i in range(space)]

    def inside(moves):
        return [(i, j) for i, j in moves if 0 <= j < space]

    near_row = lax.ppermute(edge, "space", inside(beyond))
    _, my_pre, my_grad = lax.optimization_barrier((edge, pre, grad))
    their_grad = lax.ppermute(my_grad, "space", pairs)
    their_pre = lax.ppermute(my_pre, "space", pairs)
    pick = pl.pallas_call(
        pick_kernel,
        out_shape=jax.ShapeDtypeStruct((9 * group, 9 * group), F32),
        in_specs=[anywhere()],
        out_specs=vmem(),
        compiler_params=params,
        cost_estimate=pl.CostEstimate(flops=flops, bytes_accessed=4000000, transcendentals=0),
        name="pick_rows",
    )(edge)
    pick, own_pre, own_grad = lax.optimization_barrier((pick, pre, grad))
    def input_part(side, edge_rows, *before):
        count = rows // 2
        return pl.pallas_call(
            functools.partial(input_kernel, side),
            out_shape=jax.ShapeDtypeStruct((rows, chans, width), BF16),
            in_specs=[vmem()] * 4 + [anywhere()] * len(before),
            out_specs=anywhere(),
            scratch_shapes=[
                pltpu.VMEM((3 * chans, (count + 2) * width), BF16),
                pltpu.VMEM((count, chans, width), BF16),
                pltpu.SemaphoreType.DMA((count // 2,)),
            ],
            input_output_aliases={4: 0} if before else {},
            compiler_params=params,
            cost_estimate=pl.CostEstimate(
                flops=flops // 2, bytes_accessed=3000000, transcendentals=rows * width * chans // 2
            ),
            name="input_grad",
        )(pre, grad, edge_rows, kernel, *before)

    piece = jax.ShapeDtypeStruct((far, 3, block, LANES), BF16)
    term, act_edge, grad_edge = pl.pallas_call(
        chip_kernel,
        out_shape=(
            jax.ShapeDtypeStruct((3, chans, PLANE * LANES), F32),
            jax.ShapeDtypeStruct((2, chans, width), BF16),
            jax.ShapeDtypeStruct((2, half, width), BF16),
        ),
        in_specs=[vmem()] * 4,
        out_specs=(vmem(),) * 3,
        scratch_shapes=[
            pltpu.VMEM((chans, PAIR * rows * width), BF16),
            pltpu.VMEM((PLANE * LANES, PAIR * (rows + 2) * width), BF16),
        ],
        compiler_params=params,
        cost_estimate=pl.CostEstimate(flops=2 * flops, bytes_accessed=4000000, transcendentals=2 * rows * width * chans),
        name="chip_terms",
    )(own_pre, own_grad, their_pre, their_grad)
    terms = pl.pallas_call(
        edge_kernel,
        out_shape=(jax.ShapeDtypeStruct(piece.shape, F32),) + (piece,) * (NEAR * PLANE - 1),
        in_specs=[vmem()] * 4,
        out_specs=(vmem(),) * (NEAR * PLANE),
        scratch_shapes=[
            pltpu.VMEM((PLANE * LANES, 2 * width), BF16),
            pltpu.VMEM((NEAR * PLANE, far, 3, block, LANES), F32),
        ],
        compiler_params=params,
        cost_estimate=pl.CostEstimate(flops=flops // 8, bytes_accessed=4000000, transcendentals=width * chans),
        name="edge_terms",
    )(term, act_edge, grad_edge, near_row)

    got = [terms[0]]
    for k in (4, 6, 1, 7, 5, 3, 2):
        moves = []
        for z in range(blocks):
            for i in range(space):
                to_z, to_i = z ^ (k // PLANE), i ^ (k % PLANE * PAIR)
                moves.append((z * space + i, to_z * space + to_i))
        got.append(lax.ppermute(terms[k], ("dp", "space"), moves))


    their_edge = lax.dynamic_index_in_dim(their_grad, my_core() * (rows - 1), 0)
    got[1], got[2], near_row, their_edge = lax.optimization_barrier((got[1], got[2], near_row, their_edge))
    in_grad = input_part(1, their_edge, input_part(0, near_row))
    *got, in_grad = lax.optimization_barrier((*got, in_grad))
    near_sum = sum(part.astype(F32) for part in got)
    others = []
    for k in range(1, far):
        moves = [(z, z ^ (k * NEAR)) for z in range(blocks)]
        others.append(lax.ppermute(near_sum[k].astype(BF16), "dp", moves))
    total = near_sum[0] + sum(other.astype(F32) for other in others)
    total = total * factor
    if outer > 1:
        total = lax.psum(total, "space", axis_index_groups=[[o * inner + i for o in range(outer)] for i in range(inner)])
    final = total.astype(BF16)
    parts = [final]
    for k in range(1, PLANE):
        parts.append(lax.ppermute(final, "space", [(i, i ^ (k * PAIR)) for i in range(space)]))
    parts = jnp.stack(parts)
    their_parts = lax.ppermute(parts, "space", pairs)

    def place(flip, parts, *before):
        return pl.pallas_call(
            functools.partial(place_kernel, flip),
            out_shape=jax.ShapeDtypeStruct((chans, 9 * block), F32),
            in_specs=[vmem()] * 2 + [anywhere()] * len(before),
            out_specs=anywhere(),
            scratch_shapes=[
                pltpu.VMEM((3, block, PLANE * LANES), F32),
                pltpu.VMEM((9 * block, half), F32),
                pltpu.VMEM((half, 9 * block), F32),
                pltpu.SemaphoreType.DMA((2,)),
            ],
            input_output_aliases={2: 0} if before else {},
            compiler_params=params,
            cost_estimate=pl.CostEstimate(flops=81 * block * block * chans, bytes_accessed=1000000, transcendentals=0),
            name="place_rows",
        )(parts, pick, *before)

    placed = place(1, their_parts, place(0, parts))
    return jnp.swapaxes(in_grad, 1, 2)[None], placed.T


def solution(mesh):
    placed = (P("dp", "space", None, None), P("dp", "space", None, None), P())
    return jax.shard_map(
        shards,
        mesh=mesh,
        in_specs=placed,
        out_specs=(P("dp", "space", None, None), P("dp", None)),
        check_vma=False,
    )
```

```python
import functools

import jax
import jax.numpy as jnp
from jax import lax
from jax.experimental import pallas as pl
from jax.experimental.pallas import tpu as pltpu
from jax.sharding import PartitionSpec as P

F32 = jnp.float32
BF16 = jnp.bfloat16
LANES = 128
PAIR = 2
PLANE = 4
NEAR = 2
VMEM_LIMIT = 16 * 1024 * 1024
NT = (((1,), (1,)), ((), ()))


def vmem():
    return pl.BlockSpec(memory_space=pltpu.VMEM)


def anywhere():
    return pl.BlockSpec(memory_space=pl.ANY)


def column_shifts(row):
    wide = row.astype(F32)
    width = wide.shape[1]
    at = lax.broadcasted_iota(jnp.int32, wide.shape, 1)
    ahead = jnp.where(at == width - 1, 0.0, pltpu.roll(wide, width - 1, 1))
    behind = jnp.where(at == 0, 0.0, pltpu.roll(wide, 1, 1))
    return ahead.astype(BF16), row, behind.astype(BF16)


def put_taps(taps_s, slot, row):
    half, width = row.shape
    for b, shifted in enumerate(column_shifts(row)):
        taps_s[b * half : (b + 1) * half, slot * width : (slot + 1) * width] = shifted


def plane_index():
    return lax.rem(lax.axis_index("space") // PAIR, PLANE)


def near_index():
    return lax.rem(lax.axis_index("dp"), NEAR) * PLANE + plane_index()


def silu(v):
    x = v.astype(F32)
    return (x / (1.0 + jnp.exp(-x))).astype(BF16)


def my_core():
    return lax.rem(lax.axis_index("space"), PAIR)


def chip_kernel(pre_ref, grad_ref, their_pre_ref, their_grad_ref, out_ref, act_edge_ref, grad_edge_ref, act_s, taps_s):
    rows, chans, width = pre_ref.shape
    half = chans // PAIR
    core = my_core()
    first = core == 0
    mine = pl.ds(pl.multiple_of(core * half, half), half)
    zero = jnp.zeros((half, width), BF16)
    taps_s[3 * half :, :] = jnp.zeros((taps_s.shape[0] - 3 * half, taps_s.shape[1]), BF16)
    for part, (ref, other_ref, upper) in enumerate(((grad_ref, their_grad_ref, first), (their_grad_ref, grad_ref, ~first))):
        at = part * (rows + 2)
        put_taps(taps_s, at, jnp.where(upper, zero, other_ref[rows - 1, mine, :]))
        for r in range(rows):
            put_taps(taps_s, at + r + 1, ref[r, mine, :])
        put_taps(taps_s, at + rows + 1, jnp.where(upper, other_ref[0, mine, :], zero))
    for part, ref in enumerate((pre_ref, their_pre_ref)):
        for r in range(rows):
            act_s[:, (part * rows + r) * width : (part * rows + r + 1) * width] = silu(ref[r])
    for i, r in enumerate((0, rows - 1)):
        act_edge_ref[i] = act_s[:, r * width : (r + 1) * width]
        grad_edge_ref[i] = grad_ref[r, mine, :]
    for a in range(3):
        terms = []
        for part in range(PAIR):
            at = (part * (rows + 2) + 2 - a) * width
            terms.append(
                lax.dot_general(
                    act_s[:, part * rows * width : (part + 1) * rows * width],
                    taps_s[:, at : at + rows * width],
                    NT,
                    preferred_element_type=F32,
                )
            )
        out_ref[a] = terms[0] + terms[1]


def edge_kernel(term_ref, act_edge_ref, grad_edge_ref, near_ref, *refs):
    out_refs, (taps_s, term_s) = refs[: PLANE * NEAR], refs[PLANE * NEAR :]
    _, chans, width = near_ref.shape
    half = chans // PAIR
    outers, _, block, _ = out_refs[0].shape
    core = my_core()
    first = core == 0
    near_act = silu(near_ref[1])
    near_grad = near_ref[0, pl.ds(pl.multiple_of(core * half, half), half), :]
    taps_s[3 * half :, :] = jnp.zeros((taps_s.shape[0] - 3 * half, taps_s.shape[1]), BF16)
    put_taps(taps_s, 0, jnp.where(first, grad_edge_ref[0], near_grad))
    put_taps(taps_s, 1, jnp.where(first, near_grad, grad_edge_ref[1]))
    acts = {0: jnp.where(first, near_act, act_edge_ref[1]), 2: jnp.where(first, act_edge_ref[0], near_act)}
    for a in range(3):
        term = term_ref[a]
        if a in acts:
            taps = taps_s[:, a // 2 * width : (a // 2 + 1) * width]
            term += lax.dot_general(acts[a], taps, NT, preferred_element_type=F32)
        for p in range(PLANE):
            for z in range(NEAR * outers):
                term_s[z % NEAR * PLANE + p, z // NEAR, a] = term[z * block : (z + 1) * block, p * LANES : (p + 1) * LANES]
    at, outer_at = near_index(), lax.axis_index("dp") // NEAR
    for k, out_ref in enumerate(out_refs):
        for j in range(outers):
            out_ref[j] = term_s[at ^ k, outer_at ^ j].astype(out_ref.dtype)


def input_kernel(side, pre_ref, grad_ref, edge_ref, kernel_ref, *refs):
    out_hbm, taps_s, out_s, sem = refs[-4:]
    rows, chans, width = pre_ref.shape
    count = rows // 2
    upper = my_core() == side
    start = jnp.where(upper, 0, count)
    put_taps(taps_s, 0, jnp.where(upper, edge_ref[0], grad_ref[count - 1]))
    for r in range(count):
        put_taps(taps_s, r + 1, grad_ref[start + r])
    put_taps(taps_s, count + 1, jnp.where(upper, grad_ref[count], edge_ref[0]))
    step = 2
    copies = []
    for top in range(0, count, step):
        total = jnp.zeros((chans, step * width), F32)
        for a in range(3):
            at = (top + 2 - a) * width
            for b in range(3):
                taps = taps_s[b * chans : (b + 1) * chans, at : at + step * width]
                total += jnp.dot(kernel_ref[a, b], taps, preferred_element_type=F32)
        for r in range(step):
            x = pre_ref[start + top + r].astype(F32)
            sig = 1.0 / (1.0 + jnp.exp(-x))
            deriv = sig * (1.0 + x * (1.0 - sig))
            out_s[top + r] = (total[:, r * width : (r + 1) * width] * deriv).astype(out_s.dtype)
        copies.append(
            pltpu.make_async_copy(
                out_s.at[pl.ds(top, step)], out_hbm.at[pl.ds(start + top, step)], sem.at[top // step]
            )
        )
        copies[-1].start()
    for copy in copies:
        copy.wait()


def pick_kernel(after_ref, out_ref):
    size = out_ref.shape[0]
    group = size // 9
    j = lax.broadcasted_iota(jnp.int32, (size, size), 0)
    k = lax.broadcasted_iota(jnp.int32, (size, size), 1)
    pick = jnp.zeros((size, size), F32)
    for t in range(9):
        c = k - t * group
        pick = jnp.where((c >= 0) & (c < group) & (j == 9 * c + t), 1.0, pick)
    out_ref[...] = pick


def place_kernel(flip, parts_ref, pick_ref, *refs):
    out_hbm, wide_s, turned_s, out_s, sem = refs[-5:]
    _, _, block, _ = parts_ref.shape
    half = out_s.shape[0]
    width = pick_ref.shape[0]
    group = width // 9
    for k in range(PLANE):
        lanes = pl.ds(pl.multiple_of((plane_index() ^ k) * LANES, LANES), LANES)
        wide_s[:, :, lanes] = parts_ref[k].astype(F32)
    pick = pick_ref[...].astype(BF16)
    for g in range(block // group):
        rows = [wide_s[t // 3, g * group : (g + 1) * group, t % 3 * half : (t % 3 + 1) * half] for t in range(9)]
        rows = jnp.concatenate(rows, axis=0).astype(BF16)
        turned_s[g * width : (g + 1) * width, :] = jnp.dot(pick, rows, preferred_element_type=F32)
    turned = turned_s[...].astype(BF16)
    step = half // sem.shape[0]
    first = (my_core() ^ flip) * half
    copies = []
    for n in range(sem.shape[0]):
        i = lax.broadcasted_iota(jnp.int32, (step, half), 0)
        j = lax.broadcasted_iota(jnp.int32, (step, half), 1)
        same = jnp.where(i + n * step == j, 1.0, 0.0).astype(BF16)
        here = slice(n * step, (n + 1) * step)
        out_s[here, :] = lax.dot_general(same, turned, NT, preferred_element_type=F32)
        to = pl.ds(pl.multiple_of(first + n * step, 8), step)
        copies.append(pltpu.make_async_copy(out_s.at[here], out_hbm.at[to], sem.at[n]))
        copies[-1].start()
    for copy in copies:
        copy.wait()


def shards(pre_act, out_grad, kernel):
    images, rows, width, chans = pre_act.shape
    assert images == 1
    space, blocks = lax.axis_size("space"), lax.axis_size("dp")
    inner = PAIR * PLANE
    outer = space // inner
    block = chans // blocks
    half = chans // PAIR
    group = 16 if block % 16 == 0 else block
    far = blocks // NEAR
    factor = float(images * rows * width * space * blocks) ** (-0.5)
    params = pltpu.CompilerParams(vmem_limit_bytes=VMEM_LIMIT)
    flops = 2 * 9 * chans * chans * rows * width

    pre = jnp.swapaxes(pre_act[0], 1, 2)
    grad = jnp.swapaxes(out_grad[0], 1, 2)
    row = my_core() * (rows - 1)
    edge = jnp.stack([lax.dynamic_index_in_dim(grad, row, 0, False), lax.dynamic_index_in_dim(pre, row, 0, False)])
    beyond = [(i, i + 1 if i % 2 else i - 1) for i in range(space)]
    pairs = [(i, i + 1 - 2 * (i % 2)) for i in range(space)]

    def inside(moves):
        return [(i, j) for i, j in moves if 0 <= j < space]

    near_row = lax.ppermute(edge, "space", inside(beyond))
    _, my_pre, my_grad = lax.optimization_barrier((edge, pre, grad))
    their_grad = lax.ppermute(my_grad, "space", pairs)
    their_pre = lax.ppermute(my_pre, "space", pairs)
    pick = pl.pallas_call(
        pick_kernel,
        out_shape=jax.ShapeDtypeStruct((9 * group, 9 * group), F32),
        in_specs=[anywhere()],
        out_specs=vmem(),
        compiler_params=params,
        cost_estimate=pl.CostEstimate(flops=flops, bytes_accessed=4000000, transcendentals=0),
        name="pick_rows",
    )(edge)
    pick, own_pre, own_grad = lax.optimization_barrier((pick, pre, grad))
    def input_part(side, edge_rows, *before):
        count = rows // 2
        return pl.pallas_call(
            functools.partial(input_kernel, side),
            out_shape=jax.ShapeDtypeStruct((rows, chans, width), BF16),
            in_specs=[vmem()] * 4 + [anywhere()] * len(before),
            out_specs=anywhere(),
            scratch_shapes=[
                pltpu.VMEM((3 * chans, (count + 2) * width), BF16),
                pltpu.VMEM((count, chans, width), BF16),
                pltpu.SemaphoreType.DMA((count // 2,)),
            ],
            input_output_aliases={4: 0} if before else {},
            compiler_params=params,
            cost_estimate=pl.CostEstimate(
                flops=flops // 2, bytes_accessed=3000000, transcendentals=rows * width * chans // 2
            ),
            name="input_grad",
        )(pre, grad, edge_rows, kernel, *before)

    piece = jax.ShapeDtypeStruct((far, 3, block, LANES), BF16)
    term, act_edge, grad_edge = pl.pallas_call(
        chip_kernel,
        out_shape=(
            jax.ShapeDtypeStruct((3, chans, PLANE * LANES), F32),
            jax.ShapeDtypeStruct((2, chans, width), BF16),
            jax.ShapeDtypeStruct((2, half, width), BF16),
        ),
        in_specs=[vmem()] * 4,
        out_specs=(vmem(),) * 3,
        scratch_shapes=[
            pltpu.VMEM((chans, PAIR * rows * width), BF16),
            pltpu.VMEM((PLANE * LANES, PAIR * (rows + 2) * width), BF16),
        ],
        compiler_params=params,
        cost_estimate=pl.CostEstimate(flops=2 * flops, bytes_accessed=4000000, transcendentals=2 * rows * width * chans),
        name="chip_terms",
    )(own_pre, own_grad, their_pre, their_grad)
    terms = pl.pallas_call(
        edge_kernel,
        out_shape=(jax.ShapeDtypeStruct(piece.shape, F32),) + (piece,) * (NEAR * PLANE - 1),
        in_specs=[vmem()] * 4,
        out_specs=(vmem(),) * (NEAR * PLANE),
        scratch_shapes=[
            pltpu.VMEM((PLANE * LANES, 2 * width), BF16),
            pltpu.VMEM((NEAR * PLANE, far, 3, block, LANES), F32),
        ],
        compiler_params=params,
        cost_estimate=pl.CostEstimate(flops=flops // 8, bytes_accessed=4000000, transcendentals=width * chans),
        name="edge_terms",
    )(term, act_edge, grad_edge, near_row)

    got = [terms[0]]
    for k in (4, 1, 2, 7, 3, 5, 6):
        moves = []
        for z in range(blocks):
            for i in range(space):
                to_z, to_i = z ^ (k // PLANE), i ^ (k % PLANE * PAIR)
                moves.append((z * space + i, to_z * space + to_i))
        got.append(lax.ppermute(terms[k], ("dp", "space"), moves))


    their_edge = lax.dynamic_index_in_dim(their_grad, my_core() * (rows - 1), 0)
    got[1], got[2], near_row, their_edge = lax.optimization_barrier((got[1], got[2], near_row, their_edge))
    in_grad = input_part(1, their_edge, input_part(0, near_row))
    *got, in_grad = lax.optimization_barrier((*got, in_grad))
    near_sum = sum(part.astype(F32) for part in got)
    others = []
    for k in range(1, far):
        moves = [(z, z ^ (k * NEAR)) for z in range(blocks)]
        others.append(lax.ppermute(near_sum[k].astype(BF16), "dp", moves))
    total = near_sum[0] + sum(other.astype(F32) for other in others)
    total = total * factor
    if outer > 1:
        total = lax.psum(total, "space", axis_index_groups=[[o * inner + i for o in range(outer)] for i in range(inner)])
    final = total.astype(BF16)
    parts = [final]
    for k in range(1, PLANE):
        parts.append(lax.ppermute(final, "space", [(i, i ^ (k * PAIR)) for i in range(space)]))
    parts = jnp.stack(parts)
    their_parts = lax.ppermute(parts, "space", pairs)

    def place(flip, parts, *before):
        return pl.pallas_call(
            functools.partial(place_kernel, flip),
            out_shape=jax.ShapeDtypeStruct((chans, 9 * block), F32),
            in_specs=[vmem()] * 2 + [anywhere()] * len(before),
            out_specs=anywhere(),
            scratch_shapes=[
                pltpu.VMEM((3, block, PLANE * LANES), F32),
                pltpu.VMEM((9 * block, half), F32),
                pltpu.VMEM((half, 9 * block), F32),
                pltpu.SemaphoreType.DMA((2,)),
            ],
            input_output_aliases={2: 0} if before else {},
            compiler_params=params,
            cost_estimate=pl.CostEstimate(flops=81 * block * block * chans, bytes_accessed=1000000, transcendentals=0),
            name="place_rows",
        )(parts, pick, *before)

    placed = place(1, their_parts, place(0, parts))
    return jnp.swapaxes(in_grad, 1, 2)[None], placed.T


def solution(mesh):
    placed = (P("dp", "space", None, None), P("dp", "space", None, None), P())
    return jax.shard_map(
        shards,
        mesh=mesh,
        in_specs=placed,
        out_specs=(P("dp", "space", None, None), P("dp", None)),
        check_vma=False,
    )
```

```python
import functools

import jax
import jax.numpy as jnp
from jax import lax
from jax.experimental import pallas as pl
from jax.experimental.pallas import tpu as pltpu
from jax.sharding import PartitionSpec as P

F32 = jnp.float32
BF16 = jnp.bfloat16
LANES = 128
PAIR = 2
PLANE = 4
NEAR = 2
VMEM_LIMIT = 16 * 1024 * 1024
NT = (((1,), (1,)), ((), ()))


FIRST_ORDER = ((4, 2, 1, 7, 3, 6, 5), (4, 1, 2, 7, 3, 5, 6))
SPREAD_ORDER = ((2, 1, 3), (1, 2, 3))


def by_core(orders, core, slot):
    return jnp.where(core == 0, orders[0][slot], orders[1][slot])


def vmem():
    return pl.BlockSpec(memory_space=pltpu.VMEM)


def anywhere():
    return pl.BlockSpec(memory_space=pl.ANY)


def column_shifts(row):
    wide = row.astype(F32)
    width = wide.shape[1]
    at = lax.broadcasted_iota(jnp.int32, wide.shape, 1)
    ahead = jnp.where(at == width - 1, 0.0, pltpu.roll(wide, width - 1, 1))
    behind = jnp.where(at == 0, 0.0, pltpu.roll(wide, 1, 1))
    return ahead.astype(BF16), row, behind.astype(BF16)


def put_taps(taps_s, slot, row):
    half, width = row.shape
    for b, shifted in enumerate(column_shifts(row)):
        taps_s[b * half : (b + 1) * half, slot * width : (slot + 1) * width] = shifted


def plane_index():
    return lax.rem(lax.axis_index("space") // PAIR, PLANE)


def near_index():
    return lax.rem(lax.axis_index("dp"), NEAR) * PLANE + plane_index()


def silu(v):
    x = v.astype(F32)
    return (x / (1.0 + jnp.exp(-x))).astype(BF16)


def my_core():
    return lax.rem(lax.axis_index("space"), PAIR)


def chip_kernel(pre_ref, grad_ref, their_pre_ref, their_grad_ref, out_ref, act_edge_ref, grad_edge_ref, act_s, taps_s):
    rows, chans, width = pre_ref.shape
    half = chans // PAIR
    core = my_core()
    first = core == 0
    mine = pl.ds(pl.multiple_of(core * half, half), half)
    zero = jnp.zeros((half, width), BF16)
    taps_s[3 * half :, :] = jnp.zeros((taps_s.shape[0] - 3 * half, taps_s.shape[1]), BF16)
    for part, (ref, other_ref, upper) in enumerate(((grad_ref, their_grad_ref, first), (their_grad_ref, grad_ref, ~first))):
        at = part * (rows + 2)
        put_taps(taps_s, at, jnp.where(upper, zero, other_ref[rows - 1, mine, :]))
        for r in range(rows):
            put_taps(taps_s, at + r + 1, ref[r, mine, :])
        put_taps(taps_s, at + rows + 1, jnp.where(upper, other_ref[0, mine, :], zero))
    for part, ref in enumerate((pre_ref, their_pre_ref)):
        for r in range(rows):
            act_s[:, (part * rows + r) * width : (part * rows + r + 1) * width] = silu(ref[r])
    for i, r in enumerate((0, rows - 1)):
        act_edge_ref[i] = act_s[:, r * width : (r + 1) * width]
        grad_edge_ref[i] = grad_ref[r, mine, :]
    for a in range(3):
        terms = []
        for part in range(PAIR):
            at = (part * (rows + 2) + 2 - a) * width
            terms.append(
                lax.dot_general(
                    act_s[:, part * rows * width : (part + 1) * rows * width],
                    taps_s[:, at : at + rows * width],
                    NT,
                    preferred_element_type=F32,
                )
            )
        out_ref[a] = terms[0] + terms[1]


def edge_kernel(term_ref, act_edge_ref, grad_edge_ref, near_ref, *refs):
    out_refs, (taps_s, term_s) = refs[: PLANE * NEAR], refs[PLANE * NEAR :]
    _, chans, width = near_ref.shape
    half = chans // PAIR
    outers, _, block, _ = out_refs[0].shape
    core = my_core()
    first = core == 0
    near_act = silu(near_ref[1])
    near_grad = near_ref[0, pl.ds(pl.multiple_of(core * half, half), half), :]
    taps_s[3 * half :, :] = jnp.zeros((taps_s.shape[0] - 3 * half, taps_s.shape[1]), BF16)
    put_taps(taps_s, 0, jnp.where(first, grad_edge_ref[0], near_grad))
    put_taps(taps_s, 1, jnp.where(first, near_grad, grad_edge_ref[1]))
    acts = {0: jnp.where(first, near_act, act_edge_ref[1]), 2: jnp.where(first, act_edge_ref[0], near_act)}
    for a in range(3):
        term = term_ref[a]
        if a in acts:
            taps = taps_s[:, a // 2 * width : (a // 2 + 1) * width]
            term += lax.dot_general(acts[a], taps, NT, preferred_element_type=F32)
        for p in range(PLANE):
            for z in range(NEAR * outers):
                term_s[z % NEAR * PLANE + p, z // NEAR, a] = term[z * block : (z + 1) * block, p * LANES : (p + 1) * LANES]
    at, outer_at = near_index(), lax.axis_index("dp") // NEAR
    for slot, out_ref in enumerate(out_refs):
        k = by_core(FIRST_ORDER, core, slot - 1) if slot else 0
        for j in range(outers):
            out_ref[j] = term_s[at ^ k, outer_at ^ j].astype(out_ref.dtype)


def input_kernel(side, pre_ref, grad_ref, edge_ref, kernel_ref, *refs):
    out_hbm, taps_s, out_s, sem = refs[-4:]
    rows, chans, width = pre_ref.shape
    count = rows // 2
    upper = my_core() == side
    start = jnp.where(upper, 0, count)
    put_taps(taps_s, 0, jnp.where(upper, edge_ref[0], grad_ref[count - 1]))
    for r in range(count):
        put_taps(taps_s, r + 1, grad_ref[start + r])
    put_taps(taps_s, count + 1, jnp.where(upper, grad_ref[count], edge_ref[0]))
    step = 2
    copies = []
    for top in range(0, count, step):
        total = jnp.zeros((chans, step * width), F32)
        for a in range(3):
            at = (top + 2 - a) * width
            for b in range(3):
                taps = taps_s[b * chans : (b + 1) * chans, at : at + step * width]
                total += jnp.dot(kernel_ref[a, b], taps, preferred_element_type=F32)
        for r in range(step):
            x = pre_ref[start + top + r].astype(F32)
            sig = 1.0 / (1.0 + jnp.exp(-x))
            deriv = sig * (1.0 + x * (1.0 - sig))
            out_s[top + r] = (total[:, r * width : (r + 1) * width] * deriv).astype(out_s.dtype)
        copies.append(
            pltpu.make_async_copy(
                out_s.at[pl.ds(top, step)], out_hbm.at[pl.ds(start + top, step)], sem.at[top // step]
            )
        )
        copies[-1].start()
    for copy in copies:
        copy.wait()


def pick_kernel(after_ref, out_ref):
    size = out_ref.shape[0]
    group = size // 9
    j = lax.broadcasted_iota(jnp.int32, (size, size), 0)
    k = lax.broadcasted_iota(jnp.int32, (size, size), 1)
    pick = jnp.zeros((size, size), F32)
    for t in range(9):
        c = k - t * group
        pick = jnp.where((c >= 0) & (c < group) & (j == 9 * c + t), 1.0, pick)
    out_ref[...] = pick


def place_kernel(flip, parts_ref, pick_ref, *refs):
    out_hbm, wide_s, turned_s, out_s, sem = refs[-5:]
    _, _, block, _ = parts_ref.shape
    half = out_s.shape[0]
    width = pick_ref.shape[0]
    group = width // 9
    whose = my_core() ^ flip
    for slot in range(PLANE):
        k = by_core(SPREAD_ORDER, whose, slot - 1) if slot else 0
        lanes = pl.ds(pl.multiple_of((plane_index() ^ k) * LANES, LANES), LANES)
        wide_s[:, :, lanes] = parts_ref[slot].astype(F32)
    pick = pick_ref[...].astype(BF16)
    for g in range(block // group):
        rows = [wide_s[t // 3, g * group : (g + 1) * group, t % 3 * half : (t % 3 + 1) * half] for t in range(9)]
        rows = jnp.concatenate(rows, axis=0).astype(BF16)
        turned_s[g * width : (g + 1) * width, :] = jnp.dot(pick, rows, preferred_element_type=F32)
    turned = turned_s[...].astype(BF16)
    step = half // sem.shape[0]
    first = whose * half
    copies = []
    for n in range(sem.shape[0]):
        i = lax.broadcasted_iota(jnp.int32, (step, half), 0)
        j = lax.broadcasted_iota(jnp.int32, (step, half), 1)
        same = jnp.where(i + n * step == j, 1.0, 0.0).astype(BF16)
        here = slice(n * step, (n + 1) * step)
        out_s[here, :] = lax.dot_general(same, turned, NT, preferred_element_type=F32)
        to = pl.ds(pl.multiple_of(first + n * step, 8), step)
        copies.append(pltpu.make_async_copy(out_s.at[here], out_hbm.at[to], sem.at[n]))
        copies[-1].start()
    for copy in copies:
        copy.wait()


def shards(pre_act, out_grad, kernel):
    images, rows, width, chans = pre_act.shape
    assert images == 1
    space, blocks = lax.axis_size("space"), lax.axis_size("dp")
    inner = PAIR * PLANE
    outer = space // inner
    block = chans // blocks
    half = chans // PAIR
    group = 16 if block % 16 == 0 else block
    far = blocks // NEAR
    factor = float(images * rows * width * space * blocks) ** (-0.5)
    params = pltpu.CompilerParams(vmem_limit_bytes=VMEM_LIMIT)
    flops = 2 * 9 * chans * chans * rows * width

    pre = jnp.swapaxes(pre_act[0], 1, 2)
    grad = jnp.swapaxes(out_grad[0], 1, 2)
    row = my_core() * (rows - 1)
    edge = jnp.stack([lax.dynamic_index_in_dim(grad, row, 0, False), lax.dynamic_index_in_dim(pre, row, 0, False)])
    beyond = [(i, i + 1 if i % 2 else i - 1) for i in range(space)]
    pairs = [(i, i + 1 - 2 * (i % 2)) for i in range(space)]

    def inside(moves):
        return [(i, j) for i, j in moves if 0 <= j < space]

    near_row = lax.ppermute(edge, "space", inside(beyond))
    _, my_pre, my_grad = lax.optimization_barrier((edge, pre, grad))
    their_grad = lax.ppermute(my_grad, "space", pairs)
    their_pre = lax.ppermute(my_pre, "space", pairs)
    pick = pl.pallas_call(
        pick_kernel,
        out_shape=jax.ShapeDtypeStruct((9 * group, 9 * group), F32),
        in_specs=[anywhere()],
        out_specs=vmem(),
        compiler_params=params,
        cost_estimate=pl.CostEstimate(flops=flops, bytes_accessed=4000000, transcendentals=0),
        name="pick_rows",
    )(edge)
    pick, own_pre, own_grad = lax.optimization_barrier((pick, pre, grad))
    def input_part(side, edge_rows, *before):
        count = rows // 2
        return pl.pallas_call(
            functools.partial(input_kernel, side),
            out_shape=jax.ShapeDtypeStruct((rows, chans, width), BF16),
            in_specs=[vmem()] * 4 + [anywhere()] * len(before),
            out_specs=anywhere(),
            scratch_shapes=[
                pltpu.VMEM((3 * chans, (count + 2) * width), BF16),
                pltpu.VMEM((count, chans, width), BF16),
                pltpu.SemaphoreType.DMA((count // 2,)),
            ],
            input_output_aliases={4: 0} if before else {},
            compiler_params=params,
            cost_estimate=pl.CostEstimate(
                flops=flops // 2, bytes_accessed=3000000, transcendentals=rows * width * chans // 2
            ),
            name="input_grad",
        )(pre, grad, edge_rows, kernel, *before)

    piece = jax.ShapeDtypeStruct((far, 3, block, LANES), BF16)
    term, act_edge, grad_edge = pl.pallas_call(
        chip_kernel,
        out_shape=(
            jax.ShapeDtypeStruct((3, chans, PLANE * LANES), F32),
            jax.ShapeDtypeStruct((2, chans, width), BF16),
            jax.ShapeDtypeStruct((2, half, width), BF16),
        ),
        in_specs=[vmem()] * 4,
        out_specs=(vmem(),) * 3,
        scratch_shapes=[
            pltpu.VMEM((chans, PAIR * rows * width), BF16),
            pltpu.VMEM((PLANE * LANES, PAIR * (rows + 2) * width), BF16),
        ],
        compiler_params=params,
        cost_estimate=pl.CostEstimate(flops=2 * flops, bytes_accessed=4000000, transcendentals=2 * rows * width * chans),
        name="chip_terms",
    )(own_pre, own_grad, their_pre, their_grad)
    terms = pl.pallas_call(
        edge_kernel,
        out_shape=(jax.ShapeDtypeStruct(piece.shape, F32),) + (piece,) * (NEAR * PLANE - 1),
        in_specs=[vmem()] * 4,
        out_specs=(vmem(),) * (NEAR * PLANE),
        scratch_shapes=[
            pltpu.VMEM((PLANE * LANES, 2 * width), BF16),
            pltpu.VMEM((NEAR * PLANE, far, 3, block, LANES), F32),
        ],
        compiler_params=params,
        cost_estimate=pl.CostEstimate(flops=flops // 8, bytes_accessed=4000000, transcendentals=width * chans),
        name="edge_terms",
    )(term, act_edge, grad_edge, near_row)

    got = [terms[0]]
    for slot in range(NEAR * PLANE - 1):
        moves = []
        for z in range(blocks):
            for i in range(space):
                k = FIRST_ORDER[i % PAIR][slot]
                to_z, to_i = z ^ (k // PLANE), i ^ (k % PLANE * PAIR)
                moves.append((z * space + i, to_z * space + to_i))
        got.append(lax.ppermute(terms[slot + 1], ("dp", "space"), moves))

    their_edge = lax.dynamic_index_in_dim(their_grad, my_core() * (rows - 1), 0)
    got[1], got[2], near_row, their_edge = lax.optimization_barrier((got[1], got[2], near_row, their_edge))
    in_grad = input_part(1, their_edge, input_part(0, near_row))
    *got, in_grad = lax.optimization_barrier((*got, in_grad))
    near_sum = sum(part.astype(F32) for part in got)
    others = []
    for k in range(1, far):
        moves = [(z, z ^ (k * NEAR)) for z in range(blocks)]
        others.append(lax.ppermute(near_sum[k].astype(BF16), "dp", moves))
    total = near_sum[0] + sum(other.astype(F32) for other in others)
    total = total * factor
    if outer > 1:
        total = lax.psum(total, "space", axis_index_groups=[[o * inner + i for o in range(outer)] for i in range(inner)])
    final = total.astype(BF16)
    parts = [final]
    for slot in range(PLANE - 1):
        moves = [(i, i ^ (SPREAD_ORDER[i % PAIR][slot] * PAIR)) for i in range(space)]
        parts.append(lax.ppermute(final, "space", moves))
    parts = jnp.stack(parts)
    their_parts = lax.ppermute(parts, "space", pairs)

    def place(flip, parts, *before):
        return pl.pallas_call(
            functools.partial(place_kernel, flip),
            out_shape=jax.ShapeDtypeStruct((chans, 9 * block), F32),
            in_specs=[vmem()] * 2 + [anywhere()] * len(before),
            out_specs=anywhere(),
            scratch_shapes=[
                pltpu.VMEM((3, block, PLANE * LANES), F32),
                pltpu.VMEM((9 * block, half), F32),
                pltpu.VMEM((half, 9 * block), F32),
                pltpu.SemaphoreType.DMA((2,)),
            ],
            input_output_aliases={2: 0} if before else {},
            compiler_params=params,
            cost_estimate=pl.CostEstimate(flops=81 * block * block * chans, bytes_accessed=1000000, transcendentals=0),
            name="place_rows",
        )(parts, pick, *before)

    placed = place(1, their_parts, place(0, parts))
    return jnp.swapaxes(in_grad, 1, 2)[None], placed.T


def solution(mesh):
    placed = (P("dp", "space", None, None), P("dp", "space", None, None), P())
    return jax.shard_map(
        shards,
        mesh=mesh,
        in_specs=placed,
        out_specs=(P("dp", "space", None, None), P("dp", None)),
        check_vma=False,
    )
```

```python
import functools

import jax
import jax.numpy as jnp
from jax import lax
from jax.experimental import pallas as pl
from jax.experimental.pallas import tpu as pltpu
from jax.sharding import PartitionSpec as P

F32 = jnp.float32
BF16 = jnp.bfloat16
LANES = 128
PAIR = 2
PLANE = 4
NEAR = 2
VMEM_LIMIT = 16 * 1024 * 1024
NT = (((1,), (1,)), ((), ()))


def vmem():
    return pl.BlockSpec(memory_space=pltpu.VMEM)


def anywhere():
    return pl.BlockSpec(memory_space=pl.ANY)


def column_shifts(row):
    wide = row.astype(F32)
    width = wide.shape[1]
    at = lax.broadcasted_iota(jnp.int32, wide.shape, 1)
    ahead = jnp.where(at == width - 1, 0.0, pltpu.roll(wide, width - 1, 1))
    behind = jnp.where(at == 0, 0.0, pltpu.roll(wide, 1, 1))
    return ahead.astype(BF16), row, behind.astype(BF16)


def put_taps(taps_s, slot, row):
    half, width = row.shape
    for b, shifted in enumerate(column_shifts(row)):
        taps_s[b * half : (b + 1) * half, slot * width : (slot + 1) * width] = shifted


def plane_index():
    return lax.rem(lax.axis_index("space") // PAIR, PLANE)


def near_index():
    return lax.rem(lax.axis_index("dp"), NEAR) * PLANE + plane_index()


def silu(v):
    x = v.astype(F32)
    return (x / (1.0 + jnp.exp(-x))).astype(BF16)


def my_core():
    return lax.rem(lax.axis_index("space"), PAIR)


def chip_kernel(pre_ref, grad_ref, their_pre_ref, their_grad_ref, out_ref, act_edge_ref, grad_edge_ref, act_s, taps_s):
    rows, chans, width = pre_ref.shape
    half = chans // PAIR
    core = my_core()
    first = core == 0
    mine = pl.ds(pl.multiple_of(core * half, half), half)
    zero = jnp.zeros((half, width), BF16)
    taps_s[3 * half :, :] = jnp.zeros((taps_s.shape[0] - 3 * half, taps_s.shape[1]), BF16)
    for part, (ref, other_ref, upper) in enumerate(((grad_ref, their_grad_ref, first), (their_grad_ref, grad_ref, ~first))):
        at = part * (rows + 2)
        put_taps(taps_s, at, jnp.where(upper, zero, other_ref[rows - 1, mine, :]))
        for r in range(rows):
            put_taps(taps_s, at + r + 1, ref[r, mine, :])
        put_taps(taps_s, at + rows + 1, jnp.where(upper, other_ref[0, mine, :], zero))
    for part, ref in enumerate((pre_ref, their_pre_ref)):
        for r in range(rows):
            act_s[:, (part * rows + r) * width : (part * rows + r + 1) * width] = silu(ref[r])
    for i, r in enumerate((0, rows - 1)):
        act_edge_ref[i] = act_s[:, r * width : (r + 1) * width]
        grad_edge_ref[i] = grad_ref[r, mine, :]
    for a in range(3):
        terms = []
        for part in range(PAIR):
            at = (part * (rows + 2) + 2 - a) * width
            terms.append(
                lax.dot_general(
                    act_s[:, part * rows * width : (part + 1) * rows * width],
                    taps_s[:, at : at + rows * width],
                    NT,
                    preferred_element_type=F32,
                )
            )
        out_ref[a] = terms[0] + terms[1]


def edge_kernel(term_ref, act_edge_ref, grad_edge_ref, near_ref, *refs):
    out_refs, (taps_s, term_s) = refs[: PLANE * NEAR], refs[PLANE * NEAR :]
    _, chans, width = near_ref.shape
    half = chans // PAIR
    outers, _, block, _ = out_refs[0].shape
    core = my_core()
    first = core == 0
    near_act = silu(near_ref[1])
    near_grad = near_ref[0, pl.ds(pl.multiple_of(core * half, half), half), :]
    taps_s[3 * half :, :] = jnp.zeros((taps_s.shape[0] - 3 * half, taps_s.shape[1]), BF16)
    put_taps(taps_s, 0, jnp.where(first, grad_edge_ref[0], near_grad))
    put_taps(taps_s, 1, jnp.where(first, near_grad, grad_edge_ref[1]))
    acts = {0: jnp.where(first, near_act, act_edge_ref[1]), 2: jnp.where(first, act_edge_ref[0], near_act)}
    for a in range(3):
        term = term_ref[a]
        if a in acts:
            taps = taps_s[:, a // 2 * width : (a // 2 + 1) * width]
            term += lax.dot_general(acts[a], taps, NT, preferred_element_type=F32)
        for p in range(PLANE):
            for z in range(NEAR * outers):
                term_s[z % NEAR * PLANE + p, z // NEAR, a] = term[z * block : (z + 1) * block, p * LANES : (p + 1) * LANES]
    at, outer_at = near_index(), lax.axis_index("dp") // NEAR
    for k, out_ref in enumerate(out_refs):
        for j in range(outers):
            out_ref[j] = term_s[at ^ k, outer_at ^ j].astype(out_ref.dtype)


def input_kernel(side, on_core, *refs):
    @pl.when(my_core() == on_core)
    def _():
        input_rows(side, *refs)


def input_rows(side, pre_ref, grad_ref, edge_ref, kernel_ref, *refs):
    out_hbm, taps_s, out_s, sem = refs[-4:]
    rows, chans, width = pre_ref.shape
    count = rows // 2
    upper = my_core() == side
    start = jnp.where(upper, 0, count)
    put_taps(taps_s, 0, jnp.where(upper, edge_ref[0], grad_ref[count - 1]))
    for r in range(count):
        put_taps(taps_s, r + 1, grad_ref[start + r])
    put_taps(taps_s, count + 1, jnp.where(upper, grad_ref[count], edge_ref[0]))
    step = 2
    copies = []
    for top in range(0, count, step):
        total = jnp.zeros((chans, step * width), F32)
        for a in range(3):
            at = (top + 2 - a) * width
            for b in range(3):
                taps = taps_s[b * chans : (b + 1) * chans, at : at + step * width]
                total += jnp.dot(kernel_ref[a, b], taps, preferred_element_type=F32)
        for r in range(step):
            x = pre_ref[start + top + r].astype(F32)
            sig = 1.0 / (1.0 + jnp.exp(-x))
            deriv = sig * (1.0 + x * (1.0 - sig))
            out_s[top + r] = (total[:, r * width : (r + 1) * width] * deriv).astype(out_s.dtype)
        copies.append(
            pltpu.make_async_copy(
                out_s.at[pl.ds(top, step)], out_hbm.at[pl.ds(start + top, step)], sem.at[top // step]
            )
        )
        copies[-1].start()
    for copy in copies:
        copy.wait()


def pick_kernel(after_ref, out_ref):
    size = out_ref.shape[0]
    group = size // 9
    j = lax.broadcasted_iota(jnp.int32, (size, size), 0)
    k = lax.broadcasted_iota(jnp.int32, (size, size), 1)
    pick = jnp.zeros((size, size), F32)
    for t in range(9):
        c = k - t * group
        pick = jnp.where((c >= 0) & (c < group) & (j == 9 * c + t), 1.0, pick)
    out_ref[...] = pick


def place_kernel(flip, parts_ref, pick_ref, *refs):
    out_hbm, wide_s, turned_s, out_s, sem = refs[-5:]
    _, _, block, _ = parts_ref.shape
    half = out_s.shape[0]
    width = pick_ref.shape[0]
    group = width // 9
    for k in range(PLANE):
        lanes = pl.ds(pl.multiple_of((plane_index() ^ k) * LANES, LANES), LANES)
        wide_s[:, :, lanes] = parts_ref[k].astype(F32)
    pick = pick_ref[...].astype(BF16)
    for g in range(block // group):
        rows = [wide_s[t // 3, g * group : (g + 1) * group, t % 3 * half : (t % 3 + 1) * half] for t in range(9)]
        rows = jnp.concatenate(rows, axis=0).astype(BF16)
        turned_s[g * width : (g + 1) * width, :] = jnp.dot(pick, rows, preferred_element_type=F32)
    turned = turned_s[...].astype(BF16)
    step = half // sem.shape[0]
    first = (my_core() ^ flip) * half
    copies = []
    for n in range(sem.shape[0]):
        i = lax.broadcasted_iota(jnp.int32, (step, half), 0)
        j = lax.broadcasted_iota(jnp.int32, (step, half), 1)
        same = jnp.where(i + n * step == j, 1.0, 0.0).astype(BF16)
        here = slice(n * step, (n + 1) * step)
        out_s[here, :] = lax.dot_general(same, turned, NT, preferred_element_type=F32)
        to = pl.ds(pl.multiple_of(first + n * step, 8), step)
        copies.append(pltpu.make_async_copy(out_s.at[here], out_hbm.at[to], sem.at[n]))
        copies[-1].start()
    for copy in copies:
        copy.wait()


def shards(pre_act, out_grad, kernel):
    images, rows, width, chans = pre_act.shape
    assert images == 1
    space, blocks = lax.axis_size("space"), lax.axis_size("dp")
    inner = PAIR * PLANE
    outer = space // inner
    block = chans // blocks
    half = chans // PAIR
    group = 16 if block % 16 == 0 else block
    far = blocks // NEAR
    factor = float(images * rows * width * space * blocks) ** (-0.5)
    params = pltpu.CompilerParams(vmem_limit_bytes=VMEM_LIMIT)
    flops = 2 * 9 * chans * chans * rows * width

    pre = jnp.swapaxes(pre_act[0], 1, 2)
    grad = jnp.swapaxes(out_grad[0], 1, 2)
    row = my_core() * (rows - 1)
    edge = jnp.stack([lax.dynamic_index_in_dim(grad, row, 0, False), lax.dynamic_index_in_dim(pre, row, 0, False)])
    beyond = [(i, i + 1 if i % 2 else i - 1) for i in range(space)]
    pairs = [(i, i + 1 - 2 * (i % 2)) for i in range(space)]

    def inside(moves):
        return [(i, j) for i, j in moves if 0 <= j < space]

    near_row = lax.ppermute(edge, "space", inside(beyond))
    _, my_pre, my_grad = lax.optimization_barrier((edge, pre, grad))
    their_grad = lax.ppermute(my_grad, "space", pairs)
    their_pre = lax.ppermute(my_pre, "space", pairs)
    pick = pl.pallas_call(
        pick_kernel,
        out_shape=jax.ShapeDtypeStruct((9 * group, 9 * group), F32),
        in_specs=[anywhere()],
        out_specs=vmem(),
        compiler_params=params,
        cost_estimate=pl.CostEstimate(flops=flops, bytes_accessed=4000000, transcendentals=0),
        name="pick_rows",
    )(edge)
    pick, own_pre, own_grad = lax.optimization_barrier((pick, pre, grad))
    def input_part(side, on_core, edge_rows, *before):
        count = rows // 2
        return pl.pallas_call(
            functools.partial(input_kernel, side, on_core),
            out_shape=jax.ShapeDtypeStruct((rows, chans, width), BF16),
            in_specs=[vmem()] * 4 + [anywhere()] * len(before),
            out_specs=anywhere(),
            scratch_shapes=[
                pltpu.VMEM((3 * chans, (count + 2) * width), BF16),
                pltpu.VMEM((count, chans, width), BF16),
                pltpu.SemaphoreType.DMA((count // 2,)),
            ],
            input_output_aliases={4: 0} if before else {},
            compiler_params=params,
            cost_estimate=pl.CostEstimate(
                flops=flops // 2, bytes_accessed=3000000, transcendentals=rows * width * chans // 2
            ),
            name="input_grad",
        )(pre, grad, edge_rows, kernel, *before)

    piece = jax.ShapeDtypeStruct((far, 3, block, LANES), BF16)
    term, act_edge, grad_edge = pl.pallas_call(
        chip_kernel,
        out_shape=(
            jax.ShapeDtypeStruct((3, chans, PLANE * LANES), F32),
            jax.ShapeDtypeStruct((2, chans, width), BF16),
            jax.ShapeDtypeStruct((2, half, width), BF16),
        ),
        in_specs=[vmem()] * 4,
        out_specs=(vmem(),) * 3,
        scratch_shapes=[
            pltpu.VMEM((chans, PAIR * rows * width), BF16),
            pltpu.VMEM((PLANE * LANES, PAIR * (rows + 2) * width), BF16),
        ],
        compiler_params=params,
        cost_estimate=pl.CostEstimate(flops=2 * flops, bytes_accessed=4000000, transcendentals=2 * rows * width * chans),
        name="chip_terms",
    )(own_pre, own_grad, their_pre, their_grad)
    ready = lax.optimization_barrier((term, act_edge, grad_edge, their_grad))
    term, act_edge, grad_edge, their_grad = ready
    their_edge = lax.dynamic_index_in_dim(their_grad, my_core() * (rows - 1), 0)
    in_grad = input_part(1, 1, their_edge)
    terms = pl.pallas_call(
        edge_kernel,
        out_shape=(jax.ShapeDtypeStruct(piece.shape, F32),) + (piece,) * (NEAR * PLANE - 1),
        in_specs=[vmem()] * 4,
        out_specs=(vmem(),) * (NEAR * PLANE),
        scratch_shapes=[
            pltpu.VMEM((PLANE * LANES, 2 * width), BF16),
            pltpu.VMEM((NEAR * PLANE, far, 3, block, LANES), F32),
        ],
        compiler_params=params,
        cost_estimate=pl.CostEstimate(flops=flops // 8, bytes_accessed=4000000, transcendentals=width * chans),
        name="edge_terms",
    )(term, act_edge, grad_edge, near_row)

    in_grad = input_part(0, 1, near_row, in_grad)
    *terms, in_grad = lax.optimization_barrier((*terms, in_grad))

    got = [terms[0]]
    for k in (4, 1, 2, 7, 3, 5, 6):
        moves = []
        for z in range(blocks):
            for i in range(space):
                to_z, to_i = z ^ (k // PLANE), i ^ (k % PLANE * PAIR)
                moves.append((z * space + i, to_z * space + to_i))
        got.append(lax.ppermute(terms[k], ("dp", "space"), moves))


    got[1], got[2], near_row, their_edge = lax.optimization_barrier((got[1], got[2], near_row, their_edge))
    in_grad = input_part(0, 0, near_row, in_grad)
    *got, in_grad = lax.optimization_barrier((*got, in_grad))

    near_sum = sum(part.astype(F32) for part in got)
    others = []
    for k in range(1, far):
        moves = [(z, z ^ (k * NEAR)) for z in range(blocks)]
        others.append(lax.ppermute(near_sum[k].astype(BF16), "dp", moves))
    in_grad = input_part(1, 0, their_edge, in_grad)
    *others, in_grad = lax.optimization_barrier((*others, in_grad))
    total = near_sum[0] + sum(other.astype(F32) for other in others)
    total = total * factor
    if outer > 1:
        total = lax.psum(total, "space", axis_index_groups=[[o * inner + i for o in range(outer)] for i in range(inner)])
    final = total.astype(BF16)
    parts = [final]
    for k in range(1, PLANE):
        parts.append(lax.ppermute(final, "space", [(i, i ^ (k * PAIR)) for i in range(space)]))
    parts = jnp.stack(parts)
    their_parts = lax.ppermute(parts, "space", pairs)

    def place(flip, parts, *before):
        return pl.pallas_call(
            functools.partial(place_kernel, flip),
            out_shape=jax.ShapeDtypeStruct((chans, 9 * block), F32),
            in_specs=[vmem()] * 2 + [anywhere()] * len(before),
            out_specs=anywhere(),
            scratch_shapes=[
                pltpu.VMEM((3, block, PLANE * LANES), F32),
                pltpu.VMEM((9 * block, half), F32),
                pltpu.VMEM((half, 9 * block), F32),
                pltpu.SemaphoreType.DMA((2,)),
            ],
            input_output_aliases={2: 0} if before else {},
            compiler_params=params,
            cost_estimate=pl.CostEstimate(flops=81 * block * block * chans, bytes_accessed=1000000, transcendentals=0),
            name="place_rows",
        )(parts, pick, *before)

    placed = place(1, their_parts, place(0, parts))
    return jnp.swapaxes(in_grad, 1, 2)[None], placed.T


def solution(mesh):
    placed = (P("dp", "space", None, None), P("dp", "space", None, None), P())
    return jax.shard_map(
        shards,
        mesh=mesh,
        in_specs=placed,
        out_specs=(P("dp", "space", None, None), P("dp", None)),
        check_vma=False,
    )
```

```python
import functools

import jax
import jax.numpy as jnp
from jax import lax
from jax.experimental import pallas as pl
from jax.experimental.pallas import tpu as pltpu
from jax.sharding import PartitionSpec as P

F32 = jnp.float32
BF16 = jnp.bfloat16
LANES = 128
PAIR = 2
PLANE = 4
NEAR = 2
VMEM_LIMIT = 16 * 1024 * 1024
NT = (((1,), (1,)), ((), ()))


def vmem():
    return pl.BlockSpec(memory_space=pltpu.VMEM)


def anywhere():
    return pl.BlockSpec(memory_space=pl.ANY)


def column_shifts(row):
    wide = row.astype(F32)
    width = wide.shape[1]
    at = lax.broadcasted_iota(jnp.int32, wide.shape, 1)
    ahead = jnp.where(at == width - 1, 0.0, pltpu.roll(wide, width - 1, 1))
    behind = jnp.where(at == 0, 0.0, pltpu.roll(wide, 1, 1))
    return ahead.astype(BF16), row, behind.astype(BF16)


def put_taps(taps_s, slot, row):
    half, width = row.shape
    for b, shifted in enumerate(column_shifts(row)):
        taps_s[b * half : (b + 1) * half, slot * width : (slot + 1) * width] = shifted


def plane_index():
    return lax.rem(lax.axis_index("space") // PAIR, PLANE)


def near_index():
    return lax.rem(lax.axis_index("dp"), NEAR) * PLANE + plane_index()


def silu(v):
    x = v.astype(F32)
    return (x / (1.0 + jnp.exp(-x))).astype(BF16)


def my_core():
    return lax.rem(lax.axis_index("space"), PAIR)


def chip_kernel(pre_ref, grad_ref, their_pre_ref, their_grad_ref, out_ref, act_edge_ref, grad_edge_ref, act_s, taps_s):
    rows, chans, width = pre_ref.shape
    half = chans // PAIR
    core = my_core()
    first = core == 0
    mine = pl.ds(pl.multiple_of(core * half, half), half)
    zero = jnp.zeros((half, width), BF16)
    taps_s[3 * half :, :] = jnp.zeros((taps_s.shape[0] - 3 * half, taps_s.shape[1]), BF16)
    for part, (ref, other_ref, upper) in enumerate(((grad_ref, their_grad_ref, first), (their_grad_ref, grad_ref, ~first))):
        at = part * (rows + 2)
        put_taps(taps_s, at, jnp.where(upper, zero, other_ref[rows - 1, mine, :]))
        for r in range(rows):
            put_taps(taps_s, at + r + 1, ref[r, mine, :])
        put_taps(taps_s, at + rows + 1, jnp.where(upper, other_ref[0, mine, :], zero))
    for part, ref in enumerate((pre_ref, their_pre_ref)):
        for r in range(rows):
            act_s[:, (part * rows + r) * width : (part * rows + r + 1) * width] = silu(ref[r])
    for i, r in enumerate((0, rows - 1)):
        act_edge_ref[i] = act_s[:, r * width : (r + 1) * width]
        grad_edge_ref[i] = grad_ref[r, mine, :]
    for a in range(3):
        terms = []
        for part in range(PAIR):
            at = (part * (rows + 2) + 2 - a) * width
            terms.append(
                lax.dot_general(
                    act_s[:, part * rows * width : (part + 1) * rows * width],
                    taps_s[:, at : at + rows * width],
                    NT,
                    preferred_element_type=F32,
                )
            )
        out_ref[a] = terms[0] + terms[1]


def edge_kernel(term_ref, act_edge_ref, grad_edge_ref, near_ref, *refs):
    out_refs, (taps_s, term_s) = refs[: PLANE * NEAR], refs[PLANE * NEAR :]
    _, chans, width = near_ref.shape
    half = chans // PAIR
    outers, _, block, _ = out_refs[0].shape
    core = my_core()
    first = core == 0
    near_act = silu(near_ref[1])
    near_grad = near_ref[0, pl.ds(pl.multiple_of(core * half, half), half), :]
    taps_s[3 * half :, :] = jnp.zeros((taps_s.shape[0] - 3 * half, taps_s.shape[1]), BF16)
    put_taps(taps_s, 0, jnp.where(first, grad_edge_ref[0], near_grad))
    put_taps(taps_s, 1, jnp.where(first, near_grad, grad_edge_ref[1]))
    acts = {0: jnp.where(first, near_act, act_edge_ref[1]), 2: jnp.where(first, act_edge_ref[0], near_act)}
    for a in range(3):
        term = term_ref[a]
        if a in acts:
            taps = taps_s[:, a // 2 * width : (a // 2 + 1) * width]
            term += lax.dot_general(acts[a], taps, NT, preferred_element_type=F32)
        for p in range(PLANE):
            for z in range(NEAR * outers):
                term_s[z % NEAR * PLANE + p, z // NEAR, a] = term[z * block : (z + 1) * block, p * LANES : (p + 1) * LANES]
    at, outer_at = near_index(), lax.axis_index("dp") // NEAR
    for k, out_ref in enumerate(out_refs):
        for j in range(outers):
            out_ref[j] = term_s[at ^ k, outer_at ^ j].astype(out_ref.dtype)


def input_kernel(side, pre_ref, grad_ref, edge_ref, kernel_ref, *refs):
    out_hbm, taps_s, out_s, sem = refs[-4:]
    rows, chans, width = pre_ref.shape
    count = rows // 2
    upper = my_core() == side
    start = jnp.where(upper, 0, count)
    put_taps(taps_s, 0, jnp.where(upper, edge_ref[0], grad_ref[count - 1]))
    for r in range(count):
        put_taps(taps_s, r + 1, grad_ref[start + r])
    put_taps(taps_s, count + 1, jnp.where(upper, grad_ref[count], edge_ref[0]))
    step = 2
    copies = []
    for top in range(0, count, step):
        total = jnp.zeros((chans, step * width), F32)
        for a in range(3):
            at = (top + 2 - a) * width
            for b in range(3):
                taps = taps_s[b * chans : (b + 1) * chans, at : at + step * width]
                total += jnp.dot(kernel_ref[a, b], taps, preferred_element_type=F32)
        for r in range(step):
            x = pre_ref[start + top + r].astype(F32)
            sig = 1.0 / (1.0 + jnp.exp(-x))
            deriv = sig * (1.0 + x * (1.0 - sig))
            out_s[top + r] = (total[:, r * width : (r + 1) * width] * deriv).astype(out_s.dtype)
        copies.append(
            pltpu.make_async_copy(
                out_s.at[pl.ds(top, step)], out_hbm.at[pl.ds(start + top, step)], sem.at[top // step]
            )
        )
        copies[-1].start()
    for copy in copies:
        copy.wait()


def pick_kernel(after_ref, out_ref):
    size = out_ref.shape[0]
    group = size // 9
    j = lax.broadcasted_iota(jnp.int32, (size, size), 0)
    k = lax.broadcasted_iota(jnp.int32, (size, size), 1)
    pick = jnp.zeros((size, size), F32)
    for t in range(9):
        c = k - t * group
        pick = jnp.where((c >= 0) & (c < group) & (j == 9 * c + t), 1.0, pick)
    out_ref[...] = pick


def place_kernel(flip, parts_ref, pick_ref, *refs):
    out_hbm, wide_s, turned_s, out_s, sem = refs[-5:]
    _, _, block, _ = parts_ref.shape
    half = out_s.shape[0]
    width = pick_ref.shape[0]
    group = width // 9
    for slot in range(PLANE):
        k = (PLANE - slot) % PLANE
        lanes = pl.ds(pl.multiple_of((plane_index() ^ k) * LANES, LANES), LANES)
        wide_s[:, :, lanes] = parts_ref[slot].astype(F32)
    pick = pick_ref[...].astype(BF16)
    for g in range(block // group):
        rows = [wide_s[t // 3, g * group : (g + 1) * group, t % 3 * half : (t % 3 + 1) * half] for t in range(9)]
        rows = jnp.concatenate(rows, axis=0).astype(BF16)
        turned_s[g * width : (g + 1) * width, :] = jnp.dot(pick, rows, preferred_element_type=F32)
    turned = turned_s[...].astype(BF16)
    step = half // sem.shape[0]
    first = (my_core() ^ flip) * half
    copies = []
    for n in range(sem.shape[0]):
        i = lax.broadcasted_iota(jnp.int32, (step, half), 0)
        j = lax.broadcasted_iota(jnp.int32, (step, half), 1)
        same = jnp.where(i + n * step == j, 1.0, 0.0).astype(BF16)
        here = slice(n * step, (n + 1) * step)
        out_s[here, :] = lax.dot_general(same, turned, NT, preferred_element_type=F32)
        to = pl.ds(pl.multiple_of(first + n * step, 8), step)
        copies.append(pltpu.make_async_copy(out_s.at[here], out_hbm.at[to], sem.at[n]))
        copies[-1].start()
    for copy in copies:
        copy.wait()


def shards(pre_act, out_grad, kernel):
    images, rows, width, chans = pre_act.shape
    assert images == 1
    space, blocks = lax.axis_size("space"), lax.axis_size("dp")
    inner = PAIR * PLANE
    outer = space // inner
    block = chans // blocks
    half = chans // PAIR
    group = 16 if block % 16 == 0 else block
    far = blocks // NEAR
    factor = float(images * rows * width * space * blocks) ** (-0.5)
    params = pltpu.CompilerParams(vmem_limit_bytes=VMEM_LIMIT)
    flops = 2 * 9 * chans * chans * rows * width

    pre = jnp.swapaxes(pre_act[0], 1, 2)
    grad = jnp.swapaxes(out_grad[0], 1, 2)
    row = my_core() * (rows - 1)
    edge = jnp.stack([lax.dynamic_index_in_dim(grad, row, 0, False), lax.dynamic_index_in_dim(pre, row, 0, False)])
    beyond = [(i, i + 1 if i % 2 else i - 1) for i in range(space)]
    pairs = [(i, i + 1 - 2 * (i % 2)) for i in range(space)]

    def inside(moves):
        return [(i, j) for i, j in moves if 0 <= j < space]

    near_row = lax.ppermute(edge, "space", inside(beyond))
    _, my_pre, my_grad = lax.optimization_barrier((edge, pre, grad))
    their_grad = lax.ppermute(my_grad, "space", pairs)
    their_pre = lax.ppermute(my_pre, "space", pairs)
    pick = pl.pallas_call(
        pick_kernel,
        out_shape=jax.ShapeDtypeStruct((9 * group, 9 * group), F32),
        in_specs=[anywhere()],
        out_specs=vmem(),
        compiler_params=params,
        cost_estimate=pl.CostEstimate(flops=flops, bytes_accessed=4000000, transcendentals=0),
        name="pick_rows",
    )(edge)
    pick, own_pre, own_grad = lax.optimization_barrier((pick, pre, grad))
    def input_part(side, edge_rows, *before):
        count = rows // 2
        return pl.pallas_call(
            functools.partial(input_kernel, side),
            out_shape=jax.ShapeDtypeStruct((rows, chans, width), BF16),
            in_specs=[vmem()] * 4 + [anywhere()] * len(before),
            out_specs=anywhere(),
            scratch_shapes=[
                pltpu.VMEM((3 * chans, (count + 2) * width), BF16),
                pltpu.VMEM((count, chans, width), BF16),
                pltpu.SemaphoreType.DMA((count // 2,)),
            ],
            input_output_aliases={4: 0} if before else {},
            compiler_params=params,
            cost_estimate=pl.CostEstimate(
                flops=flops // 2, bytes_accessed=3000000, transcendentals=rows * width * chans // 2
            ),
            name="input_grad",
        )(pre, grad, edge_rows, kernel, *before)

    piece = jax.ShapeDtypeStruct((far, 3, block, LANES), BF16)
    term, act_edge, grad_edge = pl.pallas_call(
        chip_kernel,
        out_shape=(
            jax.ShapeDtypeStruct((3, chans, PLANE * LANES), F32),
            jax.ShapeDtypeStruct((2, chans, width), BF16),
            jax.ShapeDtypeStruct((2, half, width), BF16),
        ),
        in_specs=[vmem()] * 4,
        out_specs=(vmem(),) * 3,
        scratch_shapes=[
            pltpu.VMEM((chans, PAIR * rows * width), BF16),
            pltpu.VMEM((PLANE * LANES, PAIR * (rows + 2) * width), BF16),
        ],
        compiler_params=params,
        cost_estimate=pl.CostEstimate(flops=2 * flops, bytes_accessed=4000000, transcendentals=2 * rows * width * chans),
        name="chip_terms",
    )(own_pre, own_grad, their_pre, their_grad)
    terms = pl.pallas_call(
        edge_kernel,
        out_shape=(jax.ShapeDtypeStruct(piece.shape, F32),) + (piece,) * (NEAR * PLANE - 1),
        in_specs=[vmem()] * 4,
        out_specs=(vmem(),) * (NEAR * PLANE),
        scratch_shapes=[
            pltpu.VMEM((PLANE * LANES, 2 * width), BF16),
            pltpu.VMEM((NEAR * PLANE, far, 3, block, LANES), F32),
        ],
        compiler_params=params,
        cost_estimate=pl.CostEstimate(flops=flops // 8, bytes_accessed=4000000, transcendentals=width * chans),
        name="edge_terms",
    )(term, act_edge, grad_edge, near_row)

    got = [terms[0]]
    for k in (4, 1, 2, 7, 3, 5, 6):
        moves = []
        for z in range(blocks):
            for i in range(space):
                to_z, to_i = z ^ (k // PLANE), i ^ (k % PLANE * PAIR)
                moves.append((z * space + i, to_z * space + to_i))
        got.append(lax.ppermute(terms[k], ("dp", "space"), moves))


    their_edge = lax.dynamic_index_in_dim(their_grad, my_core() * (rows - 1), 0)
    got[1], got[2], near_row, their_edge = lax.optimization_barrier((got[1], got[2], near_row, their_edge))
    in_grad = input_part(1, their_edge, input_part(0, near_row))
    *got, in_grad = lax.optimization_barrier((*got, in_grad))
    near_sum = sum(part.astype(F32) for part in got)
    others = []
    for k in range(1, far):
        moves = [(z, z ^ (k * NEAR)) for z in range(blocks)]
        others.append(lax.ppermute(near_sum[k].astype(BF16), "dp", moves))
    total = near_sum[0] + sum(other.astype(F32) for other in others)
    total = total * factor
    if outer > 1:
        total = lax.psum(total, "space", axis_index_groups=[[o * inner + i for o in range(outer)] for i in range(inner)])
    final = total.astype(BF16)
    spread = {}
    for k in range(PLANE - 1, 0, -1):
        spread[k] = lax.ppermute(final, "space", [(i, i ^ (k * PAIR)) for i in range(space)])
    parts = [final] + [spread[k] for k in range(PLANE - 1, 0, -1)]
    parts = jnp.stack(parts)
    their_parts = lax.ppermute(parts, "space", pairs)

    def place(flip, parts, *before):
        return pl.pallas_call(
            functools.partial(place_kernel, flip),
            out_shape=jax.ShapeDtypeStruct((chans, 9 * block), F32),
            in_specs=[vmem()] * 2 + [anywhere()] * len(before),
            out_specs=anywhere(),
            scratch_shapes=[
                pltpu.VMEM((3, block, PLANE * LANES), F32),
                pltpu.VMEM((9 * block, half), F32),
                pltpu.VMEM((half, 9 * block), F32),
                pltpu.SemaphoreType.DMA((2,)),
            ],
            input_output_aliases={2: 0} if before else {},
            compiler_params=params,
            cost_estimate=pl.CostEstimate(flops=81 * block * block * chans, bytes_accessed=1000000, transcendentals=0),
            name="place_rows",
        )(parts, pick, *before)

    placed = place(1, their_parts, place(0, parts))
    return jnp.swapaxes(in_grad, 1, 2)[None], placed.T


def solution(mesh):
    placed = (P("dp", "space", None, None), P("dp", "space", None, None), P())
    return jax.shard_map(
        shards,
        mesh=mesh,
        in_specs=placed,
        out_specs=(P("dp", "space", None, None), P("dp", None)),
        check_vma=False,
    )
```

```python
import functools

import jax
import jax.numpy as jnp
from jax import lax
from jax.experimental import pallas as pl
from jax.experimental.pallas import tpu as pltpu
from jax.sharding import PartitionSpec as P

F32 = jnp.float32
BF16 = jnp.bfloat16
LANES = 128
PAIR = 2
PLANE = 4
NEAR = 2
VMEM_LIMIT = 16 * 1024 * 1024
NT = (((1,), (1,)), ((), ()))


def vmem():
    return pl.BlockSpec(memory_space=pltpu.VMEM)


def anywhere():
    return pl.BlockSpec(memory_space=pl.ANY)


def column_shifts(row):
    wide = row.astype(F32)
    width = wide.shape[1]
    at = lax.broadcasted_iota(jnp.int32, wide.shape, 1)
    ahead = jnp.where(at == width - 1, 0.0, pltpu.roll(wide, width - 1, 1))
    behind = jnp.where(at == 0, 0.0, pltpu.roll(wide, 1, 1))
    return ahead.astype(BF16), row, behind.astype(BF16)


def put_taps(taps_s, slot, row):
    half, width = row.shape
    for b, shifted in enumerate(column_shifts(row)):
        taps_s[b * half : (b + 1) * half, slot * width : (slot + 1) * width] = shifted


def plane_index():
    return lax.rem(lax.axis_index("space") // PAIR, PLANE)


def near_index():
    return lax.rem(lax.axis_index("dp"), NEAR) * PLANE + plane_index()


def silu(v):
    x = v.astype(F32)
    return (x / (1.0 + jnp.exp(-x))).astype(BF16)


def my_core():
    return lax.rem(lax.axis_index("space"), PAIR)


def own_kernel(pre_ref, grad_ref, term_ref, act_edge_ref, grad_edge_ref, act_s, taps_s):
    rows, chans, width = pre_ref.shape
    half = chans // PAIR
    mine = pl.ds(pl.multiple_of(my_core() * half, half), half)
    zero = jnp.zeros((half, width), BF16)
    taps_s[3 * half :, :] = jnp.zeros((taps_s.shape[0] - 3 * half, taps_s.shape[1]), BF16)
    for r in range(rows + 2):
        put_taps(taps_s, r, grad_ref[r - 1, mine, :] if 0 < r <= rows else zero)
    for r in range(rows):
        act_s[:, r * width : (r + 1) * width] = silu(pre_ref[r])
    for i, r in enumerate((0, rows - 1)):
        act_edge_ref[i] = act_s[:, r * width : (r + 1) * width]
        grad_edge_ref[i] = grad_ref[r, mine, :]
    for a in range(3):
        at = (2 - a) * width
        term_ref[a] = lax.dot_general(act_s[...], taps_s[:, at : at + rows * width], NT, preferred_element_type=F32)


def pair_kernel(term_ref, act_edge_ref, grad_edge_ref, their_pre_ref, their_grad_ref, out_ref, act_s, taps_s):
    rows, chans, width = their_pre_ref.shape
    half = chans // PAIR
    core = my_core()
    first = core == 0
    mine = pl.ds(pl.multiple_of(core * half, half), half)
    zero = jnp.zeros((half, width), BF16)
    zero_act = jnp.zeros((chans, width), BF16)
    taps_s[3 * half :, :] = jnp.zeros((taps_s.shape[0] - 3 * half, taps_s.shape[1]), BF16)
    act_s[:, :width] = jnp.where(first, zero_act, act_edge_ref[0])
    for r in range(rows):
        act_s[:, (1 + r) * width : (2 + r) * width] = silu(their_pre_ref[r])
    act_s[:, (rows + 1) * width :] = jnp.where(first, act_edge_ref[1], zero_act)
    put_taps(taps_s, 0, their_grad_ref[rows - 1, mine, :])
    put_taps(taps_s, 1, jnp.where(first, grad_edge_ref[1], zero))
    for r in range(rows):
        put_taps(taps_s, 2 + r, their_grad_ref[r, mine, :])
    put_taps(taps_s, rows + 2, jnp.where(first, zero, grad_edge_ref[0]))
    put_taps(taps_s, rows + 3, their_grad_ref[0, mine, :])
    for a, (left, right, at) in enumerate(((1, rows + 2, 3), (1, rows + 1, 2), (0, rows + 1, 0))):
        out_ref[a] = term_ref[a] + lax.dot_general(
            act_s[:, left * width : right * width],
            taps_s[:, at * width : (at + right - left) * width],
            NT,
            preferred_element_type=F32,
        )


def edge_kernel(term_ref, act_edge_ref, grad_edge_ref, near_ref, *refs):
    out_refs, (taps_s, term_s) = refs[: PLANE * NEAR], refs[PLANE * NEAR :]
    _, chans, width = near_ref.shape
    half = chans // PAIR
    outers, _, block, _ = out_refs[0].shape
    core = my_core()
    first = core == 0
    near_act = silu(near_ref[1])
    near_grad = near_ref[0, pl.ds(pl.multiple_of(core * half, half), half), :]
    taps_s[3 * half :, :] = jnp.zeros((taps_s.shape[0] - 3 * half, taps_s.shape[1]), BF16)
    put_taps(taps_s, 0, jnp.where(first, grad_edge_ref[0], near_grad))
    put_taps(taps_s, 1, jnp.where(first, near_grad, grad_edge_ref[1]))
    acts = {0: jnp.where(first, near_act, act_edge_ref[1]), 2: jnp.where(first, act_edge_ref[0], near_act)}
    for a in range(3):
        term = term_ref[a]
        if a in acts:
            taps = taps_s[:, a // 2 * width : (a // 2 + 1) * width]
            term += lax.dot_general(acts[a], taps, NT, preferred_element_type=F32)
        for p in range(PLANE):
            for z in range(NEAR * outers):
                term_s[z % NEAR * PLANE + p, z // NEAR, a] = term[
                    z * block : (z + 1) * block, p * LANES : (p + 1) * LANES
                ].astype(term_s.dtype)
    at, outer_at = near_index(), lax.axis_index("dp") // NEAR
    for k, out_ref in enumerate(out_refs):
        for j in range(outers):
            out_ref[j] = term_s[at ^ k, outer_at ^ j]


def input_kernel(side, pre_ref, grad_ref, edge_ref, kernel_ref, *refs):
    out_hbm, taps_s, out_s, sem = refs[-4:]
    rows, chans, width = pre_ref.shape
    count = rows // 2
    upper = my_core() == side
    start = jnp.where(upper, 0, count)
    put_taps(taps_s, 0, jnp.where(upper, edge_ref[0], grad_ref[count - 1]))
    for r in range(count):
        put_taps(taps_s, r + 1, grad_ref[start + r])
    put_taps(taps_s, count + 1, jnp.where(upper, grad_ref[count], edge_ref[0]))
    step = 2
    copies = []
    for top in range(0, count, step):
        total = jnp.zeros((chans, step * width), F32)
        for a in range(3):
            at = (top + 2 - a) * width
            for b in range(3):
                taps = taps_s[b * chans : (b + 1) * chans, at : at + step * width]
                total += jnp.dot(kernel_ref[a, b], taps, preferred_element_type=F32)
        for r in range(step):
            x = pre_ref[start + top + r].astype(F32)
            sig = 1.0 / (1.0 + jnp.exp(-x))
            deriv = sig * (1.0 + x * (1.0 - sig))
            out_s[top + r] = (total[:, r * width : (r + 1) * width] * deriv).astype(out_s.dtype)
        copies.append(
            pltpu.make_async_copy(
                out_s.at[pl.ds(top, step)], out_hbm.at[pl.ds(start + top, step)], sem.at[top // step]
            )
        )
        copies[-1].start()
    for copy in copies:
        copy.wait()


def pick_kernel(after_ref, out_ref):
    size = out_ref.shape[0]
    group = size // 9
    j = lax.broadcasted_iota(jnp.int32, (size, size), 0)
    k = lax.broadcasted_iota(jnp.int32, (size, size), 1)
    pick = jnp.zeros((size, size), F32)
    for t in range(9):
        c = k - t * group
        pick = jnp.where((c >= 0) & (c < group) & (j == 9 * c + t), 1.0, pick)
    out_ref[...] = pick


def place_kernel(flip, parts_ref, pick_ref, *refs):
    out_hbm, wide_s, turned_s, out_s, sem = refs[-5:]
    _, _, block, _ = parts_ref.shape
    half = out_s.shape[0]
    width = pick_ref.shape[0]
    group = width // 9
    for k in range(PLANE):
        lanes = pl.ds(pl.multiple_of((plane_index() ^ k) * LANES, LANES), LANES)
        wide_s[:, :, lanes] = parts_ref[k].astype(F32)
    pick = pick_ref[...].astype(BF16)
    for g in range(block // group):
        rows = [wide_s[t // 3, g * group : (g + 1) * group, t % 3 * half : (t % 3 + 1) * half] for t in range(9)]
        rows = jnp.concatenate(rows, axis=0).astype(BF16)
        turned_s[g * width : (g + 1) * width, :] = jnp.dot(pick, rows, preferred_element_type=F32)
    i = lax.broadcasted_iota(jnp.int32, (half, half), 0)
    j = lax.broadcasted_iota(jnp.int32, (half, half), 1)
    same = jnp.where(i == j, 1.0, 0.0).astype(BF16)
    out_s[...] = lax.dot_general(same, turned_s[...].astype(BF16), NT, preferred_element_type=F32)
    count = sem.shape[0]
    step = half // count
    first = (my_core() ^ flip) * half
    copies = []
    for i in range(count):
        to = pl.ds(pl.multiple_of(first + i * step, 8), step)
        copies.append(pltpu.make_async_copy(out_s.at[pl.ds(i * step, step)], out_hbm.at[to], sem.at[i]))
        copies[-1].start()
    for copy in copies:
        copy.wait()


def shards(pre_act, out_grad, kernel):
    images, rows, width, chans = pre_act.shape
    assert images == 1
    space, blocks = lax.axis_size("space"), lax.axis_size("dp")
    inner = PAIR * PLANE
    outer = space // inner
    block = chans // blocks
    half = chans // PAIR
    group = 16 if block % 16 == 0 else block
    far = blocks // NEAR
    factor = float(images * rows * width * space * blocks) ** (-0.5)
    params = pltpu.CompilerParams(vmem_limit_bytes=VMEM_LIMIT)
    flops = 2 * 9 * chans * chans * rows * width

    pre = jnp.swapaxes(pre_act[0], 1, 2)
    grad = jnp.swapaxes(out_grad[0], 1, 2)
    row = my_core() * (rows - 1)
    edge = jnp.stack([lax.dynamic_index_in_dim(grad, row, 0, False), lax.dynamic_index_in_dim(pre, row, 0, False)])
    beyond = [(i, i + 1 if i % 2 else i - 1) for i in range(space)]
    pairs = [(i, i + 1 - 2 * (i % 2)) for i in range(space)]

    def inside(moves):
        return [(i, j) for i, j in moves if 0 <= j < space]

    near_row = lax.ppermute(edge, "space", inside(beyond))
    _, my_pre, my_grad = lax.optimization_barrier((edge, pre, grad))
    their_grad = lax.ppermute(my_grad, "space", pairs)
    their_pre = lax.ppermute(my_pre, "space", pairs)
    pick = pl.pallas_call(
        pick_kernel,
        out_shape=jax.ShapeDtypeStruct((9 * group, 9 * group), F32),
        in_specs=[anywhere()],
        out_specs=vmem(),
        compiler_params=params,
        cost_estimate=pl.CostEstimate(flops=flops, bytes_accessed=4000000, transcendentals=0),
        name="pick_rows",
    )(edge)
    pick, own_pre, own_grad = lax.optimization_barrier((pick, pre, grad))
    own, act_edge, grad_edge = pl.pallas_call(
        own_kernel,
        out_shape=(
            jax.ShapeDtypeStruct((3, chans, PLANE * LANES), F32),
            jax.ShapeDtypeStruct((2, chans, width), BF16),
            jax.ShapeDtypeStruct((2, half, width), BF16),
        ),
        in_specs=[vmem()] * 2,
        out_specs=(vmem(),) * 3,
        scratch_shapes=[
            pltpu.VMEM((chans, rows * width), BF16),
            pltpu.VMEM((PLANE * LANES, (rows + 2) * width), BF16),
        ],
        compiler_params=params,
        cost_estimate=pl.CostEstimate(flops=flops, bytes_accessed=4000000, transcendentals=rows * width * chans),
        name="own_terms",
    )(own_pre, own_grad)

    def input_part(side, edge_rows, *before):
        count = rows // 2
        return pl.pallas_call(
            functools.partial(input_kernel, side),
            out_shape=jax.ShapeDtypeStruct((rows, chans, width), BF16),
            in_specs=[vmem()] * 4 + [anywhere()] * len(before),
            out_specs=anywhere(),
            scratch_shapes=[
                pltpu.VMEM((3 * chans, (count + 2) * width), BF16),
                pltpu.VMEM((count, chans, width), BF16),
                pltpu.SemaphoreType.DMA((count // 2,)),
            ],
            input_output_aliases={4: 0} if before else {},
            compiler_params=params,
            cost_estimate=pl.CostEstimate(
                flops=flops // 2, bytes_accessed=3000000, transcendentals=rows * width * chans // 2
            ),
            name="input_grad",
        )(pre, grad, edge_rows, kernel, *before)

    piece = jax.ShapeDtypeStruct((far, 3, block, LANES), BF16)
    term = pl.pallas_call(
        pair_kernel,
        out_shape=jax.ShapeDtypeStruct((3, chans, PLANE * LANES), F32),
        in_specs=[vmem()] * 5,
        out_specs=vmem(),
        scratch_shapes=[
            pltpu.VMEM((chans, (rows + 2) * width), BF16),
            pltpu.VMEM((PLANE * LANES, (rows + 4) * width), BF16),
        ],
        compiler_params=params,
        cost_estimate=pl.CostEstimate(flops=flops, bytes_accessed=4000000, transcendentals=rows * width * chans),
        name="pair_terms",
    )(own, act_edge, grad_edge, their_pre, their_grad)
    terms = pl.pallas_call(
        edge_kernel,
        out_shape=(piece,) * (NEAR * PLANE),
        in_specs=[vmem()] * 4,
        out_specs=(vmem(),) * (NEAR * PLANE),
        scratch_shapes=[
            pltpu.VMEM((PLANE * LANES, 2 * width), BF16),
            pltpu.VMEM((NEAR * PLANE, far, 3, block, LANES), BF16),
        ],
        compiler_params=params,
        cost_estimate=pl.CostEstimate(flops=flops // 8, bytes_accessed=4000000, transcendentals=width * chans),
        name="edge_terms",
    )(term, act_edge, grad_edge, near_row)

    got = [terms[0]]
    for k in (4, 1, 2, 7, 3, 5, 6):
        moves = []
        for z in range(blocks):
            for i in range(space):
                to_z, to_i = z ^ (k // PLANE), i ^ (k % PLANE * PAIR)
                moves.append((z * space + i, to_z * space + to_i))
        got.append(lax.ppermute(terms[k], ("dp", "space"), moves))


    their_edge = lax.dynamic_index_in_dim(their_grad, my_core() * (rows - 1), 0)
    got[1], got[2], near_row, their_edge = lax.optimization_barrier((got[1], got[2], near_row, their_edge))
    in_grad = input_part(1, their_edge, input_part(0, near_row))
    *got, in_grad = lax.optimization_barrier((*got, in_grad))
    near_sum = sum(part.astype(F32) for part in got)
    others = []
    for k in range(1, far):
        moves = [(z, z ^ (k * NEAR)) for z in range(blocks)]
        others.append(lax.ppermute(near_sum[k].astype(BF16), "dp", moves))
    total = near_sum[0] + sum(other.astype(F32) for other in others)
    total = total * factor
    if outer > 1:
        total = lax.psum(total, "space", axis_index_groups=[[o * inner + i for o in range(outer)] for i in range(inner)])
    final = total.astype(BF16)
    parts = [final]
    for k in range(1, PLANE):
        parts.append(lax.ppermute(final, "space", [(i, i ^ (k * PAIR)) for i in range(space)]))
    parts = jnp.stack(parts)
    their_parts = lax.ppermute(parts, "space", pairs)

    def place(flip, parts, *before):
        return pl.pallas_call(
            functools.partial(place_kernel, flip),
            out_shape=jax.ShapeDtypeStruct((chans, 9 * block), F32),
            in_specs=[vmem()] * 2 + [anywhere()] * len(before),
            out_specs=anywhere(),
            scratch_shapes=[
                pltpu.VMEM((3, block, PLANE * LANES), F32),
                pltpu.VMEM((9 * block, half), F32),
                pltpu.VMEM((half, 9 * block), F32),
                pltpu.SemaphoreType.DMA((10,)),
            ],
            input_output_aliases={2: 0} if before else {},
            compiler_params=params,
            cost_estimate=pl.CostEstimate(flops=81 * block * block * chans, bytes_accessed=1000000, transcendentals=0),
            name="place_rows",
        )(parts, pick, *before)

    placed = place(1, their_parts, place(0, parts))
    return jnp.swapaxes(in_grad, 1, 2)[None], placed.T


def solution(mesh):
    placed = (P("dp", "space", None, None), P("dp", "space", None, None), P())
    return jax.shard_map(
        shards,
        mesh=mesh,
        in_specs=placed,
        out_specs=(P("dp", "space", None, None), P("dp", None)),
        check_vma=False,
    )
```
